128 devices in a mesh: leaf: 16 (over y, z), node: 8 (over x, core).
Axes of the slice: x: 4, y: 4, z: 4, core: 2. Of those that a mesh axis runs over, the one named last changes fastest.
Arguments:
- x_start: float32 [36864, 512], P(('leaf', 'node')), may hold values from 0 to 1
- y_start: float32 [36864, 2048], P(('leaf', 'node')), may hold values from 0 to 1
- cost_vec: float32 [36864, 512], P(('leaf', 'node')), may hold values from -40 to 40
- right_side: float32 [36864, 2048], P(('leaf', 'node')), may hold values from -40 to 40
- omega: float32 [1], replicated, may hold values from 0.5 to 2
- coupling: bfloat16 [3, 2048, 512], replicated, may hold values from -0.25 to 0.25
- linking: bfloat16 [2, 2048, 512], replicated, may hold values from -0.25 to 0.25
- parent: int32 [36864], P(('leaf', 'node')), may hold values from -1 to 36863, as said below
- section: int32 [36864], P(('leaf', 'node')), may hold values from 0 to 2, as said below
Outputs:
- x_average: float32 [36864, 512], P(('leaf', 'node'))
- y_average: float32 [36864, 2048], P(('leaf', 'node'))
- omega_new: float32 [1], replicated
The draws below stay inside these ranges and needn't reach their ends.
Inputs may be any that keep to these rules, and one draw needn't show every extreme that they name: Nodes of section 0 have parent -1; a node of section s >= 1 has a parent of section s - 1. On each device the first 32 nodes have section 0, then the section-1 nodes, then the section-2 nodes, 256 of the later sections together, at least one of each; the number of section-1 nodes differs from device to device. A section-1 node's parent lies on a device with the same index along node; a section-2 node's parent lies on a device with the same index along leaf. From one device, at most 32 section-1 nodes have their parents on one given device and at most 64 section-2 nodes have theirs on one given device; both bounds are reached in every draw.
All inputs are finite; a program needn't handle non-finite values.
Results may differ from the reference program's by a relative error of at most 0.0035.
Values may be sent and summed in bfloat16 or wider, within the bound.
No kernel may reach another device: no remote copies, remote signals or barrier semaphores. Data moves between devices by JAX's collectives and lax.ppermute only.
A program may use at most 128 MiB of HBM per device.

```python
import math
import jax
import jax.numpy as jnp
from jax import lax

NS = 512
NC = 2048
SECTIONS = 3
ITERS = 2
ROOTS_DEV = 32
CHILD_DEV = 256
NODES_DEV = 288
NODES = 36864
N_LEAF = 16
N_NODE = 8
DEVICES = 128


def bound_for(peers):
    most = CHILD_DEV - 1
    return min(most, 2 * ((most + peers - 1) // peers))


def tree_layout(key):
    device_ids = jnp.arange(DEVICES, dtype=jnp.int32)
    leaf_of = device_ids // N_NODE
    node_of = device_ids % N_NODE
    most = CHILD_DEV - 1
    counts = jax.random.randint(jax.random.fold_in(key, 101), (DEVICES,), 1, CHILD_DEV).astype(jnp.int32)
    chosen = jax.random.permutation(jax.random.fold_in(key, 105), DEVICES)
    counts = counts.at[chosen[0]].set(most).at[chosen[1]].set(1)
    cap_leaf = bound_for(N_LEAF)
    cap_node = bound_for(N_NODE)
    child_rank = jnp.arange(CHILD_DEV, dtype=jnp.int32)[None, :]
    is_upper = child_rank < counts[:, None]
    first_leaf = jax.random.randint(jax.random.fold_in(key, 106), (DEVICES, 1), 0, N_LEAF).astype(jnp.int32)
    first_node = jax.random.randint(jax.random.fold_in(key, 107), (DEVICES, 1), 0, N_NODE).astype(jnp.int32)
    offset_leaf = jax.random.randint(jax.random.fold_in(key, 108), (DEVICES, 1), 0, N_LEAF - 1).astype(jnp.int32)
    offset_node = jax.random.randint(jax.random.fold_in(key, 109), (DEVICES, 1), 0, N_NODE - 1).astype(jnp.int32)
    upper_rank = child_rank
    target_leaf = jnp.where(upper_rank < cap_leaf, first_leaf, first_leaf + 1 + (upper_rank - cap_leaf + offset_leaf) % (N_LEAF - 1)) % N_LEAF
    lower_rank = child_rank - counts[:, None]
    target_node = jnp.where(lower_rank < cap_node, first_node, first_node + 1 + (lower_rank - cap_node + offset_node) % (N_NODE - 1)) % N_NODE
    upper_owner = target_leaf * N_NODE + node_of[:, None]
    lower_owner = leaf_of[:, None] * N_NODE + target_node
    owners = jnp.where(is_upper, upper_owner, lower_owner).astype(jnp.int32)
    root_pick = jax.random.randint(jax.random.fold_in(key, 103), (DEVICES, CHILD_DEV), 0, ROOTS_DEV)
    middle_pick = ROOTS_DEV + jax.random.randint(jax.random.fold_in(key, 104), (DEVICES, CHILD_DEV), 0, counts[owners])
    position = jnp.where(is_upper, root_pick, middle_pick)
    child_parent = owners * NODES_DEV + position
    child_section = jnp.where(is_upper, 1, 2)
    parents = jnp.concatenate([jnp.full((DEVICES, ROOTS_DEV), -1, jnp.int32), child_parent.astype(jnp.int32)], axis=1)
    sections = jnp.concatenate([jnp.zeros((DEVICES, ROOTS_DEV), jnp.int32), child_section.astype(jnp.int32)], axis=1)
    return (parents.reshape(-1), sections.reshape(-1))


def draw_parent(key, part):
    parents, sections = tree_layout(key)
    return parents


def draw_section(key, part):
    parents, sections = tree_layout(key)
    return sections


def graded_field(key, width, rising, factor):
    fraction = jnp.arange(NODES, dtype=jnp.float32)[:, None] / NODES
    power = fraction if rising else 1.0 - fraction
    scale = jnp.exp(power * jnp.log(jnp.float32(factor)))
    base = jnp.clip(jax.random.normal(key, (NODES, width), jnp.float32), -4.0, 4.0)
    return (base * scale).astype(jnp.float32)


def draw_cost_vec(key, part):
    key = jax.random.fold_in(key, 11)
    return graded_field(key, NS, True, 10.0)


def draw_right_side(key, part):
    key = jax.random.fold_in(key, 12)
    return graded_field(key, NC, False, 10.0)


def levels(own_key, shape, split, low, high):
    loudness, own = 1.0, jax.random.fold_in(own_key, 6)
    for dim, blocks in split:
        draws = jnp.exp(jax.random.uniform(jax.random.fold_in(own, dim), (blocks,), jnp.float32, low / len(split), high / len(split)))
        loudness = loudness * jnp.repeat(draws, shape[dim] // blocks).reshape([-1 if axis == dim else 1 for axis in range(len(shape))])
    return loudness


def scatter_about(stream_key, extent, scale, reach, kind=jnp.bfloat16):
    values = scale * jax.random.normal(stream_key, extent, jnp.float32)
    return jnp.clip(values, min=-reach, max=reach).astype(kind)


def setup_inputs(seed: int = 0) -> dict:
    splits = jax.random.split(jax.random.key(seed), 10)
    x_start = jnp.clip(1.0 * jax.random.uniform(splits[0], (NODES, NS), jnp.float32) ** levels(splits[0], (NODES, NS), ((0, 128),), -0.2, 0.2), 0.0, 1.0)
    y_start = jnp.clip(1.0 * jax.random.uniform(splits[1], (NODES, NC), jnp.float32) ** levels(splits[1], (NODES, NC), ((0, 128),), -0.2, 0.2), 0.0, 1.0)
    cost_vec = draw_cost_vec(jax.random.fold_in(splits[9], 71), 0)
    right_side = draw_right_side(jax.random.fold_in(splits[9], 71), 0)
    omega = jnp.clip(jnp.exp(jax.random.uniform(splits[4], (1,), jnp.float32, math.log(0.5), math.log(2.0))), 0.5, 2.0)
    coupling = scatter_about(splits[5], (SECTIONS, NC, NS), NS ** -0.5, 0.25)
    linking = scatter_about(splits[6], (SECTIONS - 1, NC, NS), NS ** -0.5, 0.25)
    parent = draw_parent(jax.random.fold_in(splits[9], 71), 0)
    section = draw_section(jax.random.fold_in(splits[9], 71), 0)
    return {"x_start": x_start, "y_start": y_start, "cost_vec": cost_vec, "right_side": right_side, "omega": omega, "coupling": coupling, "linking": linking, "parent": parent, "section": section}


exact_mode = lax.Precision.HIGHEST
step_scale = 0.3

def pick_levels(rows, matrices, section, first_level, transpose):
    result = None
    for level in range(matrices.shape[0]):
        if transpose:
            product = jnp.dot(rows, matrices[level], precision=exact_mode)
        else:
            product = jnp.dot(rows, matrices[level].T, precision=exact_mode)
        picked = jnp.where((section == level + first_level)[:, None], product, 0.0)
        result = picked if result is None else result + picked
    return result

def reference(x_start, y_start, cost_vec, right_side, omega, coupling, linking, parent, section):
    coupling_wide = coupling.astype(jnp.float32)
    linking_wide = linking.astype(jnp.float32)
    node_total = parent.shape[0]
    has_parent = parent >= 0
    safe_parent = jnp.maximum(parent, 0).astype(jnp.int32)
    target = jnp.where(has_parent, parent, node_total).astype(jnp.int32)
    tau = step_scale / omega[0]
    sigma = step_scale * omega[0]
    primal = x_start
    dual = y_start
    primal_total = jnp.zeros_like(x_start)
    dual_total = jnp.zeros_like(y_start)
    for turn in range(ITERS):
        dual_low = lax.optimization_barrier(dual.astype(jnp.bfloat16)).astype(jnp.float32)
        own_part = pick_levels(dual_low, coupling_wide, section, 0, True)
        child_part = pick_levels(dual_low, linking_wide, section, 1, True)
        adjoint = own_part + jax.ops.segment_sum(child_part, target, node_total + 1)[:node_total]
        primal_next = jnp.maximum(primal - tau * (cost_vec - adjoint), 0.0)
        extra_low = lax.optimization_barrier((2.0 * primal_next - primal).astype(jnp.bfloat16)).astype(jnp.float32)
        parent_rows = jnp.where(has_parent[:, None], extra_low[safe_parent], 0.0)
        image = pick_levels(extra_low, coupling_wide, section, 0, False) + pick_levels(parent_rows, linking_wide, section, 1, False)
        dual = jnp.maximum(dual + sigma * (right_side - image), 0.0)
        primal = primal_next
        primal_total = primal_total + primal
        dual_total = dual_total + dual
    x_average = primal_total / ITERS
    y_average = dual_total / ITERS
    primal_move = jnp.sum((x_average - x_start) ** 2)
    dual_move = jnp.sum((y_average - y_start) ** 2)
    omega_new = jnp.sqrt((dual_move + 1e-06) / (primal_move + 1e-06)).reshape(1)
    return (x_average, y_average, omega_new)
```

```python
import jax
import jax.numpy as jnp
from jax import lax
from jax.experimental import pallas as pl
from jax.experimental.pallas import tpu as pltpu
from jax.sharding import PartitionSpec as P

NS = 512
NC = 2048
ROOTS = 32
CHILD = 256
NODES = 288
N_LEAF = 16
N_NODE = 8
CAP_NODE = 64
SLOTS = 512
STEP = 0.3
F32 = jnp.float32
BF16 = jnp.bfloat16
ROWS = slice(ROOTS, NODES)


def times(a, b):
    return lax.dot_general(a, b, (((1,), (0,)), ((), ())), preferred_element_type=F32)


def times_t(a, b):
    return lax.dot_general(a, b, (((1,), (1,)), ((), ())), preferred_element_type=F32)


def hot_rows(code, count):
    places = lax.broadcasted_iota(jnp.int32, (count, code.shape[1]), 0).astype(F32)
    return jnp.where(places == code, 1.0, 0.0).astype(BF16)


def hot_lanes(code, count):
    wide = jnp.concatenate([code] * (count // 128), axis=1)
    places = lax.broadcasted_iota(jnp.int32, wide.shape, 1).astype(F32)
    return jnp.where(places == wide, 1.0, 0.0).astype(BF16)


def to_lanes(row):
    return jnp.broadcast_to(row, (128, row.shape[1])).T


def call(kernel, outs, ins, flops, linking_level=None):
    specs, arrays = [], []
    moved = 0
    for item in ins:
        array, level = item if isinstance(item, tuple) else (item, None)
        arrays.append(array)
        if level is None:
            specs.append(pl.BlockSpec(array.shape, lambda i, r=array.ndim: (0,) * r, pipeline_mode=pl.Buffered(1)))
            moved += array.size * array.dtype.itemsize
        else:
            specs.append(
                pl.BlockSpec((None,) + array.shape[1:], lambda i, k=level: (k, 0, 0), pipeline_mode=pl.Buffered(1))
            )
            moved += array.size * array.dtype.itemsize // array.shape[0]
    out_shapes = [jax.ShapeDtypeStruct(s, d) for s, d in outs]
    moved += sum(o.size * o.dtype.itemsize for o in out_shapes)
    out_specs = [
        pl.BlockSpec(s, lambda i, r=len(s): (0,) * r, pipeline_mode=pl.Buffered(1)) for s, _ in outs
    ]
    return pl.pallas_call(
        kernel,
        grid=(1,),
        out_shape=out_shapes,
        in_specs=specs,
        out_specs=out_specs,
        compiler_params=pltpu.CompilerParams(vmem_limit_bytes=36 * 2**20),
        cost_estimate=pl.CostEstimate(flops=flops, bytes_accessed=moved, transcendentals=0),
    )(*arrays)


def first_node(code, y, link, out, ylow, ncode, ncol, lcode, lcol, scol):
    packed = code[...]
    upper = (packed >> 16) == 1
    parent = packed & 0xFFFF
    owner = ((parent.astype(F32) + 0.5) * (1.0 / NODES)).astype(jnp.int32)
    local = parent - owner * NODES
    leaf = owner >> 3
    node = owner & (N_NODE - 1)
    lrow = jnp.where(upper, leaf * ROOTS + local, -1).astype(F32)
    peers = lax.broadcasted_iota(jnp.int32, (N_NODE, CHILD), 0)
    member = jnp.where((peers == node) & jnp.logical_not(upper), 1.0, 0.0)
    before = lax.broadcasted_iota(jnp.int32, (CHILD, CHILD), 0) <= lax.broadcasted_iota(
        jnp.int32, (CHILD, CHILD), 1
    )
    counts = times(member.astype(BF16), jnp.where(before, 1.0, 0.0).astype(BF16))
    rank = jnp.sum(member * counts, axis=0, keepdims=True) - 1.0
    nrow = jnp.where(upper, -1.0, (node * CAP_NODE).astype(F32) + rank)
    mark = jnp.where(upper, 0, local - (ROOTS - 1)).astype(F32)
    ncode[...] = nrow
    lcode[...] = lrow
    ncol[...] = to_lanes(nrow)
    lcol[...] = to_lanes(lrow)
    scol[...] = to_lanes(jnp.where(upper, 1.0, 2.0))
    low = y[...].astype(BF16)
    ylow[...] = low
    product = times(low[ROWS], link[...]).astype(BF16)
    load = jnp.concatenate([product, to_lanes(mark).astype(BF16)], axis=1)
    out[...] = times(hot_rows(nrow, SLOTS), load).astype(BF16)


def own_adjoint(ylow, scol, coupling, own):
    own[:ROOTS] = times(ylow[:ROOTS], coupling[0])
    upper = jnp.concatenate([scol[...]] * (NS // 128), axis=1) == 1.0
    low = ylow[ROWS]
    own[ROWS] = jnp.where(upper, times(low, coupling[1]), times(low, coupling[2]))


def first_leaf(ylow, lcode, link, out):
    product = times(ylow[ROWS], link[...]).astype(BF16)
    out[...] = times(hot_rows(lcode[...], SLOTS), product).astype(BF16)


def primal_child(first, got, *refs):
    if first:
        own, x, cost, omega, wrow, wcol, x_next, extra, send = refs
        mark = got[:, NS:].astype(F32)
        wcol[...] = mark
        row = mark.T[:8]
        wrow[...] = row
        x_old = x[ROWS]
    else:
        own, x, cost, omega, wrow, wcol, x_next, extra, send = refs
        mark = wcol[...]
        row = wrow[...]
        x_old = x[...]
    tau = STEP / omega[...]
    gather = hot_rows(row[:1] - 1.0, CHILD)
    adjoint = own[ROWS] + times(gather, got[:, :NS])
    new = jnp.maximum(x_old - tau * (cost[ROWS] - adjoint), 0.0)
    low = (2.0 * new - x_old).astype(BF16)
    x_next[...] = new
    extra[...] = low
    send[...] = times(hot_lanes(mark - 1.0, CHILD), low).astype(BF16)


def primal_root(first, got, own, x, cost, omega, *refs):
    if first:
        x_next, extra, send = refs
        x_old = x[:ROOTS]
    else:
        x_start, x_child, x_child_next, x_next, extra, send, average, move = refs
        x_old = x[...]
    tau = STEP / omega[...]
    adjoint = own[:ROOTS]
    for peer in range(N_LEAF):
        adjoint = adjoint + got[peer * ROOTS : (peer + 1) * ROOTS].astype(F32)
    new = jnp.maximum(x_old - tau * (cost[:ROOTS] - adjoint), 0.0)
    low = (2.0 * new - x_old).astype(BF16)
    x_next[...] = new
    extra[...] = low
    for peer in range(N_LEAF):
        send[peer * ROOTS : (peer + 1) * ROOTS] = low
    if not first:
        roots = (x_old + new) * 0.5
        children = (x_child[...] + x_child_next[...]) * 0.5
        average[:ROOTS] = roots
        average[ROWS] = children
        gap_roots = roots - x_start[:ROOTS]
        gap_children = children - x_start[ROWS]
        total = jnp.sum(gap_roots * gap_roots) + jnp.sum(gap_children * gap_children)
        move[...] = jnp.full((8, 128), total, F32)


def own_image(extra, scol, coupling, image):
    low = extra[...]
    upper = jnp.concatenate([scol[...]] * (NS // 128), axis=1) == 1.0
    for part in range(NC // NS):
        cols = slice(part * NS, (part + 1) * NS)
        image[:, cols] = jnp.where(
            upper, times_t(low, coupling[1, cols]), times_t(low, coupling[2, cols])
        )


def dual_node(last, got, ncol, link, image, *refs):
    if last:
        (partial,) = refs
    else:
        y, right, omega, ncode, partial, out = refs
    rows = times(hot_lanes(ncol[...], SLOTS), got[...]).astype(BF16)
    total = None
    for part in range(NC // NS):
        cols = slice(part * NS, (part + 1) * NS)
        new_image = image[:, cols] + times_t(rows, link[cols])
        partial[:, cols] = new_image
        if not last:
            sigma = STEP * omega[...]
            dual = jnp.maximum(y[ROWS, cols] + sigma * (right[ROWS, cols] - new_image), 0.0)
            product = times(dual.astype(BF16), link[cols])
            total = product if total is None else total + product
    if not last:
        out[...] = times(hot_rows(ncode[...], SLOTS), total.astype(BF16)).astype(BF16)


def dual_leaf(last, got, lcol, link, coupling, extra_root, partial, y, right, omega, *refs):
    if last:
        y_start, primal_move, average, load = refs
    else:
        lcode, y_next, ylow, out = refs
    sigma = STEP * omega[...]
    rows = times(hot_lanes(lcol[...], SLOTS), got[...]).astype(BF16)
    root = extra_root[...]
    total = None
    move = jnp.zeros((1, NS), F32)
    for part in range(NC // NS):
        cols = slice(part * NS, (part + 1) * NS)
        weights = link[cols]
        image_root = times_t(root, coupling[cols])
        image = partial[:, cols] + times_t(rows, weights)
        new_root = jnp.maximum(y[:ROOTS, cols] + sigma * (right[:ROOTS, cols] - image_root), 0.0)
        new = jnp.maximum(y[ROWS, cols] + sigma * (right[ROWS, cols] - image), 0.0)
        if last:
            mean_root = (y[:ROOTS, cols] + new_root) * 0.5
            mean = (y[ROWS, cols] + new) * 0.5
            average[:ROOTS, cols] = mean_root
            average[ROWS, cols] = mean
            gap_root = mean_root - y_start[:ROOTS, cols]
            gap = mean - y_start[ROWS, cols]
            move = move + jnp.sum(gap_root * gap_root, axis=0, keepdims=True)
            move = move + jnp.sum(gap * gap, axis=0, keepdims=True)
        else:
            y_next[:ROOTS, cols] = new_root
            y_next[ROWS, cols] = new
            low = new.astype(BF16)
            ylow[:ROOTS, cols] = new_root.astype(BF16)
            ylow[ROWS, cols] = low
            product = times(low, weights)
            total = product if total is None else total + product
    if last:
        lane = lax.broadcasted_iota(jnp.int32, (8, 128), 1)
        load[...] = jnp.broadcast_to(
            jnp.where(lane == 0, primal_move[...], jnp.sum(move))[None], load.shape
        )
    else:
        out[...] = times(hot_rows(lcode[...], SLOTS), total.astype(BF16)).astype(BF16)


def swap(rows, axis, peers):
    blocks = rows.reshape(peers, rows.shape[0] // peers, rows.shape[1])
    return lax.all_to_all(blocks, axis, split_axis=0, concat_axis=0, tiled=True).reshape(rows.shape)


def part_of(kernel, flag):
    def run(*refs):
        kernel(flag, *refs)

    return run


def shards(x_start, y_start, cost_vec, right_side, omega, coupling, linking, parent, section):
    unit = 2 * CHILD * NS * NC
    code = (section * 65536 + parent)[ROOTS:].reshape(1, CHILD)
    omega = omega.reshape(1, 1)
    field = ((NODES, NC), F32)
    slots = ((SLOTS, NS), BF16)
    kids = ((CHILD, NS), F32)
    kids_low = ((CHILD, NS), BF16)
    tops = ((ROOTS, NS), F32)
    tops_low = ((ROOTS, NS), BF16)
    row = ((1, CHILD), F32)
    col = ((CHILD, 128), F32)

    out_node, ylow, ncode, ncol, lcode, lcol, scol = call(
        first_node,
        [((SLOTS, NS + 128), BF16), ((NODES, NC), BF16), row, col, row, col, col],
        [code, y_start, (linking, 1)],
        unit,
    )
    got_node = swap(out_node, "node", N_NODE)
    (out_leaf,) = call(first_leaf, [slots], [ylow, lcode, (linking, 0)], unit)
    (own,) = call(own_adjoint, [((NODES, NS), F32)], [ylow, scol, coupling], 2 * unit)
    got_leaf = swap(out_leaf, "leaf", N_LEAF)

    wrow, wcol, x_child, extra_child, send_node = call(
        part_of(primal_child, True),
        [((8, SLOTS), F32), ((SLOTS, 128), F32), kids, kids_low, slots],
        [got_node, own, x_start, cost_vec, omega],
        unit // 4,
    )
    back_node = swap(send_node, "node", N_NODE)
    x_root, extra_root, send_leaf = call(
        part_of(primal_root, True), [tops, tops_low, slots], [got_leaf, own, x_start, cost_vec, omega], 0
    )
    (image,) = call(own_image, [((CHILD, NC), F32)], [extra_child, scol, coupling], 2 * unit)
    back_leaf = swap(send_leaf, "leaf", N_LEAF)

    partial, out_node = call(
        part_of(dual_node, False),
        [((CHILD, NC), F32), slots],
        [back_node, ncol, (linking, 1), image, y_start, right_side, omega, ncode],
        2 * unit,
    )
    got_node = swap(out_node, "node", N_NODE)
    y_next, ylow, out_leaf = call(
        part_of(dual_leaf, False),
        [field, ((NODES, NC), BF16), slots],
        [back_leaf, lcol, (linking, 0), (coupling, 0), extra_root, partial, y_start, right_side, omega, lcode],
        2 * unit,
    )
    got_leaf = swap(out_leaf, "leaf", N_LEAF)
    (own,) = call(own_adjoint, [((NODES, NS), F32)], [ylow, scol, coupling], 2 * unit)

    x_child_next, extra_child, send_node = call(
        lambda got, own, x, cost, om, wrow, wcol, *outs: primal_child(
            False, got, own, x, cost, om, wrow, wcol, *outs
        ),
        [kids, kids_low, slots],
        [got_node, own, x_child, cost_vec, omega, wrow, wcol],
        unit // 4,
    )
    back_node = swap(send_node, "node", N_NODE)
    _, extra_root, send_leaf, x_average, primal_move = call(
        part_of(primal_root, False),
        [tops, tops_low, slots, ((NODES, NS), F32), ((8, 128), F32)],
        [got_leaf, own, x_root, cost_vec, omega, x_start, x_child, x_child_next],
        0,
    )
    (image,) = call(own_image, [((CHILD, NC), F32)], [extra_child, scol, coupling], 2 * unit)
    back_leaf = swap(send_leaf, "leaf", N_LEAF)
    (partial,) = call(
        part_of(dual_node, True), [((CHILD, NC), F32)], [back_node, ncol, (linking, 1), image], unit
    )
    y_average, load = call(
        part_of(dual_leaf, True),
        [field, ((N_LEAF * N_NODE, 8, 128), F32)],
        [
            back_leaf, lcol, (linking, 0), (coupling, 0), extra_root, partial, y_next, right_side, omega,
            y_start, primal_move,
        ],
        unit,
    )
    moves = lax.all_to_all(load, ("leaf", "node"), split_axis=0, concat_axis=0, tiled=True)
    moves = jnp.sum(moves[:, 0, :2], axis=0)
    omega_new = jnp.sqrt((moves[1] + 1e-06) / (moves[0] + 1e-06)).reshape(1)
    return (x_average, y_average, omega_new)


def solution(mesh):
    both = P(("leaf", "node"), None)
    flat = P(("leaf", "node"))
    return jax.shard_map(
        shards,
        mesh=mesh,
        in_specs=(both, both, both, both, P(), P(), P(), flat, flat),
        out_specs=(both, both, P()),
        check_vma=False,
    )
```

```python
import jax
import jax.numpy as jnp
from jax import lax
from jax.experimental import pallas as pl
from jax.experimental.pallas import tpu as pltpu
from jax.sharding import PartitionSpec as P

NS = 512
NC = 2048
ROOTS = 32
CHILD = 256
NODES = 288
N_LEAF = 16
N_NODE = 8
CAP_NODE = 64
SLOTS = 512
TILE = 512
VMEM_LIMIT = 24 * 2**20
STEP = 0.3
F32 = jnp.float32
BF16 = jnp.bfloat16
ROWS = slice(ROOTS, NODES)


def times(a, b):
    return lax.dot_general(a, b, (((1,), (0,)), ((), ())), preferred_element_type=F32)


def times_t(a, b):
    return lax.dot_general(a, b, (((1,), (1,)), ((), ())), preferred_element_type=F32)


def hot_rows(code, count):
    places = lax.broadcasted_iota(jnp.int32, (count, code.shape[1]), 0).astype(F32)
    return jnp.where(places == code, 1.0, 0.0).astype(BF16)


def hot_lanes(code, count):
    wide = jnp.concatenate([code] * (count // 128), axis=1)
    places = lax.broadcasted_iota(jnp.int32, wide.shape, 1).astype(F32)
    return jnp.where(places == wide, 1.0, 0.0).astype(BF16)


def to_lanes(row):
    return jnp.broadcast_to(row, (128, row.shape[1])).T


def call(kernel, outs, arrays, flops, scratch=()):
    out_shapes = [jax.ShapeDtypeStruct(shape, dtype) for shape, dtype in outs]
    moved = sum(a.size * a.dtype.itemsize for a in list(arrays) + out_shapes)
    return pl.pallas_call(
        kernel,
        out_shape=out_shapes,
        in_specs=[pl.BlockSpec(memory_space=pltpu.VMEM)] * len(arrays),
        out_specs=[pl.BlockSpec(memory_space=pltpu.VMEM)] * len(outs),
        scratch_shapes=list(scratch),
        compiler_params=pltpu.CompilerParams(vmem_limit_bytes=VMEM_LIMIT),
        cost_estimate=pl.CostEstimate(flops=flops, bytes_accessed=moved // 8, transcendentals=0),
    )(*arrays)


def parts():
    return [slice(i * TILE, (i + 1) * TILE) for i in range(NC // TILE)]


def first_node(code, y, linking, *refs):
    *outs, ylow, nsend, nback, lsend, lback, scol = refs
    packed = code[...]
    upper = ((packed >> 16) & 3) == 1
    parent = packed & 0xFFFF
    here = packed >> 18
    owner = ((parent.astype(F32) + 0.5) * (1.0 / NODES)).astype(jnp.int32)
    local = parent - owner * NODES
    ry = ((owner >> 5) - (here >> 5)) & 3
    rz = ((owner >> 3) - (here >> 3)) & 3
    rx = ((owner >> 1) - (here >> 1)) & 3
    rc = (owner ^ here) & 1
    lrow = jnp.where(upper, ry * 128 + rz * ROOTS + local, -1).astype(F32)
    lend = jnp.where(upper, ((-ry) & 3) * 128 + ((-rz) & 3) * ROOTS + local, -1).astype(F32)
    peer = rx * 2 + rc
    peers = lax.broadcasted_iota(jnp.int32, (N_NODE, CHILD), 0)
    member = jnp.where((peers == peer) & jnp.logical_not(upper), 1.0, 0.0)
    before = lax.broadcasted_iota(jnp.int32, (CHILD, CHILD), 0) <= lax.broadcasted_iota(
        jnp.int32, (CHILD, CHILD), 1
    )
    counts = times(member.astype(BF16), jnp.where(before, 1.0, 0.0).astype(BF16))
    rank = jnp.sum(member * counts, axis=0, keepdims=True) - 1.0
    nrow = jnp.where(upper, -1.0, (peer * CAP_NODE).astype(F32) + rank)
    nend = jnp.where(upper, -1.0, (rc * 256 + rx * CAP_NODE).astype(F32) + rank)
    mark = jnp.where(upper, 0, local - (ROOTS - 1)).astype(F32)
    nsend[...] = nrow
    lsend[...] = lrow
    nback[...] = to_lanes(nend)
    lback[...] = to_lanes(lend)
    scol[...] = to_lanes(jnp.where(upper, 1.0, 2.0))
    low = y[...].astype(BF16)
    ylow[...] = low
    product = times(low[ROWS], linking[1]).astype(BF16)
    load = jnp.concatenate([product, to_lanes(mark).astype(BF16)], axis=1)
    spread(nrow, load, outs)


def spread(row, load, outs):
    hot = hot_rows(row, SLOTS)
    for k, out in enumerate(outs):
        out[...] = times(hot[k * 128 : (k + 1) * 128], load).astype(BF16)


def first_leaf(ylow, lsend, linking, *outs):
    product = times(ylow[ROWS], linking[0]).astype(BF16)
    spread(lsend[...], product, outs)


def own_adjoint(ylow, scol, coupling, own):
    own[:ROOTS] = times(ylow[:ROOTS], coupling[0])
    upper = jnp.concatenate([scol[...]] * (NS // 128), axis=1) == 1.0
    low = ylow[ROWS]
    own[ROWS] = jnp.where(upper, times(low, coupling[1]), times(low, coupling[2]))


def join(blocks, swapped, held):
    for k, block in enumerate(blocks):
        held[k * CAP_NODE : (k + 1) * CAP_NODE] = block[:CAP_NODE]
    held[256:] = swapped[...]


def primal_first(g0, g1, g2, g3, swapped, own, x, cost, omega, wrow, wcol, x_next, extra, *refs):
    *sends, held = refs
    join((g0, g1, g2, g3), swapped, held)
    mark = held[:, NS:].astype(F32)
    row = mark.T[:8]
    wcol[...] = mark
    wrow[...] = row
    primal_child(held[:, :NS], own, x[ROWS], cost, omega, mark, row, x_next, extra, sends)


def primal_second(g0, g1, g2, g3, swapped, own, x, cost, omega, wrow, wcol, x_next, extra, *refs):
    *sends, held = refs
    join((g0, g1, g2, g3), swapped, held)
    primal_child(held[...], own, x[...], cost, omega, wcol[...], wrow[...], x_next, extra, sends)


def primal_child(got, own, x_old, cost, omega, mark, row, x_next, extra, sends):
    tau = STEP / omega[...]
    adjoint = own[ROWS] + times(hot_rows(row[:1] - 1.0, CHILD), got)
    new = jnp.maximum(x_old - tau * (cost[ROWS] - adjoint), 0.0)
    low = (2.0 * new - x_old).astype(BF16)
    x_next[...] = new
    extra[...] = low
    reply = times(hot_lanes(mark - 1.0, CHILD), low).astype(BF16)
    for k, send in enumerate(sends):
        send[:CAP_NODE] = reply[k * CAP_NODE : (k + 1) * CAP_NODE]
        send[CAP_NODE:] = reply[256 + k * CAP_NODE : 256 + (k + 1) * CAP_NODE]


def primal_root(first, g0, g1, g2, g3, own, x, cost, omega, *refs):
    if first:
        x_next, extra = refs
        x_old = x[:ROOTS]
    else:
        x_start, x_child, x_child_next, extra, average, move = refs
        x_old = x[...]
    tau = STEP / omega[...]
    adjoint = own[:ROOTS]
    for got in (g0, g1, g2, g3):
        adjoint = adjoint + got[...].astype(F32)
    new = jnp.maximum(x_old - tau * (cost[:ROOTS] - adjoint), 0.0)
    extra[...] = (2.0 * new - x_old).astype(BF16)
    if first:
        x_next[...] = new
    else:
        roots = (x_old + new) * 0.5
        children = (x_child[...] + x_child_next[...]) * 0.5
        average[:ROOTS] = roots
        average[ROWS] = children
        gap_roots = roots - x_start[:ROOTS]
        gap_children = children - x_start[ROWS]
        total = jnp.sum(gap_roots * gap_roots) + jnp.sum(gap_children * gap_children)
        move[...] = jnp.full((8, 128), total, F32)


def own_image(extra_child, scol, coupling, y, right, omega, base):
    sigma = STEP * omega[...]
    upper = jnp.concatenate([scol[...]] * (TILE // 128), axis=1) == 1.0
    child = extra_child[...]
    for cols in parts():
        image = jnp.where(
            upper, times_t(child, coupling[1, cols]), times_t(child, coupling[2, cols])
        )
        base[:, cols] = y[ROWS, cols] + sigma * (right[ROWS, cols] - image)


def dual_node(last, g0, g1, g2, g3, swapped, nback, linking, base, omega, *refs):
    if last:
        later, held = refs
    else:
        nsend, later, *outs, held = refs
    join((g0, g1, g2, g3), swapped, held)
    rows = times(hot_lanes(nback[...], SLOTS), held[...]).astype(BF16)
    sigma = STEP * omega[...]
    total = None
    for cols in parts():
        weights = linking[1, cols]
        new = base[:, cols] - sigma * times_t(rows, weights)
        later[:, cols] = new
        if not last:
            product = times(jnp.maximum(new, 0.0).astype(BF16), weights)
            total = product if total is None else total + product
    if not last:
        spread(nsend[...], total.astype(BF16), outs)


def from_leaf(blocks, lback):
    hot = hot_lanes(lback[...], SLOTS)
    rows = None
    for k, block in enumerate(blocks):
        term = times(hot[:, k * 128 : (k + 1) * 128], block[...])
        rows = term if rows is None else rows + term
    return rows.astype(BF16)


def dual_leaf(b0, b1, b2, b3, lback, linking, base, omega, lsend, extra_root, coupling, y, right, *refs):
    y_next, ylow, *outs = refs
    rows = from_leaf((b0, b1, b2, b3), lback)
    sigma = STEP * omega[...]
    root = extra_root[...]
    total = None
    for cols in parts():
        weights = linking[0, cols]
        image_root = times_t(root, coupling[0, cols])
        new_root = jnp.maximum(y[:ROOTS, cols] + sigma * (right[:ROOTS, cols] - image_root), 0.0)
        new = jnp.maximum(base[:, cols] - sigma * times_t(rows, weights), 0.0)
        low = new.astype(BF16)
        y_next[:ROOTS, cols] = new_root
        y_next[ROWS, cols] = new
        ylow[:ROOTS, cols] = new_root.astype(BF16)
        ylow[ROWS, cols] = low
        product = times(low, weights)
        total = product if total is None else total + product
    spread(lsend[...], total.astype(BF16), outs)


def dual_last(
    b0, b1, b2, b3, lback, linking, base, omega, extra_root, coupling, y, right, y_start, primal_move,
    average, load
):
    rows = from_leaf((b0, b1, b2, b3), lback)
    sigma = STEP * omega[...]
    root = extra_root[...]
    move = jnp.zeros((1, TILE), F32)
    for cols in parts():
        image_root = times_t(root, coupling[0, cols])
        new_root = jnp.maximum(y[:ROOTS, cols] + sigma * (right[:ROOTS, cols] - image_root), 0.0)
        new = jnp.maximum(base[:, cols] - sigma * times_t(rows, linking[0, cols]), 0.0)
        mean_root = (y[:ROOTS, cols] + new_root) * 0.5
        mean = (y[ROWS, cols] + new) * 0.5
        average[:ROOTS, cols] = mean_root
        average[ROWS, cols] = mean
        gap_root = mean_root - y_start[:ROOTS, cols]
        gap = mean - y_start[ROWS, cols]
        move = move + jnp.sum(gap_root * gap_root, axis=0, keepdims=True)
        move = move + jnp.sum(gap * gap, axis=0, keepdims=True)
    lane = lax.broadcasted_iota(jnp.int32, (8, 128), 1)
    load[...] = jnp.where(lane == 0, primal_move[...], jnp.sum(move))


def along(axis, size, stride, ring, change):
    pairs = []
    for i in range(size):
        digit = (i // stride) % ring
        pairs.append((i, i + (change(digit) - digit) * stride))
    return pairs


def ring_y(k):
    return "leaf", along("leaf", N_LEAF, 4, 4, lambda d: (d + k) % 4)


def ring_z(k):
    return "leaf", along("leaf", N_LEAF, 1, 4, lambda d: (d + k) % 4)


def ring_x(k):
    return "node", along("node", N_NODE, 2, 4, lambda d: (d + k) % 4)


def sibling(array):
    return lax.ppermute(array, "node", along("node", N_NODE, 1, 2, lambda d: 1 - d))


def shifted(blocks, ring, sign=1):
    got = {0: blocks[0]}
    for k in (2, 1, 3):
        got[k] = lax.ppermute(blocks[k], *ring((sign * k) % 4))
    return [got[k] for k in range(4)]


def swap_node(blocks, sign):
    got = shifted(blocks, ring_x, sign)
    return got + [sibling(jnp.concatenate([block[CAP_NODE:] for block in got], axis=0))]


def sum_leaf(blocks):
    got = [block.astype(F32) for block in shifted(blocks, ring_y)]
    total = (((got[0] + got[1]) + got[2]) + got[3]).astype(BF16)
    return shifted([total[k * ROOTS : (k + 1) * ROOTS] for k in range(4)], ring_z)


def gather_leaf(rows):
    plane = jnp.concatenate(shifted([rows] * 4, ring_z), axis=0)
    return shifted([plane] * 4, ring_y)


def sum_all(load):
    load = load + sibling(load)
    for axis, size, stride in (("node", N_NODE, 2), ("leaf", N_LEAF, 1), ("leaf", N_LEAF, 4)):
        got = [
            lax.ppermute(load, axis, along(axis, size, stride, 4, lambda d, k=k: d ^ k)) for k in (1, 2, 3)
        ]
        load = (load + got[0]) + (got[1] + got[2])
    return load


def part_of(kernel, flag):
    def run(*refs):
        kernel(flag, *refs)

    return run


def shards(x_start, y_start, cost_vec, right_side, omega, coupling, linking, parent, section):
    unit = 2 * CHILD * NS * NC
    here = lax.axis_index("leaf") * N_NODE + lax.axis_index("node")
    code = ((here * 4 + section) * 65536 + parent)[ROOTS:].reshape(1, CHILD)
    omega = omega.reshape(1, 1)
    field = ((NODES, NC), F32)
    field_low = ((NODES, NC), BF16)
    states = ((NODES, NS), F32)
    block = ((128, NS), BF16)
    block_mark = ((128, NS + 128), BF16)
    kids = ((CHILD, NS), F32)
    kids_low = ((CHILD, NS), BF16)
    kids_field = ((CHILD, NC), F32)
    tops = ((ROOTS, NS), F32)
    tops_low = ((ROOTS, NS), BF16)
    row = ((1, CHILD), F32)
    col = ((CHILD, 128), F32)
    held = [pltpu.VMEM((SLOTS, NS), BF16)]

    *out_node, ylow, nsend, nback, lsend, lback, scol = call(
        first_node,
        [block_mark] * 4 + [field_low, row, col, row, col, col],
        [code, y_start, linking],
        unit,
    )
    got_node = swap_node(out_node, 1)
    out_leaf = call(first_leaf, [block] * 4, [ylow, lsend, linking], unit)
    got_leaf = sum_leaf(out_leaf)
    (own,) = call(own_adjoint, [states], [ylow, scol, coupling], 2 * unit)

    wrow, wcol, x_child, extra_child, *out_node = call(
        primal_first,
        [((8, SLOTS), F32), ((SLOTS, 128), F32), kids, kids_low] + [block] * 4,
        got_node + [own, x_start, cost_vec, omega],
        unit // 4,
        [pltpu.VMEM((SLOTS, NS + 128), BF16)],
    )
    back_node = swap_node(out_node, -1)
    x_root, extra_root = call(
        part_of(primal_root, True), [tops, tops_low], got_leaf + [own, x_start, cost_vec, omega], 0
    )
    back_leaf = gather_leaf(extra_root)
    (base,) = call(
        own_image, [kids_field], [extra_child, scol, coupling, y_start, right_side, omega], 2 * unit
    )
    base, *out_node = call(
        part_of(dual_node, False),
        [kids_field] + [block] * 4,
        back_node + [nback, linking, base, omega, nsend],
        2 * unit,
        held,
    )
    got_node = swap_node(out_node, 1)
    y_next, ylow, *out_leaf = call(
        dual_leaf,
        [field, field_low] + [block] * 4,
        back_leaf + [lback, linking, base, omega, lsend, extra_root, coupling, y_start, right_side],
        2 * unit,
    )
    got_leaf = sum_leaf(out_leaf)
    (own,) = call(own_adjoint, [states], [ylow, scol, coupling], 2 * unit)

    x_child_next, extra_child, *out_node = call(
        primal_second,
        [kids, kids_low] + [block] * 4,
        got_node + [own, x_child, cost_vec, omega, wrow, wcol],
        unit // 4,
        held,
    )
    back_node = swap_node(out_node, -1)
    extra_root, x_average, primal_move = call(
        part_of(primal_root, False),
        [tops_low, states, ((8, 128), F32)],
        got_leaf + [own, x_root, cost_vec, omega, x_start, x_child, x_child_next],
        0,
    )
    back_leaf = gather_leaf(extra_root)
    (base,) = call(
        own_image, [kids_field], [extra_child, scol, coupling, y_next, right_side, omega], 2 * unit
    )
    (base,) = call(
        part_of(dual_node, True), [kids_field], back_node + [nback, linking, base, omega], unit, held
    )
    y_average, load = call(
        dual_last,
        [field, ((8, 128), F32)],
        back_leaf
        + [lback, linking, base, omega, extra_root, coupling, y_next, right_side, y_start, primal_move],
        unit,
    )
    moves = sum_all(load)
    omega_new = jnp.sqrt((moves[0, 1:2] + 1e-06) / (moves[0, 0:1] + 1e-06))
    return (x_average, y_average, omega_new)


def solution(mesh):
    both = P(("leaf", "node"), None)
    flat = P(("leaf", "node"))
    return jax.shard_map(
        shards,
        mesh=mesh,
        in_specs=(both, both, both, both, P(), P(), P(), flat, flat),
        out_specs=(both, both, P()),
        check_vma=False,
    )
```

```python
import jax
import jax.numpy as jnp
from jax import lax
from jax.experimental import pallas as pl
from jax.experimental.pallas import tpu as pltpu
from jax.sharding import PartitionSpec as P

NS = 512
NC = 2048
ROOTS = 32
CHILD = 256
NODES = 288
N_LEAF = 16
N_NODE = 8
CAP_NODE = 64
SLOTS = 512
TILE = 512
VMEM_LIMIT = 24 * 2**20
STEP = 0.3
F32 = jnp.float32
BF16 = jnp.bfloat16
ROWS = slice(ROOTS, NODES)


def times(a, b):
    return lax.dot_general(a, b, (((1,), (0,)), ((), ())), preferred_element_type=F32)


def times_t(a, b):
    return lax.dot_general(a, b, (((1,), (1,)), ((), ())), preferred_element_type=F32)


def hot_rows(code, count):
    places = lax.broadcasted_iota(jnp.int32, (count, code.shape[1]), 0).astype(F32)
    return jnp.where(places == code, 1.0, 0.0).astype(BF16)


def hot_lanes(code, count):
    wide = jnp.concatenate([code] * (count // 128), axis=1)
    places = lax.broadcasted_iota(jnp.int32, wide.shape, 1).astype(F32)
    return jnp.where(places == wide, 1.0, 0.0).astype(BF16)


def to_lanes(row):
    return jnp.broadcast_to(row, (128, row.shape[1])).T


def call(kernel, outs, arrays, flops, scratch=(), far=()):
    out_shapes = [jax.ShapeDtypeStruct(shape, dtype) for shape, dtype in outs]
    moved = sum(a.size * a.dtype.itemsize for a in list(arrays) + out_shapes)
    out_shapes = [pltpu.VMEM(shape, dtype) for shape, dtype in outs]
    arrays = [
        pltpu.with_memory_space_constraint(a, pltpu.HBM) if i in far else a for i, a in enumerate(arrays)
    ]
    return pl.pallas_call(
        kernel,
        out_shape=out_shapes,
        in_specs=[pl.BlockSpec(memory_space=pl.ANY if i in far else pltpu.VMEM) for i in range(len(arrays))],
        out_specs=[pl.BlockSpec(memory_space=pltpu.VMEM)] * len(outs),
        scratch_shapes=list(scratch),
        compiler_params=pltpu.CompilerParams(vmem_limit_bytes=VMEM_LIMIT),
        cost_estimate=pl.CostEstimate(flops=flops, bytes_accessed=moved // 8, transcendentals=0),
    )(*arrays)


def parts():
    return [slice(i * TILE, (i + 1) * TILE) for i in range(NC // TILE)]


def first(code, y_far, linking_far, *refs):
    *outs, y, linking, ylow, nsend, nback, lsend, lback, scol, sem = refs
    chunks = parts()
    copies = []
    for cols in chunks:
        copies.append((y_far.at[:, cols], y.at[:, cols]))
        copies.append((linking_far.at[1, cols], linking.at[1, cols]))
    for cols in chunks:
        copies.append((linking_far.at[0, cols], linking.at[0, cols]))
    copies = [pltpu.make_async_copy(a, b, sem.at[i]) for i, (a, b) in enumerate(copies)]
    for copy in copies:
        copy.start()
    packed = code[...]
    upper = ((packed >> 16) & 3) == 1
    parent = packed & 0xFFFF
    here = packed >> 18
    owner = ((parent.astype(F32) + 0.5) * (1.0 / NODES)).astype(jnp.int32)
    local = parent - owner * NODES
    ry = ((owner >> 5) - (here >> 5)) & 3
    rz = ((owner >> 3) - (here >> 3)) & 3
    rx = ((owner >> 1) - (here >> 1)) & 3
    rc = (owner ^ here) & 1
    lrow = jnp.where(upper, ry * 128 + rz * ROOTS + local, -1).astype(F32)
    lend = jnp.where(upper, ((-ry) & 3) * 128 + ((-rz) & 3) * ROOTS + local, -1).astype(F32)
    peer = rx * 2 + rc
    peers = lax.broadcasted_iota(jnp.int32, (N_NODE, CHILD), 0)
    member = jnp.where((peers == peer) & jnp.logical_not(upper), 1.0, 0.0)
    before = lax.broadcasted_iota(jnp.int32, (CHILD, CHILD), 0) <= lax.broadcasted_iota(
        jnp.int32, (CHILD, CHILD), 1
    )
    counts = times(member.astype(BF16), jnp.where(before, 1.0, 0.0).astype(BF16))
    rank = jnp.sum(member * counts, axis=0, keepdims=True) - 1.0
    nrow = jnp.where(upper, -1.0, (peer * CAP_NODE).astype(F32) + rank)
    nend = jnp.where(upper, -1.0, (rc * 256 + rx * CAP_NODE).astype(F32) + rank)
    mark = jnp.where(upper, 0, local - (ROOTS - 1)).astype(F32)
    nsend[...] = nrow
    lsend[...] = lrow
    nback[...] = to_lanes(nend)
    lback[...] = to_lanes(lend)
    scol[...] = to_lanes(jnp.where(upper, 1.0, 2.0))
    total = None
    for i, cols in enumerate(chunks):
        copies[2 * i].wait()
        copies[2 * i + 1].wait()
        low = y[:, cols].astype(BF16)
        ylow[:, cols] = low
        term = times(low[ROWS], linking[1, cols])
        total = term if total is None else total + term
    load = jnp.concatenate([total.astype(BF16), to_lanes(mark).astype(BF16)], axis=1)
    spread(nrow, load, outs[:4])
    total = None
    for i, cols in enumerate(chunks):
        copies[2 * len(chunks) + i].wait()
        term = times(ylow[ROWS, cols], linking[0, cols])
        total = term if total is None else total + term
    spread(lrow, total.astype(BF16), outs[4:])


def spread(row, load, outs):
    hot = hot_rows(row, SLOTS)
    for k, out in enumerate(outs):
        out[...] = times(hot[k * 128 : (k + 1) * 128], load).astype(BF16)


def own_adjoint(ylow, scol, coupling, own):
    own[:ROOTS] = times(ylow[:ROOTS], coupling[0])
    upper = jnp.concatenate([scol[...]] * (NS // 128), axis=1) == 1.0
    low = ylow[ROWS]
    own[ROWS] = jnp.where(upper, times(low, coupling[1]), times(low, coupling[2]))


def join(blocks, swapped, held):
    for k, block in enumerate(blocks):
        held[k * CAP_NODE : (k + 1) * CAP_NODE] = block[:CAP_NODE]
    held[256:] = swapped[...]


def primal_first(g0, g1, g2, g3, swapped, own, x, cost, rates, wrow, wcol, x_next, extra, *refs):
    *sends, held = refs
    join((g0, g1, g2, g3), swapped, held)
    mark = held[:, NS:].astype(F32)
    row = mark.T[:8]
    wcol[...] = mark
    wrow[...] = row
    primal_child(held[:, :NS], own, x[ROWS], cost, rates, mark, row, x_next, extra, sends)


def primal_second(g0, g1, g2, g3, swapped, own, x, cost, rates, wrow, wcol, x_next, extra, *refs):
    *sends, held = refs
    join((g0, g1, g2, g3), swapped, held)
    primal_child(held[...], own, x[...], cost, rates, wcol[...], wrow[...], x_next, extra, sends)


def primal_child(got, own, x_old, cost, rates, mark, row, x_next, extra, sends):
    tau = rates[:1, :1]
    adjoint = own[ROWS] + times(hot_rows(row[:1] - 1.0, CHILD), got)
    new = jnp.maximum(x_old - tau * (cost[ROWS] - adjoint), 0.0)
    low = (2.0 * new - x_old).astype(BF16)
    x_next[...] = new
    extra[...] = low
    reply = times(hot_lanes(mark - 1.0, CHILD), low).astype(BF16)
    for k, send in enumerate(sends):
        send[:CAP_NODE] = reply[k * CAP_NODE : (k + 1) * CAP_NODE]
        send[CAP_NODE:] = reply[256 + k * CAP_NODE : 256 + (k + 1) * CAP_NODE]


def primal_root(first, g0, g1, g2, g3, own, x, cost, rates, *refs):
    if first:
        x_next, extra = refs
        x_old = x[:ROOTS]
    else:
        x_start, x_child, x_child_next, extra, average, move = refs
        x_old = x[...]
    tau = rates[:1, :1]
    adjoint = own[:ROOTS]
    for got in (g0, g1, g2, g3):
        adjoint = adjoint + got[...].astype(F32)
    new = jnp.maximum(x_old - tau * (cost[:ROOTS] - adjoint), 0.0)
    extra[...] = (2.0 * new - x_old).astype(BF16)
    if first:
        x_next[...] = new
    else:
        roots = (x_old + new) * 0.5
        children = (x_child[...] + x_child_next[...]) * 0.5
        average[:ROOTS] = roots
        average[ROWS] = children
        gap_roots = roots - x_start[:ROOTS]
        gap_children = children - x_start[ROWS]
        total = jnp.sum(gap_roots * gap_roots) + jnp.sum(gap_children * gap_children)
        move[...] = jnp.full((8, 128), total, F32)


def own_image(extra_child, scol, coupling, y, right, rates, base):
    sigma = rates[1:2, :1]
    upper = jnp.concatenate([scol[...]] * (TILE // 128), axis=1) == 1.0
    child = extra_child[...]
    for cols in parts():
        image = jnp.where(
            upper, times_t(child, coupling[1, cols]), times_t(child, coupling[2, cols])
        )
        base[:, cols] = y[ROWS, cols] + sigma * (right[ROWS, cols] - image)


def dual_node(last, g0, g1, g2, g3, swapped, nback, linking, base, rates, *refs):
    if last:
        later, held = refs
    else:
        nsend, later, *outs, held = refs
    join((g0, g1, g2, g3), swapped, held)
    rows = times(hot_lanes(nback[...], SLOTS), held[...]).astype(BF16)
    sigma = rates[1:2, :1]
    total = None
    for cols in parts():
        weights = linking[1, cols]
        new = base[:, cols] - sigma * times_t(rows, weights)
        later[:, cols] = new
        if not last:
            product = times(jnp.maximum(new, 0.0).astype(BF16), weights)
            total = product if total is None else total + product
    if not last:
        spread(nsend[...], total.astype(BF16), outs)


def from_leaf(blocks, lback):
    hot = hot_lanes(lback[...], SLOTS)
    rows = None
    for k, block in enumerate(blocks):
        term = times(hot[:, k * 128 : (k + 1) * 128], block[...])
        rows = term if rows is None else rows + term
    return rows.astype(BF16)


def dual_leaf(b0, b1, b2, b3, lback, linking, base, rates, lsend, extra_root, coupling, y, right, *refs):
    y_next, ylow, *outs = refs
    rows = from_leaf((b0, b1, b2, b3), lback)
    sigma = rates[1:2, :1]
    root = extra_root[...]
    total = None
    for cols in parts():
        weights = linking[0, cols]
        image_root = times_t(root, coupling[0, cols])
        new_root = jnp.maximum(y[:ROOTS, cols] + sigma * (right[:ROOTS, cols] - image_root), 0.0)
        new = jnp.maximum(base[:, cols] - sigma * times_t(rows, weights), 0.0)
        low = new.astype(BF16)
        y_next[:ROOTS, cols] = new_root
        y_next[ROWS, cols] = new
        ylow[:ROOTS, cols] = new_root.astype(BF16)
        ylow[ROWS, cols] = low
        product = times(low, weights)
        total = product if total is None else total + product
    spread(lsend[...], total.astype(BF16), outs)


def dual_last(
    b0, b1, b2, b3, lback, linking, base, rates, extra_root, coupling, y, right, y_start, primal_move,
    average, load
):
    rows = from_leaf((b0, b1, b2, b3), lback)
    sigma = rates[1:2, :1]
    root = extra_root[...]
    move = jnp.zeros((1, TILE), F32)
    for cols in parts():
        image_root = times_t(root, coupling[0, cols])
        new_root = jnp.maximum(y[:ROOTS, cols] + sigma * (right[:ROOTS, cols] - image_root), 0.0)
        new = jnp.maximum(base[:, cols] - sigma * times_t(rows, linking[0, cols]), 0.0)
        mean_root = (y[:ROOTS, cols] + new_root) * 0.5
        mean = (y[ROWS, cols] + new) * 0.5
        average[:ROOTS, cols] = mean_root
        average[ROWS, cols] = mean
        gap_root = mean_root - y_start[:ROOTS, cols]
        gap = mean - y_start[ROWS, cols]
        move = move + jnp.sum(gap_root * gap_root, axis=0, keepdims=True)
        move = move + jnp.sum(gap * gap, axis=0, keepdims=True)
    lane = lax.broadcasted_iota(jnp.int32, (8, 128), 1)
    load[...] = jnp.where(lane == 0, primal_move[...], jnp.sum(move))


def along(axis, size, stride, ring, change):
    pairs = []
    for i in range(size):
        digit = (i // stride) % ring
        pairs.append((i, i + (change(digit) - digit) * stride))
    return pairs


def ring_y(k):
    return "leaf", along("leaf", N_LEAF, 4, 4, lambda d: (d + k) % 4)


def ring_z(k):
    return "leaf", along("leaf", N_LEAF, 1, 4, lambda d: (d + k) % 4)


def ring_x(k):
    return "node", along("node", N_NODE, 2, 4, lambda d: (d + k) % 4)


def sibling(array):
    return lax.ppermute(array, "node", along("node", N_NODE, 1, 2, lambda d: 1 - d))


def shifted(blocks, ring, sign=1):
    got = {0: blocks[0]}
    for k in (2, 1, 3):
        got[k] = lax.ppermute(blocks[k], *ring((sign * k) % 4))
    return [got[k] for k in range(4)]


def swap_node(blocks, sign, beside=None):
    got = shifted(blocks, ring_x, sign)
    halves = jnp.concatenate([block[CAP_NODE:] for block in got], axis=0)
    if beside is not None:
        halves, beside = lax.optimization_barrier((halves, beside))
        return got + [sibling(halves)], beside
    return got + [sibling(halves)]


def sum_leaf(blocks, beside):
    got = [block.astype(F32) for block in shifted(blocks, ring_y)]
    total = (((got[0] + got[1]) + got[2]) + got[3]).astype(BF16)
    total, beside = lax.optimization_barrier((total, beside))
    return shifted([total[k * ROOTS : (k + 1) * ROOTS] for k in range(4)], ring_z), beside


def gather_leaf(rows):
    plane = jnp.concatenate(shifted([rows] * 4, ring_z), axis=0)
    return shifted([plane] * 4, ring_y)


def sum_all(load):
    load = load + sibling(load)
    for axis, size, stride in (("node", N_NODE, 2), ("leaf", N_LEAF, 1), ("leaf", N_LEAF, 4)):
        got = [
            lax.ppermute(load, axis, along(axis, size, stride, 4, lambda d, k=k: d ^ k)) for k in (1, 2, 3)
        ]
        load = (load + got[0]) + (got[1] + got[2])
    return load


def part_of(kernel, flag):
    def run(*refs):
        kernel(flag, *refs)

    return run


def shards(x_start, y_start, cost_vec, right_side, omega, coupling, linking, parent, section):
    unit = 2 * CHILD * NS * NC
    here = lax.axis_index("leaf") * N_NODE + lax.axis_index("node")
    code = ((here * 4 + section) * 65536 + parent)[ROOTS:].reshape(1, CHILD)
    rates = jnp.broadcast_to(jnp.stack([STEP / omega[0], STEP * omega[0]])[:, None], (2, 128))
    field = ((NODES, NC), F32)
    field_low = ((NODES, NC), BF16)
    states = ((NODES, NS), F32)
    block = ((128, NS), BF16)
    block_mark = ((128, NS + 128), BF16)
    kids = ((CHILD, NS), F32)
    kids_low = ((CHILD, NS), BF16)
    kids_field = ((CHILD, NC), F32)
    tops = ((ROOTS, NS), F32)
    tops_low = ((ROOTS, NS), BF16)
    row = ((1, CHILD), F32)
    col = ((CHILD, 128), F32)
    held = [pltpu.VMEM((SLOTS, NS), BF16)]

    *sent, y_start, linking, ylow, nsend, nback, lsend, lback, scol = call(
        first,
        [block_mark] * 4 + [block] * 4
        + [field, ((2, NC, NS), BF16), field_low, row, col, row, col, col],
        [code, y_start, linking],
        2 * unit,
        [pltpu.SemaphoreType.DMA((3 * NC // TILE,))],
        (1, 2),
    )
    coupling, sent = lax.optimization_barrier((coupling, sent))
    got_node = swap_node(sent[:4], 1)
    (own,) = call(own_adjoint, [states], [ylow, scol, coupling], 2 * unit)
    got_leaf, own = sum_leaf(sent[4:], own)

    wrow, wcol, x_child, extra_child, *out_node = call(
        primal_first,
        [((8, SLOTS), F32), ((SLOTS, 128), F32), kids, kids_low] + [block] * 4,
        got_node + [own, x_start, cost_vec, rates],
        unit // 4,
        [pltpu.VMEM((SLOTS, NS + 128), BF16)],
    )
    (base,) = call(
        own_image, [kids_field], [extra_child, scol, coupling, y_start, right_side, rates], 2 * unit
    )
    back_node, base = swap_node(out_node, -1, base)
    x_root, extra_root = call(
        part_of(primal_root, True), [tops, tops_low], got_leaf + [own, x_start, cost_vec, rates], 0
    )
    back_leaf = gather_leaf(extra_root)
    base, *out_node = call(
        part_of(dual_node, False),
        [kids_field] + [block] * 4,
        back_node + [nback, linking, base, rates, nsend],
        2 * unit,
        held,
    )
    got_node = swap_node(out_node, 1)
    y_next, ylow, *out_leaf = call(
        dual_leaf,
        [field, field_low] + [block] * 4,
        back_leaf + [lback, linking, base, rates, lsend, extra_root, coupling, y_start, right_side],
        2 * unit,
    )
    (own,) = call(own_adjoint, [states], [ylow, scol, coupling], 2 * unit)
    got_leaf, own = sum_leaf(out_leaf, own)

    x_child_next, extra_child, *out_node = call(
        primal_second,
        [kids, kids_low] + [block] * 4,
        got_node + [own, x_child, cost_vec, rates, wrow, wcol],
        unit // 4,
        held,
    )
    (base,) = call(
        own_image, [kids_field], [extra_child, scol, coupling, y_next, right_side, rates], 2 * unit
    )
    back_node, base = swap_node(out_node, -1, base)
    extra_root, x_average, primal_move = call(
        part_of(primal_root, False),
        [tops_low, states, ((8, 128), F32)],
        got_leaf + [own, x_root, cost_vec, rates, x_start, x_child, x_child_next],
        0,
    )
    back_leaf = gather_leaf(extra_root)
    (base,) = call(
        part_of(dual_node, True), [kids_field], back_node + [nback, linking, base, rates], unit, held
    )
    y_average, load = call(
        dual_last,
        [field, ((8, 128), F32)],
        back_leaf
        + [lback, linking, base, rates, extra_root, coupling, y_next, right_side, y_start, primal_move],
        unit,
    )
    moves = sum_all(load)
    omega_new = jnp.sqrt((moves[0, 1:2] + 1e-06) / (moves[0, 0:1] + 1e-06))
    return (x_average, y_average, omega_new)


def solution(mesh):
    both = P(("leaf", "node"), None)
    flat = P(("leaf", "node"))
    return jax.shard_map(
        shards,
        mesh=mesh,
        in_specs=(both, both, both, both, P(), P(), P(), flat, flat),
        out_specs=(both, both, P()),
        check_vma=False,
    )
```

```python
import jax
import jax.numpy as jnp
from jax import lax
from jax.experimental import pallas as pl
from jax.experimental.pallas import tpu as pltpu
from jax.sharding import PartitionSpec as P

NS = 512
NC = 2048
ROOTS = 32
CHILD = 256
NODES = 288
N_LEAF = 16
N_NODE = 8
CAP_NODE = 64
SLOTS = 512
TILE = 512
VMEM_LIMIT = 24 * 2**20
STEP = 0.3
F32 = jnp.float32
BF16 = jnp.bfloat16
ROWS = slice(ROOTS, NODES)


def times(a, b):
    return lax.dot_general(a, b, (((1,), (0,)), ((), ())), preferred_element_type=F32)


def times_t(a, b):
    return lax.dot_general(a, b, (((1,), (1,)), ((), ())), preferred_element_type=F32)


def hot_rows(code, count):
    places = lax.broadcasted_iota(jnp.int32, (count, code.shape[1]), 0).astype(F32)
    return jnp.where(places == code, 1.0, 0.0).astype(BF16)


def hot_lanes(code, count):
    wide = jnp.concatenate([code] * (count // 128), axis=1)
    places = lax.broadcasted_iota(jnp.int32, wide.shape, 1).astype(F32)
    return jnp.where(places == wide, 1.0, 0.0).astype(BF16)


def to_lanes(row):
    return jnp.broadcast_to(row, (128, row.shape[1])).T


def call(kernel, outs, arrays, flops, scratch=(), far=()):
    out_shapes = [jax.ShapeDtypeStruct(shape, dtype) for shape, dtype in outs]
    moved = sum(a.size * a.dtype.itemsize for a in list(arrays) + out_shapes)
    out_shapes = [pltpu.VMEM(shape, dtype) for shape, dtype in outs]
    arrays = [
        pltpu.with_memory_space_constraint(a, pltpu.HBM) if i in far else a for i, a in enumerate(arrays)
    ]
    return pl.pallas_call(
        kernel,
        out_shape=out_shapes,
        in_specs=[pl.BlockSpec(memory_space=pl.ANY if i in far else pltpu.VMEM) for i in range(len(arrays))],
        out_specs=[pl.BlockSpec(memory_space=pltpu.VMEM)] * len(outs),
        scratch_shapes=list(scratch),
        compiler_params=pltpu.CompilerParams(vmem_limit_bytes=VMEM_LIMIT),
        cost_estimate=pl.CostEstimate(flops=flops, bytes_accessed=moved // 8, transcendentals=0),
    )(*arrays)


def parts():
    return [slice(i * TILE, (i + 1) * TILE) for i in range(NC // TILE)]


def first(code, y_far, linking_far, *refs):
    *outs, y, linking, ylow, nsend, nback, lsend, lback, scol, sem = refs
    chunks = parts()
    copies = []
    for cols in chunks:
        copies.append((y_far.at[:, cols], y.at[:, cols]))
        copies.append((linking_far.at[1, cols], linking.at[1, cols]))
    for cols in chunks:
        copies.append((linking_far.at[0, cols], linking.at[0, cols]))
    copies = [pltpu.make_async_copy(a, b, sem.at[i]) for i, (a, b) in enumerate(copies)]
    for copy in copies:
        copy.start()
    packed = code[...]
    upper = ((packed >> 16) & 3) == 1
    parent = packed & 0xFFFF
    here = packed >> 18
    owner = ((parent.astype(F32) + 0.5) * (1.0 / NODES)).astype(jnp.int32)
    local = parent - owner * NODES
    ry = ((owner >> 5) - (here >> 5)) & 3
    rz = ((owner >> 3) - (here >> 3)) & 3
    rx = ((owner >> 1) - (here >> 1)) & 3
    rc = (owner ^ here) & 1
    lrow = jnp.where(upper, ry * 128 + rz * ROOTS + local, -1).astype(F32)
    lend = jnp.where(upper, ((-ry) & 3) * 128 + ((-rz) & 3) * ROOTS + local, -1).astype(F32)
    peer = rx * 2 + rc
    peers = lax.broadcasted_iota(jnp.int32, (N_NODE, CHILD), 0)
    member = jnp.where((peers == peer) & jnp.logical_not(upper), 1.0, 0.0)
    before = lax.broadcasted_iota(jnp.int32, (CHILD, CHILD), 0) <= lax.broadcasted_iota(
        jnp.int32, (CHILD, CHILD), 1
    )
    counts = times(member.astype(BF16), jnp.where(before, 1.0, 0.0).astype(BF16))
    rank = jnp.sum(member * counts, axis=0, keepdims=True) - 1.0
    nrow = jnp.where(upper, -1.0, (peer * CAP_NODE).astype(F32) + rank)
    nend = jnp.where(upper, -1.0, (rc * 256 + rx * CAP_NODE).astype(F32) + rank)
    mark = jnp.where(upper, 0, local - (ROOTS - 1)).astype(F32)
    nsend[...] = nrow
    lsend[...] = lrow
    nback[...] = to_lanes(nend)
    lback[...] = to_lanes(lend)
    scol[...] = to_lanes(jnp.where(upper, 1.0, 2.0))
    total = None
    for i, cols in enumerate(chunks):
        copies[2 * i].wait()
        copies[2 * i + 1].wait()
        low = y[:, cols].astype(BF16)
        ylow[:, cols] = low
        term = times(low[ROWS], linking[1, cols])
        total = term if total is None else total + term
    load = jnp.concatenate([total.astype(BF16), to_lanes(mark).astype(BF16)], axis=1)
    spread(nrow, load, outs[:4])
    total = None
    for i, cols in enumerate(chunks):
        copies[2 * len(chunks) + i].wait()
        term = times(ylow[ROWS, cols], linking[0, cols])
        total = term if total is None else total + term
    spread(lrow, total.astype(BF16), outs[4:])


def spread(row, load, outs):
    hot = hot_rows(row, SLOTS)
    for k, out in enumerate(outs):
        out[...] = times(hot[k * 128 : (k + 1) * 128], load).astype(BF16)


def own_adjoint(ylow, scol, coupling, own):
    own[:ROOTS] = times(ylow[:ROOTS], coupling[0])
    upper = jnp.concatenate([scol[...]] * (NS // 128), axis=1) == 1.0
    low = ylow[ROWS]
    own[ROWS] = jnp.where(upper, times(low, coupling[1]), times(low, coupling[2]))


def join(blocks, swapped, held):
    for k, block in enumerate(blocks):
        held[k * CAP_NODE : (k + 1) * CAP_NODE] = block[:CAP_NODE]
    held[256:] = swapped[...]


def primal_first(g0, g1, g2, g3, swapped, own, x, cost, rates, wrow, wcol, x_next, extra, *refs):
    *sends, held = refs
    join((g0, g1, g2, g3), swapped, held)
    mark = held[:, NS:].astype(F32)
    row = mark.T[:8]
    wcol[...] = mark
    wrow[...] = row
    primal_child(held[:, :NS], own, x[ROWS], cost, rates, mark, row, x_next, extra, sends)


def primal_second(g0, g1, g2, g3, swapped, own, x, cost, rates, wrow, wcol, x_next, extra, *refs):
    *sends, held = refs
    join((g0, g1, g2, g3), swapped, held)
    primal_child(held[...], own, x[...], cost, rates, wcol[...], wrow[...], x_next, extra, sends)


def primal_child(got, own, x_old, cost, rates, mark, row, x_next, extra, sends):
    tau = rates[:1, :1]
    adjoint = own[ROWS] + times(hot_rows(row[:1] - 1.0, CHILD), got)
    new = jnp.maximum(x_old - tau * (cost[ROWS] - adjoint), 0.0)
    low = (2.0 * new - x_old).astype(BF16)
    x_next[...] = new
    extra[...] = low
    reply = times(hot_lanes(mark - 1.0, CHILD), low).astype(BF16)
    for k, send in enumerate(sends):
        send[:CAP_NODE] = reply[k * CAP_NODE : (k + 1) * CAP_NODE]
        send[CAP_NODE:] = reply[256 + k * CAP_NODE : 256 + (k + 1) * CAP_NODE]


def primal_root(first, g0, g1, g2, g3, own, x, cost, rates, *refs):
    if first:
        x_next, extra = refs
        x_old = x[:ROOTS]
    else:
        x_start, x_child, x_child_next, extra, average, move = refs
        x_old = x[...]
    tau = rates[:1, :1]
    adjoint = own[:ROOTS]
    for got in (g0, g1, g2, g3):
        adjoint = adjoint + got[...].astype(F32)
    new = jnp.maximum(x_old - tau * (cost[:ROOTS] - adjoint), 0.0)
    extra[...] = (2.0 * new - x_old).astype(BF16)
    if first:
        x_next[...] = new
    else:
        roots = (x_old + new) * 0.5
        children = (x_child[...] + x_child_next[...]) * 0.5
        average[:ROOTS] = roots
        average[ROWS] = children
        gap_roots = roots - x_start[:ROOTS]
        gap_children = children - x_start[ROWS]
        total = jnp.sum(gap_roots * gap_roots) + jnp.sum(gap_children * gap_children)
        move[...] = jnp.full((8, 128), total, F32)


def own_image(extra_child, scol, coupling, y, right, rates, base):
    sigma = rates[1:2, :1]
    upper = jnp.concatenate([scol[...]] * (TILE // 128), axis=1) == 1.0
    child = extra_child[...]
    for cols in parts():
        image = jnp.where(
            upper, times_t(child, coupling[1, cols]), times_t(child, coupling[2, cols])
        )
        base[:, cols] = y[ROWS, cols] + sigma * (right[ROWS, cols] - image)


def dual_node(last, g0, g1, g2, g3, swapped, nback, linking, base, rates, *refs):
    if last:
        later, held = refs
    else:
        nsend, later, *outs, held = refs
    join((g0, g1, g2, g3), swapped, held)
    rows = times(hot_lanes(nback[...], SLOTS), held[...]).astype(BF16)
    sigma = rates[1:2, :1]
    total = None
    for cols in parts():
        weights = linking[1, cols]
        new = base[:, cols] - sigma * times_t(rows, weights)
        later[:, cols] = new
        if not last:
            product = times(jnp.maximum(new, 0.0).astype(BF16), weights)
            total = product if total is None else total + product
    if not last:
        spread(nsend[...], total.astype(BF16), outs)


def from_leaf(blocks, lback):
    hot = hot_lanes(lback[...], SLOTS)
    rows = None
    for k, block in enumerate(blocks):
        term = times(hot[:, k * 128 : (k + 1) * 128], block[...])
        rows = term if rows is None else rows + term
    return rows.astype(BF16)


def dual_leaf(b0, b1, b2, b3, lback, linking, base, rates, lsend, extra_root, coupling, y, right, *refs):
    y_next, ylow, *outs = refs
    rows = from_leaf((b0, b1, b2, b3), lback)
    sigma = rates[1:2, :1]
    root = extra_root[...]
    total = None
    for cols in parts():
        weights = linking[0, cols]
        image_root = times_t(root, coupling[0, cols])
        new_root = jnp.maximum(y[:ROOTS, cols] + sigma * (right[:ROOTS, cols] - image_root), 0.0)
        new = jnp.maximum(base[:, cols] - sigma * times_t(rows, weights), 0.0)
        low = new.astype(BF16)
        y_next[:ROOTS, cols] = new_root
        y_next[ROWS, cols] = new
        ylow[:ROOTS, cols] = new_root.astype(BF16)
        ylow[ROWS, cols] = low
        product = times(low, weights)
        total = product if total is None else total + product
    spread(lsend[...], total.astype(BF16), outs)


def dual_last(
    b0, b1, b2, b3, lback, linking, base, rates, extra_root, coupling, y, right, y_start, primal_move,
    average, load
):
    rows = from_leaf((b0, b1, b2, b3), lback)
    sigma = rates[1:2, :1]
    root = extra_root[...]
    move = jnp.zeros((1, TILE), F32)
    for cols in parts():
        image_root = times_t(root, coupling[0, cols])
        new_root = jnp.maximum(y[:ROOTS, cols] + sigma * (right[:ROOTS, cols] - image_root), 0.0)
        new = jnp.maximum(base[:, cols] - sigma * times_t(rows, linking[0, cols]), 0.0)
        mean_root = (y[:ROOTS, cols] + new_root) * 0.5
        mean = (y[ROWS, cols] + new) * 0.5
        average[:ROOTS, cols] = mean_root
        average[ROWS, cols] = mean
        gap_root = mean_root - y_start[:ROOTS, cols]
        gap = mean - y_start[ROWS, cols]
        move = move + jnp.sum(gap_root * gap_root, axis=0, keepdims=True)
        move = move + jnp.sum(gap * gap, axis=0, keepdims=True)
    lane = lax.broadcasted_iota(jnp.int32, load.shape, 2)
    load[...] = jnp.where(lane == 0, primal_move[:1], jnp.sum(move))


def along(axis, size, stride, ring, change):
    pairs = []
    for i in range(size):
        digit = (i // stride) % ring
        pairs.append((i, i + (change(digit) - digit) * stride))
    return pairs


def ring_y(k):
    return "leaf", along("leaf", N_LEAF, 4, 4, lambda d: (d + k) % 4)


def ring_z(k):
    return "leaf", along("leaf", N_LEAF, 1, 4, lambda d: (d + k) % 4)


def ring_x(k):
    return "node", along("node", N_NODE, 2, 4, lambda d: (d + k) % 4)


def sibling(array):
    return lax.ppermute(array, "node", along("node", N_NODE, 1, 2, lambda d: 1 - d))


def shifted(blocks, ring, sign=1):
    got = {0: blocks[0]}
    for k in (2, 1, 3):
        got[k] = lax.ppermute(blocks[k], *ring((sign * k) % 4))
    return [got[k] for k in range(4)]


def swap_node(blocks, sign, before):
    got = shifted(blocks, ring_x, sign)
    halves = jnp.concatenate([block[CAP_NODE:] for block in got], axis=0)
    halves, before = lax.optimization_barrier((halves, before))
    return got + [sibling(halves)], before


def sum_leaf(blocks, beside):
    got = [block.astype(F32) for block in shifted(blocks, ring_y)]
    total = (((got[0] + got[1]) + got[2]) + got[3]).astype(BF16)
    total, beside = lax.optimization_barrier((total, beside))
    return shifted([total[k * ROOTS : (k + 1) * ROOTS] for k in range(4)], ring_z), beside


def part_of(kernel, flag):
    def run(*refs):
        kernel(flag, *refs)

    return run


def shards(x_start, y_start, cost_vec, right_side, omega, coupling, linking, parent, section):
    unit = 2 * CHILD * NS * NC
    here = lax.axis_index("leaf") * N_NODE + lax.axis_index("node")
    code = ((here * 4 + section) * 65536 + parent)[ROOTS:].reshape(1, CHILD)
    rates = jnp.broadcast_to(jnp.stack([STEP / omega[0], STEP * omega[0]])[:, None], (2, 128))
    field = ((NODES, NC), F32)
    field_low = ((NODES, NC), BF16)
    states = ((NODES, NS), F32)
    block = ((128, NS), BF16)
    block_mark = ((128, NS + 128), BF16)
    kids = ((CHILD, NS), F32)
    kids_low = ((CHILD, NS), BF16)
    kids_field = ((CHILD, NC), F32)
    tops = ((ROOTS, NS), F32)
    tops_low = ((ROOTS, NS), BF16)
    row = ((1, CHILD), F32)
    col = ((CHILD, 128), F32)
    held = [pltpu.VMEM((SLOTS, NS), BF16)]

    *sent, y_start, linking, ylow, nsend, nback, lsend, lback, scol = call(
        first,
        [block_mark] * 4 + [block] * 4
        + [field, ((2, NC, NS), BF16), field_low, row, col, row, col, col],
        [code, y_start, linking],
        2 * unit,
        [pltpu.SemaphoreType.DMA((3 * NC // TILE,))],
        (1, 2),
    )
    coupling, sent = lax.optimization_barrier((coupling, sent))
    (own,) = call(own_adjoint, [states], [ylow, scol, coupling], 2 * unit)
    got_leaf, own = sum_leaf(sent[4:], own)
    got_node, got_leaf = swap_node(sent[:4], 1, got_leaf)

    wrow, wcol, x_child, extra_child, *out_node = call(
        primal_first,
        [((8, SLOTS), F32), ((SLOTS, 128), F32), kids, kids_low] + [block] * 4,
        got_node + [own, x_start, cost_vec, rates],
        unit // 4,
        [pltpu.VMEM((SLOTS, NS + 128), BF16)],
    )
    (base,) = call(
        own_image, [kids_field], [extra_child, scol, coupling, y_start, right_side, rates], 2 * unit
    )
    x_root, extra_root = call(
        part_of(primal_root, True), [tops, tops_low], got_leaf + [own, x_start, cost_vec, rates], 0
    )
    plane = jnp.concatenate(shifted([extra_root] * 4, ring_z), axis=0)
    back_node, (plane, base) = swap_node(out_node, -1, (plane, base))
    back_leaf = shifted([plane] * 4, ring_y)
    base, *out_node = call(
        part_of(dual_node, False),
        [kids_field] + [block] * 4,
        back_node + [nback, linking, base, rates, nsend],
        2 * unit,
        held,
    )
    y_next, ylow, *out_leaf = call(
        dual_leaf,
        [field, field_low] + [block] * 4,
        back_leaf + [lback, linking, base, rates, lsend, extra_root, coupling, y_start, right_side],
        2 * unit,
    )
    (own,) = call(own_adjoint, [states], [ylow, scol, coupling], 2 * unit)
    got_leaf, own = sum_leaf(out_leaf, own)
    got_node, got_leaf = swap_node(out_node, 1, got_leaf)

    x_child_next, extra_child, *out_node = call(
        primal_second,
        [kids, kids_low] + [block] * 4,
        got_node + [own, x_child, cost_vec, rates, wrow, wcol],
        unit // 4,
        held,
    )
    (base,) = call(
        own_image, [kids_field], [extra_child, scol, coupling, y_next, right_side, rates], 2 * unit
    )
    extra_root, x_average, primal_move = call(
        part_of(primal_root, False),
        [tops_low, states, ((8, 128), F32)],
        got_leaf + [own, x_root, cost_vec, rates, x_start, x_child, x_child_next],
        0,
    )
    plane = jnp.concatenate(shifted([extra_root] * 4, ring_z), axis=0)
    back_node, (plane, base) = swap_node(out_node, -1, (plane, base))
    back_leaf = shifted([plane] * 4, ring_y)
    (base,) = call(
        part_of(dual_node, True), [kids_field], back_node + [nback, linking, base, rates], unit, held
    )
    y_average, load = call(
        dual_last,
        [field, ((N_LEAF * N_NODE, 1, 128), F32)],
        back_leaf
        + [lback, linking, base, rates, extra_root, coupling, y_next, right_side, y_start, primal_move],
        unit,
    )
    moves = lax.all_to_all(load, ("leaf", "node"), split_axis=0, concat_axis=0, tiled=True)
    moves = jnp.sum(moves[:, 0, :2], axis=0)
    omega_new = jnp.sqrt((moves[1:] + 1e-06) / (moves[:1] + 1e-06))
    return (x_average, y_average, omega_new)


def solution(mesh):
    both = P(("leaf", "node"), None)
    flat = P(("leaf", "node"))
    return jax.shard_map(
        shards,
        mesh=mesh,
        in_specs=(both, both, both, both, P(), P(), P(), flat, flat),
        out_specs=(both, both, P()),
        check_vma=False,
    )
```

```python
import jax
import jax.numpy as jnp
from jax import lax
from jax.experimental import pallas as pl
from jax.experimental.pallas import tpu as pltpu
from jax.sharding import PartitionSpec as P

NS = 512
NC = 2048
ROOTS = 32
CHILD = 256
NODES = 288
N_LEAF = 16
N_NODE = 8
CAP_NODE = 64
SLOTS = 512
TILE = 512
VMEM_LIMIT = 24 * 2**20
STEP = 0.3
F32 = jnp.float32
BF16 = jnp.bfloat16
ROWS = slice(ROOTS, NODES)


def times(a, b):
    return lax.dot_general(a, b, (((1,), (0,)), ((), ())), preferred_element_type=F32)


def times_t(a, b):
    return lax.dot_general(a, b, (((1,), (1,)), ((), ())), preferred_element_type=F32)


def hot_rows(code, count):
    places = lax.broadcasted_iota(jnp.int32, (count, code.shape[1]), 0).astype(F32)
    return jnp.where(places == code, 1.0, 0.0).astype(BF16)


def hot_lanes(code, count):
    wide = jnp.concatenate([code] * (count // 128), axis=1)
    places = lax.broadcasted_iota(jnp.int32, wide.shape, 1).astype(F32)
    return jnp.where(places == wide, 1.0, 0.0).astype(BF16)


def to_lanes(row):
    return jnp.broadcast_to(row, (128, row.shape[1])).T


def call(kernel, outs, arrays, flops, scratch=(), far=()):
    out_shapes = [jax.ShapeDtypeStruct(shape, dtype) for shape, dtype in outs]
    moved = sum(a.size * a.dtype.itemsize for a in list(arrays) + out_shapes)
    out_shapes = [pltpu.VMEM(shape, dtype) for shape, dtype in outs]
    arrays = [
        pltpu.with_memory_space_constraint(a, pltpu.HBM) if i in far else a for i, a in enumerate(arrays)
    ]
    return pl.pallas_call(
        kernel,
        out_shape=out_shapes,
        in_specs=[pl.BlockSpec(memory_space=pl.ANY if i in far else pltpu.VMEM) for i in range(len(arrays))],
        out_specs=[pl.BlockSpec(memory_space=pltpu.VMEM)] * len(outs),
        scratch_shapes=list(scratch),
        compiler_params=pltpu.CompilerParams(vmem_limit_bytes=VMEM_LIMIT),
        cost_estimate=pl.CostEstimate(flops=flops, bytes_accessed=moved // 8, transcendentals=0),
    )(*arrays)


def parts():
    return [slice(i * TILE, (i + 1) * TILE) for i in range(NC // TILE)]


def first(code, y_far, linking_far, *refs):
    *outs, y, linking, ylow, nsend, nback, lsend, lback, scol, sem = refs
    chunks = parts()
    copies = []
    for cols in chunks:
        copies.append((y_far.at[:, cols], y.at[:, cols]))
        copies.append((linking_far.at[1, cols], linking.at[1, cols]))
    for cols in chunks:
        copies.append((linking_far.at[0, cols], linking.at[0, cols]))
    copies = [pltpu.make_async_copy(a, b, sem.at[i]) for i, (a, b) in enumerate(copies)]
    for copy in copies:
        copy.start()
    packed = code[...]
    upper = ((packed >> 16) & 3) == 1
    parent = packed & 0xFFFF
    here = packed >> 18
    owner = ((parent.astype(F32) + 0.5) * (1.0 / NODES)).astype(jnp.int32)
    local = parent - owner * NODES
    ry = ((owner >> 5) - (here >> 5)) & 3
    rz = ((owner >> 3) - (here >> 3)) & 3
    rx = ((owner >> 1) - (here >> 1)) & 3
    rc = (owner ^ here) & 1
    odd = (here & 1) == 1
    outer = jnp.where(odd, rz, ry)
    inner = jnp.where(odd, ry, rz)
    lrow = jnp.where(upper, outer * 128 + inner * ROOTS + local, -1).astype(F32)
    lend = jnp.where(upper, ((-outer) & 3) * 128 + ((-inner) & 3) * ROOTS + local, -1).astype(F32)
    peer = rx * 2 + rc
    peers = lax.broadcasted_iota(jnp.int32, (N_NODE, CHILD), 0)
    member = jnp.where((peers == peer) & jnp.logical_not(upper), 1.0, 0.0)
    before = lax.broadcasted_iota(jnp.int32, (CHILD, CHILD), 0) <= lax.broadcasted_iota(
        jnp.int32, (CHILD, CHILD), 1
    )
    counts = times(member.astype(BF16), jnp.where(before, 1.0, 0.0).astype(BF16))
    rank = jnp.sum(member * counts, axis=0, keepdims=True) - 1.0
    nrow = jnp.where(upper, -1.0, (peer * CAP_NODE).astype(F32) + rank)
    nend = jnp.where(upper, -1.0, (rc * 256 + rx * CAP_NODE).astype(F32) + rank)
    mark = jnp.where(upper, 0, local - (ROOTS - 1)).astype(F32)
    nsend[...] = nrow
    lsend[...] = lrow
    nback[...] = to_lanes(nend)
    lback[...] = to_lanes(lend)
    scol[...] = to_lanes(jnp.where(upper, 1.0, 2.0))
    total = None
    for i, cols in enumerate(chunks):
        copies[2 * i].wait()
        copies[2 * i + 1].wait()
        low = y[:, cols].astype(BF16)
        ylow[:, cols] = low
        term = times(low[ROWS], linking[1, cols])
        total = term if total is None else total + term
    load = jnp.concatenate([total.astype(BF16), to_lanes(mark).astype(BF16)], axis=1)
    spread(nrow, load, outs[:4])
    total = None
    for i, cols in enumerate(chunks):
        copies[2 * len(chunks) + i].wait()
        term = times(ylow[ROWS, cols], linking[0, cols])
        total = term if total is None else total + term
    spread(lrow, total.astype(BF16), outs[4:])


def spread(row, load, outs):
    hot = hot_rows(row, SLOTS)
    for k, out in enumerate(outs):
        out[...] = times(hot[k * 128 : (k + 1) * 128], load).astype(BF16)


def own_adjoint(ylow, scol, coupling, own):
    own[:ROOTS] = times(ylow[:ROOTS], coupling[0])
    upper = jnp.concatenate([scol[...]] * (NS // 128), axis=1) == 1.0
    low = ylow[ROWS]
    own[ROWS] = jnp.where(upper, times(low, coupling[1]), times(low, coupling[2]))


def join(blocks, swapped, held):
    for k, block in enumerate(blocks):
        held[k * CAP_NODE : (k + 1) * CAP_NODE] = block[:CAP_NODE]
    held[256:] = swapped[...]


def primal_first(g0, g1, g2, g3, swapped, own, x, cost, rates, wrow, wcol, x_next, extra, *refs):
    *sends, held = refs
    join((g0, g1, g2, g3), swapped, held)
    mark = held[:, NS:].astype(F32)
    row = mark.T[:8]
    wcol[...] = mark
    wrow[...] = row
    primal_child(held[:, :NS], own, x[ROWS], cost, rates, mark, row, x_next, extra, sends)


def primal_second(g0, g1, g2, g3, swapped, own, x, cost, rates, wrow, wcol, x_next, extra, *refs):
    *sends, held = refs
    join((g0, g1, g2, g3), swapped, held)
    primal_child(held[...], own, x[...], cost, rates, wcol[...], wrow[...], x_next, extra, sends)


def primal_child(got, own, x_old, cost, rates, mark, row, x_next, extra, sends):
    tau = rates[:1, :1]
    adjoint = own[ROWS] + times(hot_rows(row[:1] - 1.0, CHILD), got)
    new = jnp.maximum(x_old - tau * (cost[ROWS] - adjoint), 0.0)
    low = (2.0 * new - x_old).astype(BF16)
    x_next[...] = new
    extra[...] = low
    reply = times(hot_lanes(mark - 1.0, CHILD), low).astype(BF16)
    for k, send in enumerate(sends):
        send[:CAP_NODE] = reply[k * CAP_NODE : (k + 1) * CAP_NODE]
        send[CAP_NODE:] = reply[256 + k * CAP_NODE : 256 + (k + 1) * CAP_NODE]


def primal_root(first, g0, g1, g2, g3, own, x, cost, rates, *refs):
    if first:
        x_next, extra = refs
        x_old = x[:ROOTS]
    else:
        x_start, x_child, x_child_next, extra, average, move = refs
        x_old = x[...]
    tau = rates[:1, :1]
    adjoint = own[:ROOTS]
    for got in (g0, g1, g2, g3):
        adjoint = adjoint + got[...].astype(F32)
    new = jnp.maximum(x_old - tau * (cost[:ROOTS] - adjoint), 0.0)
    extra[...] = (2.0 * new - x_old).astype(BF16)
    if first:
        x_next[...] = new
    else:
        roots = (x_old + new) * 0.5
        children = (x_child[...] + x_child_next[...]) * 0.5
        average[:ROOTS] = roots
        average[ROWS] = children
        gap_roots = roots - x_start[:ROOTS]
        gap_children = children - x_start[ROWS]
        total = jnp.sum(gap_roots * gap_roots) + jnp.sum(gap_children * gap_children)
        move[...] = jnp.full((8, 128), total, F32)


def own_image(extra_child, scol, coupling, y, right, rates, base):
    sigma = rates[1:2, :1]
    upper = jnp.concatenate([scol[...]] * (TILE // 128), axis=1) == 1.0
    child = extra_child[...]
    for cols in parts():
        image = jnp.where(
            upper, times_t(child, coupling[1, cols]), times_t(child, coupling[2, cols])
        )
        base[:, cols] = y[ROWS, cols] + sigma * (right[ROWS, cols] - image)


def dual_node(last, g0, g1, g2, g3, swapped, nback, linking, base, rates, *refs):
    if last:
        later, held = refs
    else:
        nsend, later, *outs, held = refs
    join((g0, g1, g2, g3), swapped, held)
    rows = times(hot_lanes(nback[...], SLOTS), held[...]).astype(BF16)
    sigma = rates[1:2, :1]
    total = None
    for cols in parts():
        weights = linking[1, cols]
        new = base[:, cols] - sigma * times_t(rows, weights)
        later[:, cols] = new
        if not last:
            product = times(jnp.maximum(new, 0.0).astype(BF16), weights)
            total = product if total is None else total + product
    if not last:
        spread(nsend[...], total.astype(BF16), outs)


def from_leaf(blocks, lback):
    hot = hot_lanes(lback[...], SLOTS)
    rows = None
    for k, block in enumerate(blocks):
        term = times(hot[:, k * 128 : (k + 1) * 128], block[...])
        rows = term if rows is None else rows + term
    return rows.astype(BF16)


def dual_leaf(b0, b1, b2, b3, lback, linking, base, rates, lsend, extra_root, coupling, y, right, *refs):
    y_next, ylow, *outs = refs
    rows = from_leaf((b0, b1, b2, b3), lback)
    sigma = rates[1:2, :1]
    root = extra_root[...]
    total = None
    for cols in parts():
        weights = linking[0, cols]
        image_root = times_t(root, coupling[0, cols])
        new_root = jnp.maximum(y[:ROOTS, cols] + sigma * (right[:ROOTS, cols] - image_root), 0.0)
        new = jnp.maximum(base[:, cols] - sigma * times_t(rows, weights), 0.0)
        low = new.astype(BF16)
        y_next[:ROOTS, cols] = new_root
        y_next[ROWS, cols] = new
        ylow[:ROOTS, cols] = new_root.astype(BF16)
        ylow[ROWS, cols] = low
        product = times(low, weights)
        total = product if total is None else total + product
    spread(lsend[...], total.astype(BF16), outs)


def dual_last(
    b0, b1, b2, b3, lback, linking, base, rates, extra_root, coupling, y, right, y_start, primal_move,
    average, load
):
    rows = from_leaf((b0, b1, b2, b3), lback)
    sigma = rates[1:2, :1]
    root = extra_root[...]
    move = jnp.zeros((1, TILE), F32)
    for cols in parts():
        image_root = times_t(root, coupling[0, cols])
        new_root = jnp.maximum(y[:ROOTS, cols] + sigma * (right[:ROOTS, cols] - image_root), 0.0)
        new = jnp.maximum(base[:, cols] - sigma * times_t(rows, linking[0, cols]), 0.0)
        mean_root = (y[:ROOTS, cols] + new_root) * 0.5
        mean = (y[ROWS, cols] + new) * 0.5
        average[:ROOTS, cols] = mean_root
        average[ROWS, cols] = mean
        gap_root = mean_root - y_start[:ROOTS, cols]
        gap = mean - y_start[ROWS, cols]
        move = move + jnp.sum(gap_root * gap_root, axis=0, keepdims=True)
        move = move + jnp.sum(gap * gap, axis=0, keepdims=True)
    lane = lax.broadcasted_iota(jnp.int32, load.shape, 2)
    load[...] = jnp.where(lane == 0, primal_move[:1], jnp.sum(move))


def pairs_of(place):
    pairs = []
    for i in range(N_LEAF * N_NODE):
        y, z, x, core = place(i >> 5, (i >> 3) & 3, (i >> 1) & 3, i & 1)
        pairs.append((i, ((y & 3) * 4 + (z & 3)) * N_NODE + (x & 3) * 2 + core))
    return ("leaf", "node"), pairs


def outer_ring(k):
    return pairs_of(lambda y, z, x, c: (y, z + k, x, c) if c else (y + k, z, x, c))


def inner_ring(k):
    return pairs_of(lambda y, z, x, c: (y + k, z, x, c) if c else (y, z + k, x, c))


def ring_x(k):
    return pairs_of(lambda y, z, x, c: (y, z, x + k, c))


def sibling(array):
    return lax.ppermute(array, *pairs_of(lambda y, z, x, c: (y, z, x, 1 - c)))


def shifted(blocks, ring, sign=1):
    got = {0: blocks[0]}
    for k in (2, 1, 3):
        got[k] = lax.ppermute(blocks[k], *ring((sign * k) % 4))
    return [got[k] for k in range(4)]


def swap_node(blocks, sign, before):
    got = shifted(blocks, ring_x, sign)
    halves = jnp.concatenate([block[CAP_NODE:] for block in got], axis=0)
    halves, before = lax.optimization_barrier((halves, before))
    return got + [sibling(halves)], before


def sum_leaf(blocks, beside):
    got = [block.astype(F32) for block in shifted(blocks, outer_ring)]
    total = (((got[0] + got[1]) + got[2]) + got[3]).astype(BF16)
    total, beside = lax.optimization_barrier((total, beside))
    return shifted([total[k * ROOTS : (k + 1) * ROOTS] for k in range(4)], inner_ring), beside


def gather_leaf(rows):
    plane = jnp.concatenate(shifted([rows] * 4, inner_ring), axis=0)
    return shifted([plane] * 4, outer_ring)


def part_of(kernel, flag):
    def run(*refs):
        kernel(flag, *refs)

    return run


def shards(x_start, y_start, cost_vec, right_side, omega, coupling, linking, parent, section):
    unit = 2 * CHILD * NS * NC
    here = lax.axis_index("leaf") * N_NODE + lax.axis_index("node")
    code = ((here * 4 + section) * 65536 + parent)[ROOTS:].reshape(1, CHILD)
    rates = jnp.broadcast_to(jnp.stack([STEP / omega[0], STEP * omega[0]])[:, None], (2, 128))
    field = ((NODES, NC), F32)
    field_low = ((NODES, NC), BF16)
    states = ((NODES, NS), F32)
    block = ((128, NS), BF16)
    block_mark = ((128, NS + 128), BF16)
    kids = ((CHILD, NS), F32)
    kids_low = ((CHILD, NS), BF16)
    kids_field = ((CHILD, NC), F32)
    tops = ((ROOTS, NS), F32)
    tops_low = ((ROOTS, NS), BF16)
    row = ((1, CHILD), F32)
    col = ((CHILD, 128), F32)
    held = [pltpu.VMEM((SLOTS, NS), BF16)]

    *sent, y_start, linking, ylow, nsend, nback, lsend, lback, scol = call(
        first,
        [block_mark] * 4 + [block] * 4
        + [field, ((2, NC, NS), BF16), field_low, row, col, row, col, col],
        [code, y_start, linking],
        2 * unit,
        [pltpu.SemaphoreType.DMA((3 * NC // TILE,))],
        (1, 2),
    )
    coupling, sent = lax.optimization_barrier((coupling, sent))
    (own,) = call(own_adjoint, [states], [ylow, scol, coupling], 2 * unit)
    got_leaf, own = sum_leaf(sent[4:], own)
    got_node, got_leaf[1] = swap_node(sent[:4], 1, got_leaf[1])

    wrow, wcol, x_child, extra_child, *out_node = call(
        primal_first,
        [((8, SLOTS), F32), ((SLOTS, 128), F32), kids, kids_low] + [block] * 4,
        got_node + [own, x_start, cost_vec, rates],
        unit // 4,
        [pltpu.VMEM((SLOTS, NS + 128), BF16)],
    )
    (base,) = call(
        own_image, [kids_field], [extra_child, scol, coupling, y_start, right_side, rates], 2 * unit
    )
    x_root, extra_root = call(
        part_of(primal_root, True), [tops, tops_low], got_leaf + [own, x_start, cost_vec, rates], 0
    )
    back_leaf = gather_leaf(extra_root)
    back_node, (back_leaf, base) = swap_node(out_node, -1, (back_leaf, base))
    base, *out_node = call(
        part_of(dual_node, False),
        [kids_field] + [block] * 4,
        back_node + [nback, linking, base, rates, nsend],
        2 * unit,
        held,
    )
    y_next, ylow, *out_leaf = call(
        dual_leaf,
        [field, field_low] + [block] * 4,
        back_leaf + [lback, linking, base, rates, lsend, extra_root, coupling, y_start, right_side],
        2 * unit,
    )
    (own,) = call(own_adjoint, [states], [ylow, scol, coupling], 2 * unit)
    got_leaf, own = sum_leaf(out_leaf, own)
    got_node, got_leaf[1] = swap_node(out_node, 1, got_leaf[1])

    x_child_next, extra_child, *out_node = call(
        primal_second,
        [kids, kids_low] + [block] * 4,
        got_node + [own, x_child, cost_vec, rates, wrow, wcol],
        unit // 4,
        held,
    )
    (base,) = call(
        own_image, [kids_field], [extra_child, scol, coupling, y_next, right_side, rates], 2 * unit
    )
    extra_root, x_average, primal_move = call(
        part_of(primal_root, False),
        [tops_low, states, ((8, 128), F32)],
        got_leaf + [own, x_root, cost_vec, rates, x_start, x_child, x_child_next],
        0,
    )
    back_leaf = gather_leaf(extra_root)
    back_node, (back_leaf, base) = swap_node(out_node, -1, (back_leaf, base))
    (base,) = call(
        part_of(dual_node, True), [kids_field], back_node + [nback, linking, base, rates], unit, held
    )
    y_average, load = call(
        dual_last,
        [field, ((N_LEAF * N_NODE, 1, 128), F32)],
        back_leaf
        + [lback, linking, base, rates, extra_root, coupling, y_next, right_side, y_start, primal_move],
        unit,
    )
    moves = lax.all_to_all(load, ("leaf", "node"), split_axis=0, concat_axis=0, tiled=True)
    moves = jnp.sum(moves[:, 0, :2], axis=0)
    omega_new = jnp.sqrt((moves[1:] + 1e-06) / (moves[:1] + 1e-06))
    return (x_average, y_average, omega_new)


def solution(mesh):
    both = P(("leaf", "node"), None)
    flat = P(("leaf", "node"))
    return jax.shard_map(
        shards,
        mesh=mesh,
        in_specs=(both, both, both, both, P(), P(), P(), flat, flat),
        out_specs=(both, both, P()),
        check_vma=False,
    )
```

```python
import jax
import jax.numpy as jnp
from jax import lax
from jax.experimental import pallas as pl
from jax.experimental.pallas import tpu as pltpu
from jax.sharding import PartitionSpec as P

NS = 512
NC = 2048
ROOTS = 32
CHILD = 256
NODES = 288
N_LEAF = 16
N_NODE = 8
CAP_NODE = 64
SLOTS = 512
TILE = 512
VMEM_LIMIT = 24 * 2**20
STEP = 0.3
F32 = jnp.float32
BF16 = jnp.bfloat16
ROWS = slice(ROOTS, NODES)


def times(a, b):
    return lax.dot_general(a, b, (((1,), (0,)), ((), ())), preferred_element_type=F32)


def times_t(a, b):
    return lax.dot_general(a, b, (((1,), (1,)), ((), ())), preferred_element_type=F32)


def hot_rows(code, count):
    places = lax.broadcasted_iota(jnp.int32, (count, code.shape[1]), 0).astype(F32)
    return jnp.where(places == code, 1.0, 0.0).astype(BF16)


def hot_lanes(code, count):
    wide = jnp.concatenate([code] * (count // 128), axis=1)
    places = lax.broadcasted_iota(jnp.int32, wide.shape, 1).astype(F32)
    return jnp.where(places == wide, 1.0, 0.0).astype(BF16)


def to_lanes(row):
    return jnp.broadcast_to(row, (128, row.shape[1])).T


def call(kernel, outs, arrays, flops, scratch=(), far=()):
    out_shapes = [jax.ShapeDtypeStruct(shape, dtype) for shape, dtype in outs]
    moved = sum(a.size * a.dtype.itemsize for a in list(arrays) + out_shapes)
    out_shapes = [pltpu.VMEM(shape, dtype) for shape, dtype in outs]
    arrays = [
        pltpu.with_memory_space_constraint(a, pltpu.HBM) if i in far else a for i, a in enumerate(arrays)
    ]
    return pl.pallas_call(
        kernel,
        out_shape=out_shapes,
        in_specs=[pl.BlockSpec(memory_space=pl.ANY if i in far else pltpu.VMEM) for i in range(len(arrays))],
        out_specs=[pl.BlockSpec(memory_space=pltpu.VMEM)] * len(outs),
        scratch_shapes=list(scratch),
        compiler_params=pltpu.CompilerParams(vmem_limit_bytes=VMEM_LIMIT),
        cost_estimate=pl.CostEstimate(flops=flops, bytes_accessed=moved // 8, transcendentals=0),
    )(*arrays)


def parts():
    return [slice(i * TILE, (i + 1) * TILE) for i in range(NC // TILE)]


def first(code, y_far, linking_far, *refs):
    *outs, y, linking, ylow, nsend, nback, lsend, lback, scol, sem = refs
    chunks = parts()
    copies = []
    for cols in chunks:
        copies.append((y_far.at[:, cols], y.at[:, cols]))
        copies.append((linking_far.at[1, cols], linking.at[1, cols]))
    for cols in chunks:
        copies.append((linking_far.at[0, cols], linking.at[0, cols]))
    copies = [pltpu.make_async_copy(a, b, sem.at[i]) for i, (a, b) in enumerate(copies)]
    for copy in copies:
        copy.start()
    packed = code[...]
    upper = ((packed >> 16) & 3) == 1
    parent = packed & 0xFFFF
    here = packed >> 18
    owner = ((parent.astype(F32) + 0.5) * (1.0 / NODES)).astype(jnp.int32)
    local = parent - owner * NODES
    ry = ((owner >> 5) - (here >> 5)) & 3
    rz = ((owner >> 3) - (here >> 3)) & 3
    rx = ((owner >> 1) - (here >> 1)) & 3
    rc = (owner ^ here) & 1
    odd = (here & 1) == 1
    outer = jnp.where(odd, rz, ry)
    inner = jnp.where(odd, ry, rz)
    lrow = jnp.where(upper, outer * 128 + inner * ROOTS + local, -1).astype(F32)
    lend = jnp.where(upper, ((-outer) & 3) * 128 + ((-inner) & 3) * ROOTS + local, -1).astype(F32)
    peer = rx * 2 + rc
    peers = lax.broadcasted_iota(jnp.int32, (N_NODE, CHILD), 0)
    member = jnp.where((peers == peer) & jnp.logical_not(upper), 1.0, 0.0)
    before = lax.broadcasted_iota(jnp.int32, (CHILD, CHILD), 0) <= lax.broadcasted_iota(
        jnp.int32, (CHILD, CHILD), 1
    )
    counts = times(member.astype(BF16), jnp.where(before, 1.0, 0.0).astype(BF16))
    rank = jnp.sum(member * counts, axis=0, keepdims=True) - 1.0
    nrow = jnp.where(upper, -1.0, (peer * CAP_NODE).astype(F32) + rank)
    nend = jnp.where(upper, -1.0, (rc * 256 + rx * CAP_NODE).astype(F32) + rank)
    mark = jnp.where(upper, 0, local - (ROOTS - 1)).astype(F32)
    nsend[...] = nrow
    lsend[...] = lrow
    nback[...] = to_lanes(nend)
    lback[...] = to_lanes(lend)
    scol[...] = to_lanes(jnp.where(upper, 1.0, 2.0))
    total = None
    for i, cols in enumerate(chunks):
        copies[2 * i].wait()
        copies[2 * i + 1].wait()
        low = y[:, cols].astype(BF16)
        ylow[:, cols] = low
        term = times(low[ROWS], linking[1, cols])
        total = term if total is None else total + term
    load = jnp.concatenate([total.astype(BF16), to_lanes(mark).astype(BF16)], axis=1)
    spread(nrow, load, outs[:4])
    total = None
    for i, cols in enumerate(chunks):
        copies[2 * len(chunks) + i].wait()
        term = times(ylow[ROWS, cols], linking[0, cols])
        total = term if total is None else total + term
    spread(lrow, total.astype(BF16), outs[4:])


def spread(row, load, outs):
    hot = hot_rows(row, SLOTS)
    for k, out in enumerate(outs):
        out[...] = times(hot[k * 128 : (k + 1) * 128], load).astype(BF16)


def own_adjoint(ylow, scol, coupling, own):
    own[:ROOTS] = times(ylow[:ROOTS], coupling[0])
    upper = jnp.concatenate([scol[...]] * (NS // 128), axis=1) == 1.0
    low = ylow[ROWS]
    own[ROWS] = jnp.where(upper, times(low, coupling[1]), times(low, coupling[2]))


def join(blocks, swapped, held):
    for k, block in enumerate(blocks):
        held[k * CAP_NODE : (k + 1) * CAP_NODE] = block[:CAP_NODE]
    held[256:] = swapped[...]


def primal_first(g0, g1, g2, g3, swapped, own, x, cost, rates, wrow, wcol, x_next, extra, *refs):
    *sends, held = refs
    join((g0, g1, g2, g3), swapped, held)
    mark = held[:, NS:].astype(F32)
    row = mark.T[:8]
    wcol[...] = mark
    wrow[...] = row
    primal_child(held[:, :NS], own, x[ROWS], cost, rates, mark, row, x_next, extra, sends)


def primal_second(g0, g1, g2, g3, swapped, own, x, cost, rates, wrow, wcol, x_next, extra, *refs):
    *sends, held = refs
    join((g0, g1, g2, g3), swapped, held)
    primal_child(held[...], own, x[...], cost, rates, wcol[...], wrow[...], x_next, extra, sends)


def primal_child(got, own, x_old, cost, rates, mark, row, x_next, extra, sends):
    tau = rates[:1, :1]
    adjoint = own[ROWS] + times(hot_rows(row[:1] - 1.0, CHILD), got)
    new = jnp.maximum(x_old - tau * (cost[ROWS] - adjoint), 0.0)
    low = (2.0 * new - x_old).astype(BF16)
    x_next[...] = new
    extra[...] = low
    reply = times(hot_lanes(mark - 1.0, CHILD), low).astype(BF16)
    for k, send in enumerate(sends):
        send[:CAP_NODE] = reply[k * CAP_NODE : (k + 1) * CAP_NODE]
        send[CAP_NODE:] = reply[256 + k * CAP_NODE : 256 + (k + 1) * CAP_NODE]


def primal_root(first, g0, g1, g2, g3, own, x, cost, rates, *refs):
    if first:
        x_next, extra = refs
        x_old = x[:ROOTS]
    else:
        x_start, x_child, x_child_next, extra, average, move = refs
        x_old = x[...]
    tau = rates[:1, :1]
    adjoint = own[:ROOTS]
    for got in (g0, g1, g2, g3):
        adjoint = adjoint + got[...].astype(F32)
    new = jnp.maximum(x_old - tau * (cost[:ROOTS] - adjoint), 0.0)
    extra[...] = (2.0 * new - x_old).astype(BF16)
    if first:
        x_next[...] = new
    else:
        roots = (x_old + new) * 0.5
        children = (x_child[...] + x_child_next[...]) * 0.5
        average[:ROOTS] = roots
        average[ROWS] = children
        gap_roots = roots - x_start[:ROOTS]
        gap_children = children - x_start[ROWS]
        total = jnp.sum(gap_roots * gap_roots) + jnp.sum(gap_children * gap_children)
        move[...] = jnp.full((8, 128), total, F32)


def own_image(extra_child, extra_root, scol, coupling, y, right, rates, base):
    sigma = rates[1:2, :1]
    upper = jnp.concatenate([scol[...]] * (TILE // 128), axis=1) == 1.0
    child = extra_child[...]
    for cols in parts():
        image = jnp.where(
            upper, times_t(child, coupling[1, cols]), times_t(child, coupling[2, cols])
        )
        image_root = times_t(extra_root[...], coupling[0, cols])
        base[:ROOTS, cols] = y[:ROOTS, cols] + sigma * (right[:ROOTS, cols] - image_root)
        base[ROWS, cols] = y[ROWS, cols] + sigma * (right[ROWS, cols] - image)


def from_leaf(blocks, lback):
    hot = hot_lanes(lback[...], SLOTS)
    rows = None
    for k, block in enumerate(blocks):
        term = times(hot[:, k * 128 : (k + 1) * 128], block[...])
        rows = term if rows is None else rows + term
    return rows.astype(BF16)


def dual_leaf(last, b0, b1, b2, b3, lback, linking, base, rates, *refs):
    if last:
        (later,) = refs
    else:
        lsend, later, *outs = refs
    rows = from_leaf((b0, b1, b2, b3), lback)
    sigma = rates[1:2, :1]
    total = None
    for cols in parts():
        weights = linking[0, cols]
        new = base[ROWS, cols] - sigma * times_t(rows, weights)
        later[:, cols] = new
        if not last:
            product = times(jnp.maximum(new, 0.0).astype(BF16), weights)
            total = product if total is None else total + product
    if not last:
        spread(lsend[...], total.astype(BF16), outs)


def from_node(blocks, swapped, nback, held):
    join(blocks, swapped, held)
    return times(hot_lanes(nback[...], SLOTS), held[...]).astype(BF16)


def dual_node(g0, g1, g2, g3, swapped, nback, linking, base, later, rates, nsend, *refs):
    y_next, ylow, *outs, held = refs
    rows = from_node((g0, g1, g2, g3), swapped, nback, held)
    sigma = rates[1:2, :1]
    total = None
    for cols in parts():
        weights = linking[1, cols]
        new_root = jnp.maximum(base[:ROOTS, cols], 0.0)
        new = jnp.maximum(later[:, cols] - sigma * times_t(rows, weights), 0.0)
        low = new.astype(BF16)
        y_next[:ROOTS, cols] = new_root
        y_next[ROWS, cols] = new
        ylow[:ROOTS, cols] = new_root.astype(BF16)
        ylow[ROWS, cols] = low
        product = times(low, weights)
        total = product if total is None else total + product
    spread(nsend[...], total.astype(BF16), outs)


def dual_last(
    g0, g1, g2, g3, swapped, nback, linking, base, later, rates, y, y_start, primal_move, average, load, held
):
    rows = from_node((g0, g1, g2, g3), swapped, nback, held)
    sigma = rates[1:2, :1]
    move = jnp.zeros((1, TILE), F32)
    for cols in parts():
        new_root = jnp.maximum(base[:ROOTS, cols], 0.0)
        new = jnp.maximum(later[:, cols] - sigma * times_t(rows, linking[1, cols]), 0.0)
        mean_root = (y[:ROOTS, cols] + new_root) * 0.5
        mean = (y[ROWS, cols] + new) * 0.5
        average[:ROOTS, cols] = mean_root
        average[ROWS, cols] = mean
        gap_root = mean_root - y_start[:ROOTS, cols]
        gap = mean - y_start[ROWS, cols]
        move = move + jnp.sum(gap_root * gap_root, axis=0, keepdims=True)
        move = move + jnp.sum(gap * gap, axis=0, keepdims=True)
    lane = lax.broadcasted_iota(jnp.int32, load.shape, 2)
    load[...] = jnp.where(lane == 0, primal_move[:1], jnp.sum(move))


def pairs_of(place):
    pairs = []
    for i in range(N_LEAF * N_NODE):
        y, z, x, core = place(i >> 5, (i >> 3) & 3, (i >> 1) & 3, i & 1)
        pairs.append((i, ((y & 3) * 4 + (z & 3)) * N_NODE + (x & 3) * 2 + core))
    return ("leaf", "node"), pairs


def outer_ring(k):
    return pairs_of(lambda y, z, x, c: (y, z + k, x, c) if c else (y + k, z, x, c))


def inner_ring(k):
    return pairs_of(lambda y, z, x, c: (y + k, z, x, c) if c else (y, z + k, x, c))


def ring_x(k):
    return pairs_of(lambda y, z, x, c: (y, z, x + k, c))


def sibling(array):
    return lax.ppermute(array, *pairs_of(lambda y, z, x, c: (y, z, x, 1 - c)))


def shifted(blocks, ring, sign=1):
    got = {0: blocks[0]}
    for k in (2, 1, 3):
        got[k] = lax.ppermute(blocks[k], *ring((sign * k) % 4))
    return [got[k] for k in range(4)]


def swap_node(blocks, sign, before):
    got = shifted(blocks, ring_x, sign)
    halves = jnp.concatenate([block[CAP_NODE:] for block in got], axis=0)
    halves, before = lax.optimization_barrier((halves, before))
    return got + [sibling(halves)], before


def sum_leaf(blocks, before):
    got, before = lax.optimization_barrier((shifted(blocks, outer_ring), before))
    got = [block.astype(F32) for block in got]
    total = (((got[0] + got[1]) + got[2]) + got[3]).astype(BF16)
    return shifted([total[k * ROOTS : (k + 1) * ROOTS] for k in range(4)], inner_ring), before


def gather_leaf(rows):
    plane = jnp.concatenate(shifted([rows] * 4, inner_ring), axis=0)
    return shifted([plane] * 4, outer_ring)


def part_of(kernel, flag):
    def run(*refs):
        kernel(flag, *refs)

    return run


def shards(x_start, y_start, cost_vec, right_side, omega, coupling, linking, parent, section):
    unit = 2 * CHILD * NS * NC
    here = lax.axis_index("leaf") * N_NODE + lax.axis_index("node")
    code = ((here * 4 + section) * 65536 + parent)[ROOTS:].reshape(1, CHILD)
    rates = jnp.broadcast_to(jnp.stack([STEP / omega[0], STEP * omega[0]])[:, None], (2, 128))
    field = ((NODES, NC), F32)
    field_low = ((NODES, NC), BF16)
    states = ((NODES, NS), F32)
    block = ((128, NS), BF16)
    block_mark = ((128, NS + 128), BF16)
    kids = ((CHILD, NS), F32)
    kids_low = ((CHILD, NS), BF16)
    kids_field = ((CHILD, NC), F32)
    tops = ((ROOTS, NS), F32)
    tops_low = ((ROOTS, NS), BF16)
    row = ((1, CHILD), F32)
    col = ((CHILD, 128), F32)
    held = [pltpu.VMEM((SLOTS, NS), BF16)]

    *sent, y_start, linking, ylow, nsend, nback, lsend, lback, scol = call(
        first,
        [block_mark] * 4 + [block] * 4
        + [field, ((2, NC, NS), BF16), field_low, row, col, row, col, col],
        [code, y_start, linking],
        2 * unit,
        [pltpu.SemaphoreType.DMA((3 * NC // TILE,))],
        (1, 2),
    )
    coupling, sent = lax.optimization_barrier((coupling, sent))
    (own,) = call(own_adjoint, [states], [ylow, scol, coupling], 2 * unit)
    got_leaf, own = sum_leaf(sent[4:], own)
    got_node, got_leaf = swap_node(sent[:4], 1, got_leaf)

    wrow, wcol, x_child, extra_child, *out_node = call(
        primal_first,
        [((8, SLOTS), F32), ((SLOTS, 128), F32), kids, kids_low] + [block] * 4,
        got_node + [own, x_start, cost_vec, rates],
        unit // 4,
        [pltpu.VMEM((SLOTS, NS + 128), BF16)],
    )
    x_root, extra_root = call(
        part_of(primal_root, True), [tops, tops_low], got_leaf + [own, x_start, cost_vec, rates], 0
    )
    (base,) = call(
        own_image,
        [field],
        [extra_child, extra_root, scol, coupling, y_start, right_side, rates],
        2 * unit,
    )
    back_leaf = gather_leaf(extra_root)
    back_node, (back_leaf, base) = swap_node(out_node, -1, (back_leaf, base))
    later, *out_leaf = call(
        part_of(dual_leaf, False),
        [kids_field] + [block] * 4,
        back_leaf + [lback, linking, base, rates, lsend],
        2 * unit,
    )
    y_next, ylow, *out_node = call(
        dual_node,
        [field, field_low] + [block] * 4,
        back_node + [nback, linking, base, later, rates, nsend],
        2 * unit,
        held,
    )
    got_leaf, ylow = sum_leaf(out_leaf, ylow)
    (own,) = call(own_adjoint, [states], [ylow, scol, coupling], 2 * unit)
    got_node, got_leaf = swap_node(out_node, 1, got_leaf)

    x_child_next, extra_child, *out_node = call(
        primal_second,
        [kids, kids_low] + [block] * 4,
        got_node + [own, x_child, cost_vec, rates, wrow, wcol],
        unit // 4,
        held,
    )
    extra_root, x_average, primal_move = call(
        part_of(primal_root, False),
        [tops_low, states, ((8, 128), F32)],
        got_leaf + [own, x_root, cost_vec, rates, x_start, x_child, x_child_next],
        0,
    )
    (base,) = call(
        own_image,
        [field],
        [extra_child, extra_root, scol, coupling, y_next, right_side, rates],
        2 * unit,
    )
    back_leaf = gather_leaf(extra_root)
    back_node, (back_leaf, base) = swap_node(out_node, -1, (back_leaf, base))
    (later,) = call(
        part_of(dual_leaf, True), [kids_field], back_leaf + [lback, linking, base, rates], unit
    )
    y_average, load = call(
        dual_last,
        [field, ((N_LEAF * N_NODE, 1, 128), F32)],
        back_node + [nback, linking, base, later, rates, y_next, y_start, primal_move],
        unit,
        held,
    )
    moves = lax.all_to_all(load, ("leaf", "node"), split_axis=0, concat_axis=0, tiled=True)
    moves = jnp.sum(moves[:, 0, :2], axis=0)
    omega_new = jnp.sqrt((moves[1:] + 1e-06) / (moves[:1] + 1e-06))
    return (x_average, y_average, omega_new)


def solution(mesh):
    both = P(("leaf", "node"), None)
    flat = P(("leaf", "node"))
    return jax.shard_map(
        shards,
        mesh=mesh,
        in_specs=(both, both, both, both, P(), P(), P(), flat, flat),
        out_specs=(both, both, P()),
        check_vma=False,
    )
```

```python
import jax
import jax.numpy as jnp
from jax import lax
from jax.experimental import pallas as pl
from jax.experimental.pallas import tpu as pltpu
from jax.sharding import PartitionSpec as P

NS = 512
NC = 2048
ROOTS = 32
CHILD = 256
NODES = 288
N_LEAF = 16
N_NODE = 8
CAP_NODE = 64
SLOTS = 512
TILE = 512
VMEM_LIMIT = 24 * 2**20
STEP = 0.3
F32 = jnp.float32
BF16 = jnp.bfloat16
ROWS = slice(ROOTS, NODES)


def times(a, b):
    return lax.dot_general(a, b, (((1,), (0,)), ((), ())), preferred_element_type=F32)


def times_t(a, b):
    return lax.dot_general(a, b, (((1,), (1,)), ((), ())), preferred_element_type=F32)


def hot_rows(code, count):
    places = lax.broadcasted_iota(jnp.int32, (count, code.shape[1]), 0).astype(F32)
    return jnp.where(places == code, 1.0, 0.0).astype(BF16)


def hot_lanes(code, count):
    wide = jnp.concatenate([code] * (count // 128), axis=1)
    places = lax.broadcasted_iota(jnp.int32, wide.shape, 1).astype(F32)
    return jnp.where(places == wide, 1.0, 0.0).astype(BF16)


def to_lanes(row):
    return jnp.broadcast_to(row, (128, row.shape[1])).T


def call(kernel, outs, arrays, flops, scratch=(), far=()):
    out_shapes = [jax.ShapeDtypeStruct(shape, dtype) for shape, dtype in outs]
    moved = sum(a.size * a.dtype.itemsize for a in list(arrays) + out_shapes)
    out_shapes = [pltpu.VMEM(shape, dtype) for shape, dtype in outs]
    arrays = [
        pltpu.with_memory_space_constraint(a, pltpu.HBM) if i in far else a for i, a in enumerate(arrays)
    ]
    return pl.pallas_call(
        kernel,
        out_shape=out_shapes,
        in_specs=[pl.BlockSpec(memory_space=pl.ANY if i in far else pltpu.VMEM) for i in range(len(arrays))],
        out_specs=[pl.BlockSpec(memory_space=pltpu.VMEM)] * len(outs),
        scratch_shapes=list(scratch),
        compiler_params=pltpu.CompilerParams(vmem_limit_bytes=VMEM_LIMIT),
        cost_estimate=pl.CostEstimate(flops=flops, bytes_accessed=moved // 8, transcendentals=0),
    )(*arrays)


def parts():
    return [slice(i * TILE, (i + 1) * TILE) for i in range(NC // TILE)]


def first(code, y_far, linking_far, x_far, cost_far, *refs):
    *outs, y, linking, ylow, nsend, nback, lsend, lback, scol, state, near, sem = refs
    chunks = parts()
    copies = []
    for cols in chunks:
        copies.append((y_far.at[:, cols], y.at[:, cols]))
        copies.append((linking_far.at[1, cols], linking.at[1, cols]))
    for cols in chunks:
        copies.append((linking_far.at[0, cols], linking.at[0, cols]))
    for i, array in enumerate((x_far, cost_far)):
        copies.append((array.at[:ROOTS], near.at[i]))
    copies = [pltpu.make_async_copy(a, b, sem.at[i]) for i, (a, b) in enumerate(copies)]
    for copy in copies:
        copy.start()
    packed = code[...]
    upper = ((packed >> 16) & 3) == 1
    parent = packed & 0xFFFF
    here = packed >> 18
    owner = ((parent.astype(F32) + 0.5) * (1.0 / NODES)).astype(jnp.int32)
    local = parent - owner * NODES
    ry = ((owner >> 5) - (here >> 5)) & 3
    rz = ((owner >> 3) - (here >> 3)) & 3
    rx = ((owner >> 1) - (here >> 1)) & 3
    rc = (owner ^ here) & 1
    odd = (here & 1) == 1
    outer = jnp.where(odd, rz, ry)
    inner = jnp.where(odd, ry, rz)
    lrow = jnp.where(upper, outer * 128 + inner * ROOTS + local, -1).astype(F32)
    lend = jnp.where(upper, ((-outer) & 3) * 128 + inner * ROOTS + local, -1).astype(F32)
    peer = rx * 2 + rc
    peers = lax.broadcasted_iota(jnp.int32, (N_NODE, CHILD), 0)
    member = jnp.where((peers == peer) & jnp.logical_not(upper), 1.0, 0.0)
    before = lax.broadcasted_iota(jnp.int32, (CHILD, CHILD), 0) <= lax.broadcasted_iota(
        jnp.int32, (CHILD, CHILD), 1
    )
    counts = times(member.astype(BF16), jnp.where(before, 1.0, 0.0).astype(BF16))
    rank = jnp.sum(member * counts, axis=0, keepdims=True) - 1.0
    nrow = jnp.where(upper, -1.0, (peer * CAP_NODE).astype(F32) + rank)
    nend = jnp.where(upper, -1.0, (rc * 256 + rx * CAP_NODE).astype(F32) + rank)
    mark = jnp.where(upper, 0, local - (ROOTS - 1)).astype(F32)
    nsend[...] = nrow
    lsend[...] = lrow
    nback[...] = to_lanes(nend)
    lback[...] = to_lanes(lend)
    scol[...] = to_lanes(jnp.where(upper, 1.0, 2.0))
    total = None
    for i, cols in enumerate(chunks):
        copies[2 * i].wait()
        copies[2 * i + 1].wait()
        low = y[:, cols].astype(BF16)
        ylow[:, cols] = low
        term = times(low[ROWS], linking[1, cols])
        total = term if total is None else total + term
    load = jnp.concatenate([total.astype(BF16), to_lanes(mark).astype(BF16)], axis=1)
    spread(nrow, load, outs[:4])
    total = None
    for i, cols in enumerate(chunks):
        copies[2 * len(chunks) + i].wait()
        term = times(ylow[ROWS, cols], linking[0, cols])
        total = term if total is None else total + term
    spread(lrow, total.astype(BF16), outs[4:])
    for i in range(2):
        copies[3 * len(chunks) + i].wait()
        value = near[i]
        high = value.astype(BF16)
        state[2 * i * ROOTS : (2 * i + 1) * ROOTS] = high
        state[(2 * i + 1) * ROOTS : (2 * i + 2) * ROOTS] = (value - high.astype(F32)).astype(BF16)


def spread(row, load, outs):
    hot = hot_rows(row, SLOTS)
    for k, out in enumerate(outs):
        out[...] = times(hot[k * 128 : (k + 1) * 128], load).astype(BF16)


def own_adjoint(ylow, scol, coupling, own):
    upper = jnp.concatenate([scol[...]] * (NS // 128), axis=1) == 1.0
    low = ylow[ROWS]
    own[...] = jnp.where(upper, times(low, coupling[1]), times(low, coupling[2]))


def own_first(ylow, scol, coupling, own, own_root):
    own_adjoint(ylow, scol, coupling, own)
    own_root[...] = times(ylow[:ROOTS], coupling[0])


def join(blocks, swapped, held):
    for k, block in enumerate(blocks):
        held[k * CAP_NODE : (k + 1) * CAP_NODE] = block[:CAP_NODE]
    held[256:] = swapped[...]


def primal_first(g0, g1, g2, g3, swapped, own, x, cost, rates, wrow, wcol, x_next, extra, *refs):
    *sends, held = refs
    join((g0, g1, g2, g3), swapped, held)
    mark = held[:, NS:].astype(F32)
    row = mark.T[:8]
    wcol[...] = mark
    wrow[...] = row
    primal_child(held[:, :NS], own, x[ROWS], cost, rates, mark, row, x_next, extra, sends)


def primal_second(g0, g1, g2, g3, swapped, own, x, cost, rates, wrow, wcol, x_next, extra, *refs):
    *sends, held = refs
    join((g0, g1, g2, g3), swapped, held)
    primal_child(held[...], own, x[...], cost, rates, wcol[...], wrow[...], x_next, extra, sends)


def primal_child(got, own, x_old, cost, rates, mark, row, x_next, extra, sends):
    tau = rates[:1, :1]
    adjoint = own[...] + times(hot_rows(row[:1] - 1.0, CHILD), got)
    new = jnp.maximum(x_old - tau * (cost[ROWS] - adjoint), 0.0)
    low = (2.0 * new - x_old).astype(BF16)
    x_next[...] = new
    extra[...] = low
    reply = times(hot_lanes(mark - 1.0, CHILD), low).astype(BF16)
    for k, send in enumerate(sends):
        send[:CAP_NODE] = reply[k * CAP_NODE : (k + 1) * CAP_NODE]
        send[CAP_NODE:] = reply[256 + k * CAP_NODE : 256 + (k + 1) * CAP_NODE]


def rooted(j):
    return slice(j * ROOTS, (j + 1) * ROOTS)


def summed(blocks, j):
    return sum(block[rooted((j + k) & 3)].astype(F32) for k, block in enumerate(blocks))


def root_first(g0, g1, g2, g3, own, x, cost, rates, x_next, cost_next, extra):
    blocks = (g0, g1, g2, g3)
    tau = rates[:1, :1]
    for j in range(4):
        adjoint = summed(blocks, j)
        if j == 0:
            x_old, price = x[:ROOTS], cost[:ROOTS]
            adjoint = adjoint + own[...]
        else:
            home = blocks[(-j) & 3]
            x_old = home[rooted(4)].astype(F32) + home[rooted(5)].astype(F32)
            price = home[rooted(6)].astype(F32) + home[rooted(7)].astype(F32)
        new = jnp.maximum(x_old - tau * (price - adjoint), 0.0)
        x_next[rooted(j)] = new
        cost_next[rooted(j)] = price
        extra[rooted(j)] = (2.0 * new - x_old).astype(BF16)


def root_second(g0, g1, g2, g3, own, x, cost, rates, extra, x_next):
    blocks = (g0, g1, g2, g3)
    tau = rates[:1, :1]
    for j in range(4):
        adjoint = summed(blocks, j)
        if j == 0:
            adjoint = adjoint + own[...]
        x_old = x[rooted(j)]
        new = jnp.maximum(x_old - tau * (cost[rooted(j)] - adjoint), 0.0)
        extra[rooted(j)] = (2.0 * new - x_old).astype(BF16)
        if j == 0:
            x_next[...] = new


def averages(x_start, x_root, x_root_next, x_child, x_child_next, average, move):
    roots = (x_root[:ROOTS] + x_root_next[...]) * 0.5
    children = (x_child[...] + x_child_next[...]) * 0.5
    average[:ROOTS] = roots
    average[ROWS] = children
    gap_roots = roots - x_start[:ROOTS]
    gap_children = children - x_start[ROWS]
    total = jnp.sum(gap_roots * gap_roots) + jnp.sum(gap_children * gap_children)
    move[...] = jnp.full((8, 128), total, F32)


def own_image(extra_child, extra_root, scol, coupling, y, right, rates, base, own_root):
    sigma = rates[1:2, :1]
    upper = jnp.concatenate([scol[...]] * (TILE // 128), axis=1) == 1.0
    child = extra_child[...]
    root = extra_root[:ROOTS]
    total = None
    for cols in parts():
        image = jnp.where(
            upper, times_t(child, coupling[1, cols]), times_t(child, coupling[2, cols])
        )
        weights = coupling[0, cols]
        base_root = y[:ROOTS, cols] + sigma * (right[:ROOTS, cols] - times_t(root, weights))
        base[:ROOTS, cols] = base_root
        term = times(jnp.maximum(base_root, 0.0).astype(BF16), weights)
        total = term if total is None else total + term
        base[ROWS, cols] = y[ROWS, cols] + sigma * (right[ROWS, cols] - image)
    own_root[...] = total


def from_leaf(blocks, lback):
    hot = hot_lanes(lback[...], SLOTS)
    rows = None
    for k, block in enumerate(blocks):
        term = times(hot[:, k * 128 : (k + 1) * 128], block[...])
        rows = term if rows is None else rows + term
    return rows.astype(BF16)


def dual_leaf(last, b0, b1, b2, b3, lback, linking, base, rates, *refs):
    if last:
        (later,) = refs
    else:
        lsend, later, *outs = refs
    rows = from_leaf((b0, b1, b2, b3), lback)
    sigma = rates[1:2, :1]
    total = None
    for cols in parts():
        weights = linking[0, cols]
        new = base[ROWS, cols] - sigma * times_t(rows, weights)
        later[:, cols] = new
        if not last:
            product = times(jnp.maximum(new, 0.0).astype(BF16), weights)
            total = product if total is None else total + product
    if not last:
        spread(lsend[...], total.astype(BF16), outs)


def from_node(blocks, swapped, nback, held):
    join(blocks, swapped, held)
    return times(hot_lanes(nback[...], SLOTS), held[...]).astype(BF16)


def dual_node(g0, g1, g2, g3, swapped, nback, linking, base, later, rates, nsend, *refs):
    y_next, ylow, *outs, held = refs
    rows = from_node((g0, g1, g2, g3), swapped, nback, held)
    sigma = rates[1:2, :1]
    total = None
    for cols in parts():
        weights = linking[1, cols]
        new_root = jnp.maximum(base[:ROOTS, cols], 0.0)
        new = jnp.maximum(later[:, cols] - sigma * times_t(rows, weights), 0.0)
        low = new.astype(BF16)
        y_next[:ROOTS, cols] = new_root
        y_next[ROWS, cols] = new
        ylow[:ROOTS, cols] = new_root.astype(BF16)
        ylow[ROWS, cols] = low
        product = times(low, weights)
        total = product if total is None else total + product
    spread(nsend[...], total.astype(BF16), outs)


def dual_last(
    g0, g1, g2, g3, swapped, nback, linking, base, later, rates, y, y_start, primal_move, average, load, held
):
    rows = from_node((g0, g1, g2, g3), swapped, nback, held)
    sigma = rates[1:2, :1]
    move = jnp.zeros((1, TILE), F32)
    for cols in parts():
        new_root = jnp.maximum(base[:ROOTS, cols], 0.0)
        new = jnp.maximum(later[:, cols] - sigma * times_t(rows, linking[1, cols]), 0.0)
        mean_root = (y[:ROOTS, cols] + new_root) * 0.5
        mean = (y[ROWS, cols] + new) * 0.5
        average[:ROOTS, cols] = mean_root
        average[ROWS, cols] = mean
        gap_root = mean_root - y_start[:ROOTS, cols]
        gap = mean - y_start[ROWS, cols]
        move = move + jnp.sum(gap_root * gap_root, axis=0, keepdims=True)
        move = move + jnp.sum(gap * gap, axis=0, keepdims=True)
    lane = lax.broadcasted_iota(jnp.int32, load.shape, 2)
    load[...] = jnp.where(lane == 0, primal_move[:1], jnp.sum(move))


def pairs_of(place):
    pairs = []
    for i in range(N_LEAF * N_NODE):
        y, z, x, core = place(i >> 5, (i >> 3) & 3, (i >> 1) & 3, i & 1)
        pairs.append((i, ((y & 3) * 4 + (z & 3)) * N_NODE + (x & 3) * 2 + core))
    return ("leaf", "node"), pairs


def outer_ring(k):
    return pairs_of(lambda y, z, x, c: (y, z + k, x, c) if c else (y + k, z, x, c))


def inner_ring(k):
    return pairs_of(lambda y, z, x, c: (y + k, z, x, c) if c else (y, z + k, x, c))


def ring_x(k):
    return pairs_of(lambda y, z, x, c: (y, z, x + k, c))


def sibling(array):
    return lax.ppermute(array, *pairs_of(lambda y, z, x, c: (y, z, x, 1 - c)))


def shifted(blocks, ring, sign=1):
    got = {0: blocks[0]}
    for k in (2, 1, 3):
        got[k] = lax.ppermute(blocks[k], *ring((sign * k) % 4))
    return [got[k] for k in range(4)]


def swap_node(blocks, sign, before):
    got = shifted(blocks, ring_x, sign)
    halves = jnp.concatenate([block[CAP_NODE:] for block in got], axis=0)
    halves, before = lax.optimization_barrier((halves, before))
    return got + [sibling(halves)], before


def sum_leaf(blocks, own, state, before):
    got, before = lax.optimization_barrier((shifted(blocks, outer_ring), before))
    got = [block.astype(F32) for block in got]
    total = ((got[0] + got[1]) + got[2]) + got[3]
    sent = jnp.concatenate([total[:ROOTS] + own, total[ROOTS:]], axis=0).astype(BF16)
    if state is not None:
        sent = jnp.concatenate([sent, state], axis=0)
    return [total.astype(BF16)] + shifted([sent] * 4, inner_ring)[1:], before


def part_of(kernel, flag):
    def run(*refs):
        kernel(flag, *refs)

    return run


def shards(x_start, y_start, cost_vec, right_side, omega, coupling, linking, parent, section):
    unit = 2 * CHILD * NS * NC
    here = lax.axis_index("leaf") * N_NODE + lax.axis_index("node")
    code = ((here * 4 + section) * 65536 + parent)[ROOTS:].reshape(1, CHILD)
    rates = jnp.broadcast_to(jnp.stack([STEP / omega[0], STEP * omega[0]])[:, None], (2, 128))
    field = ((NODES, NC), F32)
    field_low = ((NODES, NC), BF16)
    states = ((NODES, NS), F32)
    block = ((128, NS), BF16)
    block_mark = ((128, NS + 128), BF16)
    kids = ((CHILD, NS), F32)
    kids_low = ((CHILD, NS), BF16)
    kids_field = ((CHILD, NC), F32)
    tops = ((ROOTS, NS), F32)
    plane = ((4 * ROOTS, NS), F32)
    row = ((1, CHILD), F32)
    col = ((CHILD, 128), F32)
    held = [pltpu.VMEM((SLOTS, NS), BF16)]

    *sent, y_start, linking, ylow, nsend, nback, lsend, lback, scol, state = call(
        first,
        [block_mark] * 4 + [block] * 4
        + [field, ((2, NC, NS), BF16), field_low, row, col, row, col, col, block],
        [code, y_start, linking, x_start, cost_vec],
        2 * unit,
        [pltpu.VMEM((2, ROOTS, NS), F32), pltpu.SemaphoreType.DMA((3 * NC // TILE + 2,))],
        (1, 2, 3, 4),
    )
    coupling, sent = lax.optimization_barrier((coupling, sent))
    own, own_root = call(own_first, [kids, tops], [ylow, scol, coupling], 2 * unit)
    got_leaf, own = sum_leaf(sent[4:], own_root, state, own)
    got_node, got_leaf = swap_node(sent[:4], 1, got_leaf)

    x_root, cost_root, extra_root = call(
        root_first,
        [plane, plane, block],
        got_leaf + [own_root, x_start, cost_vec, rates],
        0,
    )
    own, extra_root = lax.optimization_barrier((own, extra_root))
    wrow, wcol, x_child, extra_child, *out_node = call(
        primal_first,
        [((8, SLOTS), F32), ((SLOTS, 128), F32), kids, kids_low] + [block] * 4,
        got_node + [own, x_start, cost_vec, rates],
        unit // 4,
        [pltpu.VMEM((SLOTS, NS + 128), BF16)],
    )
    base, own_root = call(
        own_image,
        [field, tops],
        [extra_child, extra_root, scol, coupling, y_start, right_side, rates],
        2 * unit,
    )
    back_leaf = shifted([extra_root] * 4, outer_ring)
    back_node, (back_leaf, base) = swap_node(out_node, -1, (back_leaf, base))
    later, *out_leaf = call(
        part_of(dual_leaf, False),
        [kids_field] + [block] * 4,
        back_leaf + [lback, linking, base, rates, lsend],
        2 * unit,
    )
    y_next, ylow, *out_node = call(
        dual_node,
        [field, field_low] + [block] * 4,
        back_node + [nback, linking, base, later, rates, nsend],
        2 * unit,
        held,
    )
    got_leaf, ylow = sum_leaf(out_leaf, own_root, None, ylow)
    (own,) = call(own_adjoint, [kids], [ylow, scol, coupling], 2 * unit)
    got_node, (got_leaf, own) = swap_node(out_node, 1, (got_leaf, own))

    extra_root, x_top = call(
        root_second,
        [block, tops],
        got_leaf + [own_root, x_root, cost_root, rates],
        0,
    )
    own, extra_root = lax.optimization_barrier((own, extra_root))
    x_child_next, extra_child, *out_node = call(
        primal_second,
        [kids, kids_low] + [block] * 4,
        got_node + [own, x_child, cost_vec, rates, wrow, wcol],
        unit // 4,
        held,
    )
    x_average, primal_move = call(
        averages,
        [states, ((8, 128), F32)],
        [x_start, x_root, x_top, x_child, x_child_next],
        0,
    )
    base, _ = call(
        own_image,
        [field, tops],
        [extra_child, extra_root, scol, coupling, y_next, right_side, rates],
        2 * unit,
    )
    back_leaf = shifted([extra_root] * 4, outer_ring)
    back_node, (back_leaf, base) = swap_node(out_node, -1, (back_leaf, base))
    (later,) = call(
        part_of(dual_leaf, True), [kids_field], back_leaf + [lback, linking, base, rates], unit
    )
    y_average, load = call(
        dual_last,
        [field, ((N_LEAF * N_NODE, 1, 128), F32)],
        back_node + [nback, linking, base, later, rates, y_next, y_start, primal_move],
        unit,
        held,
    )
    moves = lax.all_to_all(load, ("leaf", "node"), split_axis=0, concat_axis=0, tiled=True)
    moves = jnp.sum(moves[:, 0, :2], axis=0)
    omega_new = jnp.sqrt((moves[1:] + 1e-06) / (moves[:1] + 1e-06))
    return (x_average, y_average, omega_new)


def solution(mesh):
    both = P(("leaf", "node"), None)
    flat = P(("leaf", "node"))
    return jax.shard_map(
        shards,
        mesh=mesh,
        in_specs=(both, both, both, both, P(), P(), P(), flat, flat),
        out_specs=(both, both, P()),
        check_vma=False,
    )
```

```python
import jax
import jax.numpy as jnp
from jax import lax
from jax.experimental import pallas as pl
from jax.experimental.pallas import tpu as pltpu
from jax.sharding import PartitionSpec as P

NS = 512
NC = 2048
ROOTS = 32
CHILD = 256
NODES = 288
N_LEAF = 16
N_NODE = 8
CAP_NODE = 64
SLOTS = 512
TILE = 512
VMEM_LIMIT = 24 * 2**20
STEP = 0.3
F32 = jnp.float32
BF16 = jnp.bfloat16
ROWS = slice(ROOTS, NODES)


def times(a, b):
    return lax.dot_general(a, b, (((1,), (0,)), ((), ())), preferred_element_type=F32)


def times_t(a, b):
    return lax.dot_general(a, b, (((1,), (1,)), ((), ())), preferred_element_type=F32)


def hot_rows(code, count):
    places = lax.broadcasted_iota(jnp.int32, (count, code.shape[1]), 0).astype(F32)
    return jnp.where(places == code, 1.0, 0.0).astype(BF16)


def hot_lanes(code, count):
    wide = jnp.concatenate([code] * (count // 128), axis=1)
    places = lax.broadcasted_iota(jnp.int32, wide.shape, 1).astype(F32)
    return jnp.where(places == wide, 1.0, 0.0).astype(BF16)


def to_lanes(row):
    return jnp.broadcast_to(row, (128, row.shape[1])).T


def call(kernel, outs, arrays, flops, scratch=(), far=()):
    out_shapes = [jax.ShapeDtypeStruct(shape, dtype) for shape, dtype in outs]
    moved = sum(a.size * a.dtype.itemsize for a in list(arrays) + out_shapes)
    out_shapes = [pltpu.VMEM(shape, dtype) for shape, dtype in outs]
    arrays = [
        pltpu.with_memory_space_constraint(a, pltpu.HBM) if i in far else a for i, a in enumerate(arrays)
    ]
    return pl.pallas_call(
        kernel,
        out_shape=out_shapes,
        in_specs=[pl.BlockSpec(memory_space=pl.ANY if i in far else pltpu.VMEM) for i in range(len(arrays))],
        out_specs=[pl.BlockSpec(memory_space=pltpu.VMEM)] * len(outs),
        scratch_shapes=list(scratch),
        compiler_params=pltpu.CompilerParams(vmem_limit_bytes=VMEM_LIMIT),
        cost_estimate=pl.CostEstimate(flops=flops, bytes_accessed=moved // 8, transcendentals=0),
    )(*arrays)


def parts():
    return [slice(i * TILE, (i + 1) * TILE) for i in range(NC // TILE)]


def first(parent_of, section_of, y_far, linking_far, x_far, cost_far, *refs):
    *outs, y, linking, ylow, nsend, nback, lsend, lback, scol, x_top, cost_top, state, sem = refs
    chunks = parts()
    copies = []
    for cols in chunks:
        copies.append((y_far.at[:, cols], y.at[:, cols]))
        copies.append((linking_far.at[1, cols], linking.at[1, cols]))
    for cols in chunks:
        copies.append((linking_far.at[0, cols], linking.at[0, cols]))
    copies += [(x_far.at[:ROOTS], x_top), (cost_far.at[:ROOTS], cost_top)]
    copies = [pltpu.make_async_copy(a, b, sem.at[i]) for i, (a, b) in enumerate(copies)]
    for copy in copies:
        copy.start()
    upper = section_of[...][:, ROWS] == 1
    parent = parent_of[...][:, ROWS]
    here = lax.axis_index("leaf") * N_NODE + lax.axis_index("node")
    owner = ((parent.astype(F32) + 0.5) * (1.0 / NODES)).astype(jnp.int32)
    local = parent - owner * NODES
    ry = ((owner >> 5) - (here >> 5)) & 3
    rz = ((owner >> 3) - (here >> 3)) & 3
    rx = ((owner >> 1) - (here >> 1)) & 3
    rc = (owner ^ here) & 1
    odd = (here & 1) == 1
    outer = jnp.where(odd, rz, ry)
    inner = jnp.where(odd, ry, rz)
    lrow = jnp.where(upper, outer * 128 + inner * ROOTS + local, -1).astype(F32)
    lend = jnp.where(upper, ((-outer) & 3) * 128 + inner * ROOTS + local, -1).astype(F32)
    peer = rx * 2 + rc
    peers = lax.broadcasted_iota(jnp.int32, (N_NODE, CHILD), 0)
    member = jnp.where((peers == peer) & jnp.logical_not(upper), 1.0, 0.0)
    before = lax.broadcasted_iota(jnp.int32, (CHILD, CHILD), 0) <= lax.broadcasted_iota(
        jnp.int32, (CHILD, CHILD), 1
    )
    counts = times(member.astype(BF16), jnp.where(before, 1.0, 0.0).astype(BF16))
    rank = jnp.sum(member * counts, axis=0, keepdims=True) - 1.0
    nrow = jnp.where(upper, -1.0, (peer * CAP_NODE).astype(F32) + rank)
    nend = jnp.where(upper, -1.0, (rc * 256 + rx * CAP_NODE).astype(F32) + rank)
    mark = jnp.where(upper, 0, local - (ROOTS - 1)).astype(F32)
    nsend[...] = nrow
    lsend[...] = lrow
    nback[...] = to_lanes(nend)
    lback[...] = to_lanes(lend)
    scol[...] = to_lanes(jnp.where(upper, 1.0, 2.0))
    total = None
    for i, cols in enumerate(chunks):
        copies[2 * i].wait()
        copies[2 * i + 1].wait()
        low = y[:, cols].astype(BF16)
        ylow[:, cols] = low
        term = times(low[ROWS], linking[1, cols])
        total = term if total is None else total + term
    load = jnp.concatenate([total.astype(BF16), to_lanes(mark).astype(BF16)], axis=1)
    spread(nrow, load, outs[:4])
    total = None
    for i, cols in enumerate(chunks):
        copies[2 * len(chunks) + i].wait()
        term = times(ylow[ROWS, cols], linking[0, cols])
        total = term if total is None else total + term
    spread(lrow, total.astype(BF16), outs[4:])
    copies[-2].wait()
    copies[-1].wait()
    state[...] = x_top[...].astype(BF16)


def spread(row, load, outs):
    hot = hot_rows(row, SLOTS)
    for k, out in enumerate(outs):
        out[...] = times(hot[k * 128 : (k + 1) * 128], load).astype(BF16)


def own_adjoint(ylow, scol, coupling, own):
    upper = jnp.concatenate([scol[...]] * (NS // 128), axis=1) == 1.0
    low = ylow[ROWS]
    own[...] = jnp.where(upper, times(low, coupling[0]), times(low, coupling[1]))


def own_root_first(ylow, cost_top, coupling_far, own_root, coupling_root, sem):
    copies = [
        pltpu.make_async_copy(coupling_far.at[0, cols], coupling_root.at[cols], sem.at[i])
        for i, cols in enumerate(parts())
    ]
    for copy in copies:
        copy.start()
    total = -cost_top[...]
    for copy, cols in zip(copies, parts()):
        copy.wait()
        total = total + times(ylow[:ROOTS, cols], coupling_root[cols])
    own_root[...] = total


def own_first(ylow, scol, coupling_far, own, coupling, sem):
    copies = [
        pltpu.make_async_copy(coupling_far.at[pl.ds(1, 2), cols], coupling.at[:, cols], sem.at[i])
        for i, cols in enumerate(parts())
    ]
    for copy in copies:
        copy.start()
    first_total, second_total = None, None
    for copy, cols in zip(copies, parts()):
        copy.wait()
        low = ylow[ROWS, cols]
        one, two = times(low, coupling[0, cols]), times(low, coupling[1, cols])
        first_total = one if first_total is None else first_total + one
        second_total = two if second_total is None else second_total + two
    upper = jnp.concatenate([scol[...]] * (NS // 128), axis=1) == 1.0
    own[...] = jnp.where(upper, first_total, second_total)


def join(blocks, swapped, held):
    for k, block in enumerate(blocks):
        held[k * CAP_NODE : (k + 1) * CAP_NODE] = block[:CAP_NODE]
    held[256:] = swapped[...]


def primal_first(g0, g1, g2, g3, swapped, own, x, cost, rates, wrow, wcol, x_next, extra, *refs):
    *sends, held = refs
    join((g0, g1, g2, g3), swapped, held)
    mark = held[:, NS:].astype(F32)
    row = mark.T[:8]
    wcol[...] = mark
    wrow[...] = row
    primal_child(held[:, :NS], own, x[ROWS], cost, rates, mark, row, x_next, extra, sends)


def primal_second(g0, g1, g2, g3, swapped, own, x, cost, rates, wrow, wcol, x_next, extra, *refs):
    *sends, held = refs
    join((g0, g1, g2, g3), swapped, held)
    primal_child(held[...], own, x[...], cost, rates, wcol[...], wrow[...], x_next, extra, sends)


def primal_child(got, own, x_old, cost, rates, mark, row, x_next, extra, sends):
    tau = rates[:1, :1]
    adjoint = own[...] + times(hot_rows(row[:1] - 1.0, CHILD), got)
    new = jnp.maximum(x_old - tau * (cost[ROWS] - adjoint), 0.0)
    low = (2.0 * new - x_old).astype(BF16)
    x_next[...] = new
    extra[...] = low
    reply = times(hot_lanes(mark - 1.0, CHILD), low).astype(BF16)
    for k, send in enumerate(sends):
        send[:CAP_NODE] = reply[k * CAP_NODE : (k + 1) * CAP_NODE]
        send[CAP_NODE:] = reply[256 + k * CAP_NODE : 256 + (k + 1) * CAP_NODE]


def rooted(j):
    return slice(j * ROOTS, (j + 1) * ROOTS)


def summed(blocks, j):
    return sum(block[rooted((j + k) & 3)].astype(F32) for k, block in enumerate(blocks))


def root_first(g0, g1, g2, g3, own, x, rates, x_next, extra):
    blocks = (g0, g1, g2, g3)
    tau = rates[:1, :1]
    for j in range(4):
        slope = summed(blocks, j)
        if j == 0:
            x_old = x[...]
            slope = slope + own[...]
        else:
            x_old = blocks[(-j) & 3][rooted(4)].astype(F32)
        new = jnp.maximum(x_old + tau * slope, 0.0)
        x_next[rooted(j)] = new
        extra[rooted(j)] = (2.0 * new - x_old).astype(BF16)


def root_second(g0, g1, g2, g3, own, x, rates, extra, x_next):
    blocks = (g0, g1, g2, g3)
    tau = rates[:1, :1]
    for j in range(4):
        slope = summed(blocks, j)
        if j == 0:
            slope = slope + own[...]
        x_old = x[rooted(j)]
        new = jnp.maximum(x_old + tau * slope, 0.0)
        extra[rooted(j)] = (2.0 * new - x_old).astype(BF16)
        if j == 0:
            x_next[...] = new


def averages(x_start, x_root, x_root_next, x_child, x_child_next, average, move):
    roots = (x_root[:ROOTS] + x_root_next[...]) * 0.5
    children = (x_child[...] + x_child_next[...]) * 0.5
    average[:ROOTS] = roots
    average[ROWS] = children
    gap_roots = roots - x_start[:ROOTS]
    gap_children = children - x_start[ROWS]
    total = jnp.sum(gap_roots * gap_roots) + jnp.sum(gap_children * gap_children)
    move[...] = jnp.full((8, 128), total, F32)


def own_image(
    last, extra_child, extra_root, scol, coupling_root, coupling, y, right, rates, cost_top, base, *refs
):
    sigma = rates[1:2, :1]
    upper = jnp.concatenate([scol[...]] * (TILE // 128), axis=1) == 1.0
    child = extra_child[...]
    root = extra_root[:ROOTS]
    total = -cost_top[...]
    for cols in parts():
        image = jnp.where(
            upper, times_t(child, coupling[0, cols]), times_t(child, coupling[1, cols])
        )
        weights = coupling_root[cols]
        base_root = y[:ROOTS, cols] + sigma * (right[:ROOTS, cols] - times_t(root, weights))
        base[:ROOTS, cols] = base_root
        if not last:
            total = total + times(jnp.maximum(base_root, 0.0).astype(BF16), weights)
        base[ROWS, cols] = y[ROWS, cols] + sigma * (right[ROWS, cols] - image)
    if not last:
        (own_root,) = refs
        own_root[...] = total


def from_leaf(blocks, lback):
    hot = hot_lanes(lback[...], SLOTS)
    rows = None
    for k, block in enumerate(blocks):
        term = times(hot[:, k * 128 : (k + 1) * 128], block[...])
        rows = term if rows is None else rows + term
    return rows.astype(BF16)


def dual_leaf(last, b0, b1, b2, b3, lback, linking, base, rates, *refs):
    if last:
        (later,) = refs
    else:
        lsend, later, *outs = refs
    rows = from_leaf((b0, b1, b2, b3), lback)
    sigma = rates[1:2, :1]
    total = None
    for cols in parts():
        weights = linking[0, cols]
        new = base[ROWS, cols] - sigma * times_t(rows, weights)
        later[:, cols] = new
        if not last:
            product = times(jnp.maximum(new, 0.0).astype(BF16), weights)
            total = product if total is None else total + product
    if not last:
        spread(lsend[...], total.astype(BF16), outs)


def from_node(blocks, swapped, nback, held):
    join(blocks, swapped, held)
    return times(hot_lanes(nback[...], SLOTS), held[...]).astype(BF16)


def dual_node(g0, g1, g2, g3, swapped, nback, linking, base, later, rates, nsend, *refs):
    y_next, ylow, *outs, held = refs
    rows = from_node((g0, g1, g2, g3), swapped, nback, held)
    sigma = rates[1:2, :1]
    total = None
    for cols in parts():
        weights = linking[1, cols]
        new_root = jnp.maximum(base[:ROOTS, cols], 0.0)
        new = jnp.maximum(later[:, cols] - sigma * times_t(rows, weights), 0.0)
        low = new.astype(BF16)
        y_next[:ROOTS, cols] = new_root
        y_next[ROWS, cols] = new
        ylow[:ROOTS, cols] = new_root.astype(BF16)
        ylow[ROWS, cols] = low
        product = times(low, weights)
        total = product if total is None else total + product
    spread(nsend[...], total.astype(BF16), outs)


def dual_last(
    g0, g1, g2, g3, swapped, nback, linking, base, later, rates, y, y_start, primal_move, average, load, held
):
    rows = from_node((g0, g1, g2, g3), swapped, nback, held)
    sigma = rates[1:2, :1]
    move = jnp.zeros((1, TILE), F32)
    for cols in parts():
        new_root = jnp.maximum(base[:ROOTS, cols], 0.0)
        new = jnp.maximum(later[:, cols] - sigma * times_t(rows, linking[1, cols]), 0.0)
        mean_root = (y[:ROOTS, cols] + new_root) * 0.5
        mean = (y[ROWS, cols] + new) * 0.5
        average[:ROOTS, cols] = mean_root
        average[ROWS, cols] = mean
        gap_root = mean_root - y_start[:ROOTS, cols]
        gap = mean - y_start[ROWS, cols]
        move = move + jnp.sum(gap_root * gap_root, axis=0, keepdims=True)
        move = move + jnp.sum(gap * gap, axis=0, keepdims=True)
    lane = lax.broadcasted_iota(jnp.int32, load.shape, 2)
    load[...] = jnp.where(lane == 0, primal_move[:1], jnp.sum(move))


def pairs_of(place):
    pairs = []
    for i in range(N_LEAF * N_NODE):
        y, z, x, core = place(i >> 5, (i >> 3) & 3, (i >> 1) & 3, i & 1)
        pairs.append((i, ((y & 3) * 4 + (z & 3)) * N_NODE + (x & 3) * 2 + core))
    return ("leaf", "node"), pairs


def outer_ring(k):
    return pairs_of(lambda y, z, x, c: (y, z + k, x, c) if c else (y + k, z, x, c))


def inner_ring(k):
    return pairs_of(lambda y, z, x, c: (y + k, z, x, c) if c else (y, z + k, x, c))


def ring_x(k):
    return pairs_of(lambda y, z, x, c: (y, z, x + k, c))


def sibling(array):
    return lax.ppermute(array, *pairs_of(lambda y, z, x, c: (y, z, x, 1 - c)))


def shifted(blocks, ring, sign=1):
    got = {0: blocks[0]}
    for k in (2, 1, 3):
        got[k] = lax.ppermute(blocks[k], *ring((sign * k) % 4))
    return [got[k] for k in range(4)]


def swap_node(blocks, sign, before):
    got = shifted(blocks, ring_x, sign)
    halves = jnp.concatenate([block[CAP_NODE:] for block in got], axis=0)
    halves, before = lax.optimization_barrier((halves, before))
    return got + [sibling(halves)], before


def sum_leaf(blocks, own, state, before):
    got, before = lax.optimization_barrier((shifted(blocks, outer_ring), before))
    got = [block.astype(F32) for block in got]
    total = ((got[0] + got[1]) + got[2]) + got[3]
    sent = jnp.concatenate([total[:ROOTS] + own, total[ROOTS:]], axis=0).astype(BF16)
    if state is not None:
        sent = jnp.concatenate([sent, state], axis=0)
    return [total.astype(BF16)] + shifted([sent] * 4, inner_ring)[1:], before


def part_of(kernel, flag):
    def run(*refs):
        kernel(flag, *refs)

    return run


def shards(x_start, y_start, cost_vec, right_side, omega, coupling, linking, parent, section):
    unit = 2 * CHILD * NS * NC
    rates = jnp.broadcast_to(jnp.stack([STEP / omega[0], STEP * omega[0]])[:, None], (2, 128))
    field = ((NODES, NC), F32)
    field_low = ((NODES, NC), BF16)
    states = ((NODES, NS), F32)
    block = ((128, NS), BF16)
    block_mark = ((128, NS + 128), BF16)
    kids = ((CHILD, NS), F32)
    kids_low = ((CHILD, NS), BF16)
    kids_field = ((CHILD, NC), F32)
    tops = ((ROOTS, NS), F32)
    plane = ((4 * ROOTS, NS), F32)
    row = ((1, CHILD), F32)
    col = ((CHILD, 128), F32)
    held = [pltpu.VMEM((SLOTS, NS), BF16)]

    *sent, y_start, linking, ylow, nsend, nback, lsend, lback, scol, x_top, cost_top, state = call(
        first,
        [block_mark] * 4 + [block] * 4
        + [field, ((2, NC, NS), BF16), field_low, row, col, row, col, col, tops, tops, ((ROOTS, NS), BF16)],
        [parent.reshape(1, NODES), section.reshape(1, NODES), y_start, linking, x_start, cost_vec],
        2 * unit,
        [pltpu.SemaphoreType.DMA((3 * NC // TILE + 2,))],
        (2, 3, 4, 5),
    )
    chunk_sems = [pltpu.SemaphoreType.DMA((NC // TILE,))]
    own_root, coupling_root = call(
        own_root_first, [tops, ((NC, NS), BF16)], [ylow, cost_top, coupling], unit // 8, chunk_sems, (2,)
    )
    own, coupling = call(
        own_first, [kids, ((2, NC, NS), BF16)], [ylow, scol, coupling], 2 * unit, chunk_sems, (2,)
    )
    got_leaf, _ = sum_leaf(sent[4:], own_root, state, own_root)
    got_node, (got_leaf, own) = swap_node(sent[:4], 1, (got_leaf, own))

    x_root, extra_root = call(
        root_first,
        [plane, block],
        got_leaf + [own_root, x_top, rates],
        0,
    )
    own, extra_root = lax.optimization_barrier((own, extra_root))
    wrow, wcol, x_child, extra_child, *out_node = call(
        primal_first,
        [((8, SLOTS), F32), ((SLOTS, 128), F32), kids, kids_low] + [block] * 4,
        got_node + [own, x_start, cost_vec, rates],
        unit // 4,
        [pltpu.VMEM((SLOTS, NS + 128), BF16)],
    )
    base, own_root = call(
        part_of(own_image, False),
        [field, tops],
        [
            extra_child, extra_root, scol, coupling_root, coupling, y_start, right_side, rates, cost_top
        ],
        2 * unit,
    )
    back_leaf = shifted([extra_root] * 4, outer_ring)
    back_node, (back_leaf, base) = swap_node(out_node, -1, (back_leaf, base))
    later, *out_leaf = call(
        part_of(dual_leaf, False),
        [kids_field] + [block] * 4,
        back_leaf + [lback, linking, base, rates, lsend],
        2 * unit,
    )
    y_next, ylow, *out_node = call(
        dual_node,
        [field, field_low] + [block] * 4,
        back_node + [nback, linking, base, later, rates, nsend],
        2 * unit,
        held,
    )
    got_leaf, ylow = sum_leaf(out_leaf, own_root, None, ylow)
    (own,) = call(own_adjoint, [kids], [ylow, scol, coupling], 2 * unit)
    got_node, (got_leaf, own) = swap_node(out_node, 1, (got_leaf, own))

    extra_root, x_top = call(
        root_second,
        [block, tops],
        got_leaf + [own_root, x_root, rates],
        0,
    )
    own, extra_root = lax.optimization_barrier((own, extra_root))
    x_child_next, extra_child, *out_node = call(
        primal_second,
        [kids, kids_low] + [block] * 4,
        got_node + [own, x_child, cost_vec, rates, wrow, wcol],
        unit // 4,
        held,
    )
    x_average, primal_move = call(
        averages,
        [states, ((8, 128), F32)],
        [x_start, x_root, x_top, x_child, x_child_next],
        0,
    )
    (base,) = call(
        part_of(own_image, True),
        [field],
        [extra_child, extra_root, scol, coupling_root, coupling, y_next, right_side, rates, cost_top],
        2 * unit,
    )
    back_leaf = shifted([extra_root] * 4, outer_ring)
    back_node, (back_leaf, base) = swap_node(out_node, -1, (back_leaf, base))
    (later,) = call(
        part_of(dual_leaf, True), [kids_field], back_leaf + [lback, linking, base, rates], unit
    )
    y_average, load = call(
        dual_last,
        [field, ((N_LEAF * N_NODE, 1, 128), F32)],
        back_node + [nback, linking, base, later, rates, y_next, y_start, primal_move],
        unit,
        held,
    )
    moves = lax.all_to_all(load, ("leaf", "node"), split_axis=0, concat_axis=0, tiled=True)
    moves = jnp.sum(moves[:, 0, :2], axis=0)
    omega_new = jnp.sqrt((moves[1:] + 1e-06) / (moves[:1] + 1e-06))
    return (x_average, y_average, omega_new)


def solution(mesh):
    both = P(("leaf", "node"), None)
    flat = P(("leaf", "node"))
    return jax.shard_map(
        shards,
        mesh=mesh,
        in_specs=(both, both, both, both, P(), P(), P(), flat, flat),
        out_specs=(both, both, P()),
        check_vma=False,
    )
```

```python
import jax
import jax.numpy as jnp
from jax import lax
from jax.experimental import pallas as pl
from jax.experimental.pallas import tpu as pltpu
from jax.sharding import PartitionSpec as P

NS = 512
NC = 2048
ROOTS = 32
CHILD = 256
NODES = 288
N_LEAF = 16
N_NODE = 8
CAP_NODE = 64
SLOTS = 512
TILE = 512
VMEM_LIMIT = 24 * 2**20
STEP = 0.3
F32 = jnp.float32
BF16 = jnp.bfloat16
ROWS = slice(ROOTS, NODES)


def times(a, b):
    return lax.dot_general(a, b, (((1,), (0,)), ((), ())), preferred_element_type=F32)


def times_t(a, b):
    return lax.dot_general(a, b, (((1,), (1,)), ((), ())), preferred_element_type=F32)


def hot_rows(code, count):
    places = lax.broadcasted_iota(jnp.int32, (count, code.shape[1]), 0).astype(F32)
    return jnp.where(places == code, 1.0, 0.0).astype(BF16)


def hot_lanes(code, count):
    wide = jnp.concatenate([code] * (count // 128), axis=1)
    places = lax.broadcasted_iota(jnp.int32, wide.shape, 1).astype(F32)
    return jnp.where(places == wide, 1.0, 0.0).astype(BF16)


def to_lanes(row):
    return jnp.broadcast_to(row, (128, row.shape[1])).T


def call(kernel, outs, arrays, flops, scratch=(), far=()):
    out_shapes = [jax.ShapeDtypeStruct(shape, dtype) for shape, dtype in outs]
    moved = sum(a.size * a.dtype.itemsize for a in list(arrays) + out_shapes)
    out_shapes = [pltpu.VMEM(shape, dtype) for shape, dtype in outs]
    arrays = [
        pltpu.with_memory_space_constraint(a, pltpu.HBM) if i in far else a for i, a in enumerate(arrays)
    ]
    return pl.pallas_call(
        kernel,
        out_shape=out_shapes,
        in_specs=[pl.BlockSpec(memory_space=pl.ANY if i in far else pltpu.VMEM) for i in range(len(arrays))],
        out_specs=[pl.BlockSpec(memory_space=pltpu.VMEM)] * len(outs),
        scratch_shapes=list(scratch),
        compiler_params=pltpu.CompilerParams(vmem_limit_bytes=VMEM_LIMIT),
        cost_estimate=pl.CostEstimate(flops=flops, bytes_accessed=moved // 8, transcendentals=0),
    )(*arrays)


def parts():
    return [slice(i * TILE, (i + 1) * TILE) for i in range(NC // TILE)]


def first(code, y_far, linking_far, x_far, cost_far, *refs):
    *outs, y, linking, ylow, nsend, nback, lsend, lback, scol, x_top, cost_top, state, sem = refs
    chunks = parts()
    copies = []
    for cols in chunks:
        copies.append((y_far.at[:, cols], y.at[:, cols]))
        copies.append((linking_far.at[1, cols], linking.at[1, cols]))
    for cols in chunks:
        copies.append((linking_far.at[0, cols], linking.at[0, cols]))
    copies += [(x_far.at[:ROOTS], x_top), (cost_far.at[:ROOTS], cost_top)]
    copies = [pltpu.make_async_copy(a, b, sem.at[i]) for i, (a, b) in enumerate(copies)]
    for copy in copies:
        copy.start()
    packed = code[...]
    upper = (packed >> 16) == 1
    parent = packed & 0xFFFF
    here = lax.axis_index("leaf") * N_NODE + lax.axis_index("node")
    owner = ((parent.astype(F32) + 0.5) * (1.0 / NODES)).astype(jnp.int32)
    local = parent - owner * NODES
    ry = ((owner >> 5) - (here >> 5)) & 3
    rz = ((owner >> 3) - (here >> 3)) & 3
    rx = ((owner >> 1) - (here >> 1)) & 3
    rc = (owner ^ here) & 1
    odd = (here & 1) == 1
    outer = jnp.where(odd, rz, ry)
    inner = jnp.where(odd, ry, rz)
    lrow = jnp.where(upper, outer * 128 + inner * ROOTS + local, -1).astype(F32)
    lend = jnp.where(upper, ((-outer) & 3) * 128 + inner * ROOTS + local, -1).astype(F32)
    peer = rx * 2 + rc
    peers = lax.broadcasted_iota(jnp.int32, (N_NODE, CHILD), 0)
    member = jnp.where((peers == peer) & jnp.logical_not(upper), 1.0, 0.0)
    before = lax.broadcasted_iota(jnp.int32, (CHILD, CHILD), 0) <= lax.broadcasted_iota(
        jnp.int32, (CHILD, CHILD), 1
    )
    counts = times(member.astype(BF16), jnp.where(before, 1.0, 0.0).astype(BF16))
    rank = jnp.sum(member * counts, axis=0, keepdims=True) - 1.0
    nrow = jnp.where(upper, -1.0, (peer * CAP_NODE).astype(F32) + rank)
    nend = jnp.where(upper, -1.0, (rc * 256 + rx * CAP_NODE).astype(F32) + rank)
    mark = jnp.where(upper, 0, local - (ROOTS - 1)).astype(F32)
    nsend[...] = nrow
    lsend[...] = lrow
    nback[...] = to_lanes(nend)
    lback[...] = to_lanes(lend)
    scol[...] = to_lanes(jnp.where(upper, 1.0, 2.0))
    total = None
    for i, cols in enumerate(chunks):
        copies[2 * i].wait()
        copies[2 * i + 1].wait()
        low = y[:, cols].astype(BF16)
        ylow[:, cols] = low
        term = times(low[ROWS], linking[1, cols])
        total = term if total is None else total + term
    load = jnp.concatenate([total.astype(BF16), to_lanes(mark).astype(BF16)], axis=1)
    spread(nrow, load, outs[:4])
    total = None
    for i, cols in enumerate(chunks):
        copies[2 * len(chunks) + i].wait()
        term = times(ylow[ROWS, cols], linking[0, cols])
        total = term if total is None else total + term
    spread(lrow, total.astype(BF16), outs[4:])
    copies[-2].wait()
    copies[-1].wait()
    state[...] = x_top[...].astype(BF16)


def spread(row, load, outs):
    hot = hot_rows(row, SLOTS)
    for k, out in enumerate(outs):
        out[...] = times(hot[k * 128 : (k + 1) * 128], load).astype(BF16)


def own_adjoint(ylow, scol, coupling, own):
    upper = jnp.concatenate([scol[...]] * (NS // 128), axis=1) == 1.0
    low = ylow[ROWS]
    own[...] = jnp.where(upper, times(low, coupling[0]), times(low, coupling[1]))


def own_root_first(ylow, cost_top, coupling_far, own_root, coupling_root, sem):
    copies = [
        pltpu.make_async_copy(coupling_far.at[0, cols], coupling_root.at[cols], sem.at[i])
        for i, cols in enumerate(parts())
    ]
    for copy in copies:
        copy.start()
    total = -cost_top[...]
    for copy, cols in zip(copies, parts()):
        copy.wait()
        total = total + times(ylow[:ROOTS, cols], coupling_root[cols])
    own_root[...] = total


def own_first(ylow, scol, coupling_far, own, coupling, sem):
    copies = [
        pltpu.make_async_copy(coupling_far.at[pl.ds(1, 2), cols], coupling.at[:, cols], sem.at[i])
        for i, cols in enumerate(parts())
    ]
    for copy in copies:
        copy.start()
    first_total, second_total = None, None
    for copy, cols in zip(copies, parts()):
        copy.wait()
        low = ylow[ROWS, cols]
        one, two = times(low, coupling[0, cols]), times(low, coupling[1, cols])
        first_total = one if first_total is None else first_total + one
        second_total = two if second_total is None else second_total + two
    upper = jnp.concatenate([scol[...]] * (NS // 128), axis=1) == 1.0
    own[...] = jnp.where(upper, first_total, second_total)


def join(blocks, swapped, held):
    for k, block in enumerate(blocks):
        held[k * CAP_NODE : (k + 1) * CAP_NODE] = block[:CAP_NODE]
    held[256:] = swapped[...]


def primal_first(g0, g1, g2, g3, swapped, own, x, cost, rates, wrow, wcol, x_next, extra, *refs):
    *sends, held = refs
    join((g0, g1, g2, g3), swapped, held)
    mark = held[:, NS:].astype(F32)
    row = mark.T[:8]
    wcol[...] = mark
    wrow[...] = row
    primal_child(held[:, :NS], own, x[ROWS], cost, rates, mark, row, x_next, extra, sends)


def primal_second(g0, g1, g2, g3, swapped, own, x, cost, rates, wrow, wcol, x_next, extra, *refs):
    *sends, held = refs
    join((g0, g1, g2, g3), swapped, held)
    primal_child(held[...], own, x[...], cost, rates, wcol[...], wrow[...], x_next, extra, sends)


def primal_child(got, own, x_old, cost, rates, mark, row, x_next, extra, sends):
    tau = rates[:1, :1]
    adjoint = own[...] + times(hot_rows(row[:1] - 1.0, CHILD), got)
    new = jnp.maximum(x_old - tau * (cost[ROWS] - adjoint), 0.0)
    low = (2.0 * new - x_old).astype(BF16)
    x_next[...] = new
    extra[...] = low
    reply = times(hot_lanes(mark - 1.0, CHILD), low).astype(BF16)
    for k, send in enumerate(sends):
        send[:CAP_NODE] = reply[k * CAP_NODE : (k + 1) * CAP_NODE]
        send[CAP_NODE:] = reply[256 + k * CAP_NODE : 256 + (k + 1) * CAP_NODE]


def rooted(j):
    return slice(j * ROOTS, (j + 1) * ROOTS)


def summed(blocks, j):
    return sum(block[rooted((j + k) & 3)].astype(F32) for k, block in enumerate(blocks))


def root_first(g0, g1, g2, g3, own, x, rates, x_next, extra):
    blocks = (g0, g1, g2, g3)
    tau = rates[:1, :1]
    for j in range(4):
        slope = summed(blocks, j)
        if j == 0:
            x_old = x[...]
            slope = slope + own[...]
        else:
            x_old = blocks[(-j) & 3][rooted(4)].astype(F32)
        new = jnp.maximum(x_old + tau * slope, 0.0)
        x_next[rooted(j)] = new
        extra[rooted(j)] = (2.0 * new - x_old).astype(BF16)


def root_second(g0, g1, g2, g3, own, x, rates, extra, x_next):
    blocks = (g0, g1, g2, g3)
    tau = rates[:1, :1]
    for j in range(4):
        slope = summed(blocks, j)
        if j == 0:
            slope = slope + own[...]
        x_old = x[rooted(j)]
        new = jnp.maximum(x_old + tau * slope, 0.0)
        extra[rooted(j)] = (2.0 * new - x_old).astype(BF16)
        if j == 0:
            x_next[...] = new


def averages(x_start, x_root, x_root_next, x_child, x_child_next, average, move):
    roots = (x_root[:ROOTS] + x_root_next[...]) * 0.5
    children = (x_child[...] + x_child_next[...]) * 0.5
    average[:ROOTS] = roots
    average[ROWS] = children
    gap_roots = roots - x_start[:ROOTS]
    gap_children = children - x_start[ROWS]
    total = jnp.sum(gap_roots * gap_roots) + jnp.sum(gap_children * gap_children)
    move[...] = jnp.full((8, 128), total, F32)


def own_image(
    last, extra_child, extra_root, scol, coupling_root, coupling, y, right, rates, cost_top, base, *refs
):
    sigma = rates[1:2, :1]
    upper = jnp.concatenate([scol[...]] * (TILE // 128), axis=1) == 1.0
    child = extra_child[...]
    root = extra_root[:ROOTS]
    total = -cost_top[...]
    for cols in parts():
        image = jnp.where(
            upper, times_t(child, coupling[0, cols]), times_t(child, coupling[1, cols])
        )
        weights = coupling_root[cols]
        base_root = y[:ROOTS, cols] + sigma * (right[:ROOTS, cols] - times_t(root, weights))
        base[:ROOTS, cols] = base_root
        if not last:
            total = total + times(jnp.maximum(base_root, 0.0).astype(BF16), weights)
        base[ROWS, cols] = y[ROWS, cols] + sigma * (right[ROWS, cols] - image)
    if not last:
        (own_root,) = refs
        own_root[...] = total


def from_leaf(blocks, lback):
    hot = hot_lanes(lback[...], SLOTS)
    rows = None
    for k, block in enumerate(blocks):
        term = times(hot[:, k * 128 : (k + 1) * 128], block[...])
        rows = term if rows is None else rows + term
    return rows.astype(BF16)


def dual_leaf(last, b0, b1, b2, b3, lback, linking, base, rates, *refs):
    if last:
        (later,) = refs
    else:
        lsend, later, *outs = refs
    rows = from_leaf((b0, b1, b2, b3), lback)
    sigma = rates[1:2, :1]
    total = None
    for cols in parts():
        weights = linking[0, cols]
        new = base[ROWS, cols] - sigma * times_t(rows, weights)
        later[:, cols] = new
        if not last:
            product = times(jnp.maximum(new, 0.0).astype(BF16), weights)
            total = product if total is None else total + product
    if not last:
        spread(lsend[...], total.astype(BF16), outs)


def from_node(blocks, swapped, nback, held):
    join(blocks, swapped, held)
    return times(hot_lanes(nback[...], SLOTS), held[...]).astype(BF16)


def dual_node(g0, g1, g2, g3, swapped, nback, linking, base, later, rates, nsend, *refs):
    y_next, ylow, *outs, held = refs
    rows = from_node((g0, g1, g2, g3), swapped, nback, held)
    sigma = rates[1:2, :1]
    total = None
    for cols in parts():
        weights = linking[1, cols]
        new_root = jnp.maximum(base[:ROOTS, cols], 0.0)
        new = jnp.maximum(later[:, cols] - sigma * times_t(rows, weights), 0.0)
        low = new.astype(BF16)
        y_next[:ROOTS, cols] = new_root
        y_next[ROWS, cols] = new
        ylow[:ROOTS, cols] = new_root.astype(BF16)
        ylow[ROWS, cols] = low
        product = times(low, weights)
        total = product if total is None else total + product
    spread(nsend[...], total.astype(BF16), outs)


def dual_last(
    g0, g1, g2, g3, swapped, nback, linking, base, later, rates, y, y_start, primal_move, average, load, held
):
    rows = from_node((g0, g1, g2, g3), swapped, nback, held)
    sigma = rates[1:2, :1]
    move = jnp.zeros((1, TILE), F32)
    for cols in parts():
        new_root = jnp.maximum(base[:ROOTS, cols], 0.0)
        new = jnp.maximum(later[:, cols] - sigma * times_t(rows, linking[1, cols]), 0.0)
        mean_root = (y[:ROOTS, cols] + new_root) * 0.5
        mean = (y[ROWS, cols] + new) * 0.5
        average[:ROOTS, cols] = mean_root
        average[ROWS, cols] = mean
        gap_root = mean_root - y_start[:ROOTS, cols]
        gap = mean - y_start[ROWS, cols]
        move = move + jnp.sum(gap_root * gap_root, axis=0, keepdims=True)
        move = move + jnp.sum(gap * gap, axis=0, keepdims=True)
    lane = lax.broadcasted_iota(jnp.int32, load.shape, 2)
    load[...] = jnp.where(lane == 0, primal_move[:1], jnp.sum(move))


def pairs_of(place):
    pairs = []
    for i in range(N_LEAF * N_NODE):
        y, z, x, core = place(i >> 5, (i >> 3) & 3, (i >> 1) & 3, i & 1)
        pairs.append((i, ((y & 3) * 4 + (z & 3)) * N_NODE + (x & 3) * 2 + core))
    return ("leaf", "node"), pairs


def outer_ring(k):
    return pairs_of(lambda y, z, x, c: (y, z + k, x, c) if c else (y + k, z, x, c))


def inner_ring(k):
    return pairs_of(lambda y, z, x, c: (y + k, z, x, c) if c else (y, z + k, x, c))


def ring_x(k):
    return pairs_of(lambda y, z, x, c: (y, z, x + k, c))


def sibling(array):
    return lax.ppermute(array, *pairs_of(lambda y, z, x, c: (y, z, x, 1 - c)))


def shifted(blocks, ring, sign=1):
    got = {0: blocks[0]}
    for k in (2, 1, 3):
        got[k] = lax.ppermute(blocks[k], *ring((sign * k) % 4))
    return [got[k] for k in range(4)]


def swap_node(got, before):
    halves = jnp.concatenate([block[CAP_NODE:] for block in got], axis=0)
    halves, before = lax.optimization_barrier((halves, before))
    return got + [sibling(halves)], before


def ring_gather(rows, ring):
    one = lax.ppermute(rows, *ring(1))
    three = lax.ppermute(rows, *ring(3))
    return [rows, one, lax.ppermute(one, *ring(1)), three]


def ring_sum(blocks, ring, before, beside):
    ahead = lax.ppermute(blocks[2], *ring(1))
    behind = lax.ppermute(blocks[3], *ring(3))
    (ahead, behind), before = lax.optimization_barrier(((ahead, behind), before))
    ahead = (ahead.astype(F32) + blocks[1].astype(F32)).astype(BF16)
    ahead = lax.ppermute(ahead, *ring(1))
    ahead, beside = lax.optimization_barrier((ahead, beside))
    return (blocks[0].astype(F32) + behind.astype(F32)) + ahead.astype(F32), before, beside


def sum_leaf(blocks, own, state, before, beside):
    total, before, beside = ring_sum(blocks, outer_ring, before, beside)
    sent = jnp.concatenate([total[:ROOTS] + own, total[ROOTS:]], axis=0).astype(BF16)
    if state is not None:
        sent = jnp.concatenate([sent, state], axis=0)
    return [total.astype(BF16)] + ring_gather(sent, inner_ring)[1:], before, beside


def part_of(kernel, flag):
    def run(*refs):
        kernel(flag, *refs)

    return run


def shards(x_start, y_start, cost_vec, right_side, omega, coupling, linking, parent, section):
    unit = 2 * CHILD * NS * NC
    code = (section * 65536 + parent)[ROOTS:].reshape(1, CHILD)
    rates = jnp.broadcast_to(jnp.stack([STEP / omega[0], STEP * omega[0]])[:, None], (2, 128))
    field = ((NODES, NC), F32)
    field_low = ((NODES, NC), BF16)
    states = ((NODES, NS), F32)
    block = ((128, NS), BF16)
    block_mark = ((128, NS + 128), BF16)
    kids = ((CHILD, NS), F32)
    kids_low = ((CHILD, NS), BF16)
    kids_field = ((CHILD, NC), F32)
    tops = ((ROOTS, NS), F32)
    plane = ((4 * ROOTS, NS), F32)
    row = ((1, CHILD), F32)
    col = ((CHILD, 128), F32)
    held = [pltpu.VMEM((SLOTS, NS), BF16)]

    *sent, y_start, linking, ylow, nsend, nback, lsend, lback, scol, x_top, cost_top, state = call(
        first,
        [block_mark] * 4 + [block] * 4
        + [field, ((2, NC, NS), BF16), field_low, row, col, row, col, col, tops, tops, ((ROOTS, NS), BF16)],
        [code, y_start, linking, x_start, cost_vec],
        2 * unit,
        [pltpu.SemaphoreType.DMA((3 * NC // TILE + 2,))],
        (1, 2, 3, 4),
    )
    chunk_sems = [pltpu.SemaphoreType.DMA((NC // TILE,))]
    own_root, coupling_root = call(
        own_root_first, [tops, ((NC, NS), BF16)], [ylow, cost_top, coupling], unit // 8, chunk_sems, (2,)
    )
    own, coupling = call(
        own_first, [kids, ((2, NC, NS), BF16)], [ylow, scol, coupling], 2 * unit, chunk_sems, (2,)
    )
    got_node = shifted(sent[:4], ring_x, 1)
    got_leaf, _, (own, got_node[1]) = sum_leaf(sent[4:], own_root, state, own_root, (own, got_node[1]))
    got_node, got_leaf = swap_node(got_node, got_leaf)

    x_root, extra_root = call(
        root_first,
        [plane, block],
        got_leaf + [own_root, x_top, rates],
        0,
    )
    own, extra_root = lax.optimization_barrier((own, extra_root))
    wrow, wcol, x_child, extra_child, *out_node = call(
        primal_first,
        [((8, SLOTS), F32), ((SLOTS, 128), F32), kids, kids_low] + [block] * 4,
        got_node + [own, x_start, cost_vec, rates],
        unit // 4,
        [pltpu.VMEM((SLOTS, NS + 128), BF16)],
    )
    base, own_root = call(
        part_of(own_image, False),
        [field, tops],
        [
            extra_child, extra_root, scol, coupling_root, coupling, y_start, right_side, rates, cost_top
        ],
        2 * unit,
    )
    back_leaf = ring_gather(extra_root, outer_ring)
    back_node, (back_leaf, base) = swap_node(shifted(out_node, ring_x, -1), (back_leaf, base))
    later, *out_leaf = call(
        part_of(dual_leaf, False),
        [kids_field] + [block] * 4,
        back_leaf + [lback, linking, base, rates, lsend],
        2 * unit,
    )
    y_next, ylow, *out_node = call(
        dual_node,
        [field, field_low] + [block] * 4,
        back_node + [nback, linking, base, later, rates, nsend],
        2 * unit,
        held,
    )
    (own,) = call(own_adjoint, [kids], [ylow, scol, coupling], 2 * unit)
    got_node = shifted(out_node, ring_x, 1)
    got_leaf, ylow, (own, got_node[1]) = sum_leaf(out_leaf, own_root, None, ylow, (own, got_node[1]))
    got_node, got_leaf = swap_node(got_node, got_leaf)

    extra_root, x_top = call(
        root_second,
        [block, tops],
        got_leaf + [own_root, x_root, rates],
        0,
    )
    own, extra_root = lax.optimization_barrier((own, extra_root))
    x_child_next, extra_child, *out_node = call(
        primal_second,
        [kids, kids_low] + [block] * 4,
        got_node + [own, x_child, cost_vec, rates, wrow, wcol],
        unit // 4,
        held,
    )
    x_average, primal_move = call(
        averages,
        [states, ((8, 128), F32)],
        [x_start, x_root, x_top, x_child, x_child_next],
        0,
    )
    (base,) = call(
        part_of(own_image, True),
        [field],
        [extra_child, extra_root, scol, coupling_root, coupling, y_next, right_side, rates, cost_top],
        2 * unit,
    )
    back_leaf = ring_gather(extra_root, outer_ring)
    back_node, (back_leaf, base) = swap_node(shifted(out_node, ring_x, -1), (back_leaf, base))
    (later,) = call(
        part_of(dual_leaf, True), [kids_field], back_leaf + [lback, linking, base, rates], unit
    )
    y_average, load = call(
        dual_last,
        [field, ((N_LEAF * N_NODE, 1, 128), F32)],
        back_node + [nback, linking, base, later, rates, y_next, y_start, primal_move],
        unit,
        held,
    )
    moves = lax.all_to_all(load, ("leaf", "node"), split_axis=0, concat_axis=0, tiled=True)
    moves = jnp.sum(moves[:, 0, :2], axis=0)
    omega_new = jnp.sqrt((moves[1:] + 1e-06) / (moves[:1] + 1e-06))
    return (x_average, y_average, omega_new)


def solution(mesh):
    both = P(("leaf", "node"), None)
    flat = P(("leaf", "node"))
    return jax.shard_map(
        shards,
        mesh=mesh,
        in_specs=(both, both, both, both, P(), P(), P(), flat, flat),
        out_specs=(both, both, P()),
        check_vma=False,
    )
```

```python
import jax
import jax.numpy as jnp
from jax import lax
from jax.experimental import pallas as pl
from jax.experimental.pallas import tpu as pltpu
from jax.sharding import PartitionSpec as P

NS = 512
NC = 2048
ROOTS = 32
CHILD = 256
NODES = 288
N_LEAF = 16
N_NODE = 8
CAP_NODE = 64
SLOTS = 512
TILE = 512
VMEM_LIMIT = 24 * 2**20
STEP = 0.3
F32 = jnp.float32
BF16 = jnp.bfloat16
ROWS = slice(ROOTS, NODES)


def times(a, b):
    return lax.dot_general(a, b, (((1,), (0,)), ((), ())), preferred_element_type=F32)


def times_t(a, b):
    return lax.dot_general(a, b, (((1,), (1,)), ((), ())), preferred_element_type=F32)


def hot_rows(code, count):
    places = lax.broadcasted_iota(jnp.int32, (count, code.shape[1]), 0).astype(F32)
    return jnp.where(places == code, 1.0, 0.0).astype(BF16)


def hot_lanes(code, count):
    wide = jnp.concatenate([code] * (count // 128), axis=1)
    places = lax.broadcasted_iota(jnp.int32, wide.shape, 1).astype(F32)
    return jnp.where(places == wide, 1.0, 0.0).astype(BF16)


def to_lanes(row):
    return jnp.broadcast_to(row, (128, row.shape[1])).T


def call(kernel, outs, arrays, flops, scratch=(), far=()):
    out_shapes = [jax.ShapeDtypeStruct(shape, dtype) for shape, dtype in outs]
    moved = sum(a.size * a.dtype.itemsize for a in list(arrays) + out_shapes)
    out_shapes = [pltpu.VMEM(shape, dtype) for shape, dtype in outs]
    arrays = [
        pltpu.with_memory_space_constraint(a, pltpu.HBM) if i in far else a for i, a in enumerate(arrays)
    ]
    return pl.pallas_call(
        kernel,
        out_shape=out_shapes,
        in_specs=[pl.BlockSpec(memory_space=pl.ANY if i in far else pltpu.VMEM) for i in range(len(arrays))],
        out_specs=[pl.BlockSpec(memory_space=pltpu.VMEM)] * len(outs),
        scratch_shapes=list(scratch),
        compiler_params=pltpu.CompilerParams(vmem_limit_bytes=VMEM_LIMIT),
        cost_estimate=pl.CostEstimate(flops=flops, bytes_accessed=moved // 8, transcendentals=0),
    )(*arrays)


def parts():
    return [slice(i * TILE, (i + 1) * TILE) for i in range(NC // TILE)]


def first(code, y_far, linking_far, x_far, cost_far, *refs):
    *outs, y, linking, ylow, nsend, nback, lsend, lback, scol, x_top, cost_top, state, sem = refs
    chunks = parts()
    copies = []
    for cols in chunks:
        copies.append((y_far.at[:, cols], y.at[:, cols]))
        copies.append((linking_far.at[1, cols], linking.at[1, cols]))
    for cols in chunks:
        copies.append((linking_far.at[0, cols], linking.at[0, cols]))
    copies += [(x_far.at[:ROOTS], x_top), (cost_far.at[:ROOTS], cost_top)]
    copies = [pltpu.make_async_copy(a, b, sem.at[i]) for i, (a, b) in enumerate(copies)]
    for copy in copies:
        copy.start()
    packed = code[...]
    upper = (packed >> 16) == 1
    parent = packed & 0xFFFF
    here = lax.axis_index("leaf") * N_NODE + lax.axis_index("node")
    owner = ((parent.astype(F32) + 0.5) * (1.0 / NODES)).astype(jnp.int32)
    local = parent - owner * NODES
    ry = ((owner >> 5) - (here >> 5)) & 3
    rz = ((owner >> 3) - (here >> 3)) & 3
    rx = ((owner >> 1) - (here >> 1)) & 3
    rc = (owner ^ here) & 1
    odd = (here & 1) == 1
    outer = jnp.where(odd, rz, ry)
    inner = jnp.where(odd, ry, rz)
    lrow = jnp.where(upper, outer * 128 + inner * ROOTS + local, -1).astype(F32)
    lend = jnp.where(upper, ((-outer) & 3) * 128 + inner * ROOTS + local, -1).astype(F32)
    peer = rx * 2 + rc
    peers = lax.broadcasted_iota(jnp.int32, (N_NODE, CHILD), 0)
    member = jnp.where((peers == peer) & jnp.logical_not(upper), 1.0, 0.0)
    before = lax.broadcasted_iota(jnp.int32, (CHILD, CHILD), 0) <= lax.broadcasted_iota(
        jnp.int32, (CHILD, CHILD), 1
    )
    counts = times(member.astype(BF16), jnp.where(before, 1.0, 0.0).astype(BF16))
    rank = jnp.sum(member * counts, axis=0, keepdims=True) - 1.0
    nrow = jnp.where(upper, -1.0, (peer * CAP_NODE).astype(F32) + rank)
    nend = jnp.where(upper, -1.0, (rc * 256 + rx * CAP_NODE).astype(F32) + rank)
    mark = jnp.where(upper, 0, local - (ROOTS - 1)).astype(F32)
    nsend[...] = nrow
    lsend[...] = lrow
    nback[...] = to_lanes(nend)
    lback[...] = to_lanes(lend)
    scol[...] = to_lanes(jnp.where(upper, 1.0, 2.0))
    total = None
    for i, cols in enumerate(chunks):
        copies[2 * i].wait()
        copies[2 * i + 1].wait()
        low = y[:, cols].astype(BF16)
        ylow[:, cols] = low
        term = times(low[ROWS], linking[1, cols])
        total = term if total is None else total + term
    load = jnp.concatenate([total.astype(BF16), to_lanes(mark).astype(BF16)], axis=1)
    spread(nrow, load, outs[:4])
    total = None
    for i, cols in enumerate(chunks):
        copies[2 * len(chunks) + i].wait()
        term = times(ylow[ROWS, cols], linking[0, cols])
        total = term if total is None else total + term
    spread(lrow, total.astype(BF16), outs[4:])
    copies[-2].wait()
    copies[-1].wait()
    state[...] = x_top[...].astype(BF16)


def spread(row, load, outs):
    hot = hot_rows(row, SLOTS)
    for k, out in enumerate(outs):
        out[...] = times(hot[k * 128 : (k + 1) * 128], load).astype(BF16)


def own_adjoint(ylow, scol, coupling, own):
    upper = jnp.concatenate([scol[...]] * (NS // 128), axis=1) == 1.0
    low = ylow[ROWS]
    own[...] = jnp.where(upper, times(low, coupling[0]), times(low, coupling[1]))


def own_root_first(ylow, cost_top, coupling_far, own_root, coupling_root, sem):
    copies = [
        pltpu.make_async_copy(coupling_far.at[0, cols], coupling_root.at[cols], sem.at[i])
        for i, cols in enumerate(parts())
    ]
    for copy in copies:
        copy.start()
    total = -cost_top[...]
    for copy, cols in zip(copies, parts()):
        copy.wait()
        total = total + times(ylow[:ROOTS, cols], coupling_root[cols])
    own_root[...] = total


def own_first(ylow, scol, coupling_far, own, coupling, sem):
    copies = [
        pltpu.make_async_copy(coupling_far.at[pl.ds(1, 2), cols], coupling.at[:, cols], sem.at[i])
        for i, cols in enumerate(parts())
    ]
    for copy in copies:
        copy.start()
    first_total, second_total = None, None
    for copy, cols in zip(copies, parts()):
        copy.wait()
        low = ylow[ROWS, cols]
        one, two = times(low, coupling[0, cols]), times(low, coupling[1, cols])
        first_total = one if first_total is None else first_total + one
        second_total = two if second_total is None else second_total + two
    upper = jnp.concatenate([scol[...]] * (NS // 128), axis=1) == 1.0
    own[...] = jnp.where(upper, first_total, second_total)


def join(blocks, swapped, held):
    for k, block in enumerate(blocks):
        held[k * CAP_NODE : (k + 1) * CAP_NODE] = block[:CAP_NODE]
    held[256:] = swapped[...]


def primal_first(g0, g1, g2, g3, swapped, own, x, cost, rates, wrow, wcol, x_next, extra, *refs):
    *sends, held = refs
    join((g0, g1, g2, g3), swapped, held)
    mark = held[:, NS:].astype(F32)
    row = mark.T[:8]
    wcol[...] = mark
    wrow[...] = row
    primal_child(held[:, :NS], own, x[ROWS], cost, rates, mark, row, x_next, extra, sends)


def primal_second(g0, g1, g2, g3, swapped, own, x, cost, rates, wrow, wcol, x_next, extra, *refs):
    *sends, held = refs
    join((g0, g1, g2, g3), swapped, held)
    primal_child(held[...], own, x[...], cost, rates, wcol[...], wrow[...], x_next, extra, sends)


def primal_child(got, own, x_old, cost, rates, mark, row, x_next, extra, sends):
    tau = rates[:1, :1]
    adjoint = own[...] + times(hot_rows(row[:1] - 1.0, CHILD), got)
    new = jnp.maximum(x_old - tau * (cost[ROWS] - adjoint), 0.0)
    low = (2.0 * new - x_old).astype(BF16)
    x_next[...] = new
    extra[...] = low
    reply = times(hot_lanes(mark - 1.0, CHILD), low).astype(BF16)
    for k, send in enumerate(sends):
        send[:CAP_NODE] = reply[k * CAP_NODE : (k + 1) * CAP_NODE]
        send[CAP_NODE:] = reply[256 + k * CAP_NODE : 256 + (k + 1) * CAP_NODE]


def rooted(j):
    return slice(j * ROOTS, (j + 1) * ROOTS)


def summed(blocks, j):
    return sum(block[rooted((j + k) & 3)].astype(F32) for k, block in enumerate(blocks))


def root_first(g0, g1, g2, g3, own, x, rates, x_next, extra):
    blocks = (g0, g1, g2, g3)
    tau = rates[:1, :1]
    for j in range(4):
        slope = summed(blocks, j)
        if j == 0:
            x_old = x[...]
            slope = slope + own[...]
        else:
            x_old = blocks[(-j) & 3][rooted(4)].astype(F32)
        new = jnp.maximum(x_old + tau * slope, 0.0)
        x_next[rooted(j)] = new
        extra[rooted(j)] = (2.0 * new - x_old).astype(BF16)


def root_second(g0, g1, g2, g3, own, x, rates, extra, x_next):
    blocks = (g0, g1, g2, g3)
    tau = rates[:1, :1]
    for j in range(4):
        slope = summed(blocks, j)
        if j == 0:
            slope = slope + own[...]
        x_old = x[rooted(j)]
        new = jnp.maximum(x_old + tau * slope, 0.0)
        extra[rooted(j)] = (2.0 * new - x_old).astype(BF16)
        if j == 0:
            x_next[...] = new


def averages(x_start, x_root, x_root_next, x_child, x_child_next, average, move):
    roots = (x_root[:ROOTS] + x_root_next[...]) * 0.5
    children = (x_child[...] + x_child_next[...]) * 0.5
    average[:ROOTS] = roots
    average[ROWS] = children
    gap_roots = roots - x_start[:ROOTS]
    gap_children = children - x_start[ROWS]
    total = jnp.sum(gap_roots * gap_roots) + jnp.sum(gap_children * gap_children)
    move[...] = jnp.full((8, 128), total, F32)


def own_image(
    last, extra_child, extra_root, scol, coupling_root, coupling, y, right, rates, cost_top, base, *refs
):
    sigma = rates[1:2, :1]
    upper = jnp.concatenate([scol[...]] * (TILE // 128), axis=1) == 1.0
    child = extra_child[...]
    root = extra_root[:ROOTS]
    total = -cost_top[...]
    for cols in parts():
        image = jnp.where(
            upper, times_t(child, coupling[0, cols]), times_t(child, coupling[1, cols])
        )
        weights = coupling_root[cols]
        base_root = y[:ROOTS, cols] + sigma * (right[:ROOTS, cols] - times_t(root, weights))
        base[:ROOTS, cols] = base_root
        if not last:
            total = total + times(jnp.maximum(base_root, 0.0).astype(BF16), weights)
        base[ROWS, cols] = y[ROWS, cols] + sigma * (right[ROWS, cols] - image)
    if not last:
        (own_root,) = refs
        own_root[...] = total


def from_leaf(blocks, lback):
    hot = hot_lanes(lback[...], SLOTS)
    rows = None
    for k, block in enumerate(blocks):
        term = times(hot[:, k * 128 : (k + 1) * 128], block[...])
        rows = term if rows is None else rows + term
    return rows.astype(BF16)


def dual_leaf(last, b0, b1, b2, b3, lback, linking, base, rates, *refs):
    if last:
        (later,) = refs
    else:
        lsend, later, *outs = refs
    rows = from_leaf((b0, b1, b2, b3), lback)
    sigma = rates[1:2, :1]
    total = None
    for cols in parts():
        weights = linking[0, cols]
        new = base[ROWS, cols] - sigma * times_t(rows, weights)
        later[:, cols] = new
        if not last:
            product = times(jnp.maximum(new, 0.0).astype(BF16), weights)
            total = product if total is None else total + product
    if not last:
        spread(lsend[...], total.astype(BF16), outs)


def from_node(blocks, swapped, nback, held):
    join(blocks, swapped, held)
    return times(hot_lanes(nback[...], SLOTS), held[...]).astype(BF16)


def dual_node(g0, g1, g2, g3, swapped, nback, linking, base, later, rates, nsend, *refs):
    y_next, ylow, *outs, held = refs
    rows = from_node((g0, g1, g2, g3), swapped, nback, held)
    sigma = rates[1:2, :1]
    total = None
    for cols in parts():
        weights = linking[1, cols]
        new_root = jnp.maximum(base[:ROOTS, cols], 0.0)
        new = jnp.maximum(later[:, cols] - sigma * times_t(rows, weights), 0.0)
        low = new.astype(BF16)
        y_next[:ROOTS, cols] = new_root
        y_next[ROWS, cols] = new
        ylow[:ROOTS, cols] = new_root.astype(BF16)
        ylow[ROWS, cols] = low
        product = times(low, weights)
        total = product if total is None else total + product
    spread(nsend[...], total.astype(BF16), outs)


def dual_last(
    g0, g1, g2, g3, swapped, nback, linking, base, later, rates, y, y_start, primal_move, average, load, held
):
    rows = from_node((g0, g1, g2, g3), swapped, nback, held)
    sigma = rates[1:2, :1]
    move = jnp.zeros((1, TILE), F32)
    for cols in parts():
        new_root = jnp.maximum(base[:ROOTS, cols], 0.0)
        new = jnp.maximum(later[:, cols] - sigma * times_t(rows, linking[1, cols]), 0.0)
        mean_root = (y[:ROOTS, cols] + new_root) * 0.5
        mean = (y[ROWS, cols] + new) * 0.5
        average[:ROOTS, cols] = mean_root
        average[ROWS, cols] = mean
        gap_root = mean_root - y_start[:ROOTS, cols]
        gap = mean - y_start[ROWS, cols]
        move = move + jnp.sum(gap_root * gap_root, axis=0, keepdims=True)
        move = move + jnp.sum(gap * gap, axis=0, keepdims=True)
    lane = lax.broadcasted_iota(jnp.int32, load.shape, 2)
    load[...] = jnp.where(lane == 0, primal_move[:1], jnp.sum(move))


def pairs_of(place):
    pairs = []
    for i in range(N_LEAF * N_NODE):
        y, z, x, core = place(i >> 5, (i >> 3) & 3, (i >> 1) & 3, i & 1)
        pairs.append((i, ((y & 3) * 4 + (z & 3)) * N_NODE + (x & 3) * 2 + core))
    return ("leaf", "node"), pairs


def outer_ring(k):
    return pairs_of(lambda y, z, x, c: (y, z + k, x, c) if c else (y + k, z, x, c))


def inner_ring(k):
    return pairs_of(lambda y, z, x, c: (y + k, z, x, c) if c else (y, z + k, x, c))


def ring_x(k):
    return pairs_of(lambda y, z, x, c: (y, z, x + k, c))


def sibling(array):
    return lax.ppermute(array, *pairs_of(lambda y, z, x, c: (y, z, x, 1 - c)))


def shifted(blocks, ring, sign=1):
    got = {0: blocks[0]}
    for k in (2, 1, 3):
        got[k] = lax.ppermute(blocks[k], *ring((sign * k) % 4))
    return [got[k] for k in range(4)]


def swap_node(blocks, sign, before):
    got = shifted(blocks, ring_x, sign)
    halves = jnp.concatenate([block[CAP_NODE:] for block in got], axis=0)
    halves, before = lax.optimization_barrier((halves, before))
    return got + [sibling(halves)], before


def ring_gather(rows, ring):
    one = lax.ppermute(rows, *ring(1))
    three = lax.ppermute(rows, *ring(3))
    return [rows, one, lax.ppermute(one, *ring(1)), three]


def sum_leaf(blocks, own, state, before):
    got, before = lax.optimization_barrier((shifted(blocks, outer_ring), before))
    got = [block.astype(F32) for block in got]
    total = ((got[0] + got[1]) + got[2]) + got[3]
    sent = jnp.concatenate([total[:ROOTS] + own, total[ROOTS:]], axis=0).astype(BF16)
    if state is not None:
        sent = jnp.concatenate([sent, state], axis=0)
    return [total.astype(BF16)] + shifted([sent] * 4, inner_ring)[1:], before


def part_of(kernel, flag):
    def run(*refs):
        kernel(flag, *refs)

    return run


def shards(x_start, y_start, cost_vec, right_side, omega, coupling, linking, parent, section):
    unit = 2 * CHILD * NS * NC
    code = (section * 65536 + parent)[ROOTS:].reshape(1, CHILD)
    rates = jnp.broadcast_to(jnp.stack([STEP / omega[0], STEP * omega[0]])[:, None], (2, 128))
    field = ((NODES, NC), F32)
    field_low = ((NODES, NC), BF16)
    states = ((NODES, NS), F32)
    block = ((128, NS), BF16)
    block_mark = ((128, NS + 128), BF16)
    kids = ((CHILD, NS), F32)
    kids_low = ((CHILD, NS), BF16)
    kids_field = ((CHILD, NC), F32)
    tops = ((ROOTS, NS), F32)
    plane = ((4 * ROOTS, NS), F32)
    row = ((1, CHILD), F32)
    col = ((CHILD, 128), F32)
    held = [pltpu.VMEM((SLOTS, NS), BF16)]

    *sent, y_start, linking, ylow, nsend, nback, lsend, lback, scol, x_top, cost_top, state = call(
        first,
        [block_mark] * 4 + [block] * 4
        + [field, ((2, NC, NS), BF16), field_low, row, col, row, col, col, tops, tops, ((ROOTS, NS), BF16)],
        [code, y_start, linking, x_start, cost_vec],
        2 * unit,
        [pltpu.SemaphoreType.DMA((3 * NC // TILE + 2,))],
        (1, 2, 3, 4),
    )
    chunk_sems = [pltpu.SemaphoreType.DMA((NC // TILE,))]
    own_root, coupling_root = call(
        own_root_first, [tops, ((NC, NS), BF16)], [ylow, cost_top, coupling], unit // 8, chunk_sems, (2,)
    )
    own, coupling = call(
        own_first, [kids, ((2, NC, NS), BF16)], [ylow, scol, coupling], 2 * unit, chunk_sems, (2,)
    )
    got_leaf, _ = sum_leaf(sent[4:], own_root, state, own_root)
    got_node, (got_leaf, own) = swap_node(sent[:4], 1, (got_leaf, own))

    x_root, extra_root = call(
        root_first,
        [plane, block],
        got_leaf + [own_root, x_top, rates],
        0,
    )
    own, extra_root = lax.optimization_barrier((own, extra_root))
    wrow, wcol, x_child, extra_child, *out_node = call(
        primal_first,
        [((8, SLOTS), F32), ((SLOTS, 128), F32), kids, kids_low] + [block] * 4,
        got_node + [own, x_start, cost_vec, rates],
        unit // 4,
        [pltpu.VMEM((SLOTS, NS + 128), BF16)],
    )
    base, own_root = call(
        part_of(own_image, False),
        [field, tops],
        [
            extra_child, extra_root, scol, coupling_root, coupling, y_start, right_side, rates, cost_top
        ],
        2 * unit,
    )
    back_leaf = ring_gather(extra_root, outer_ring)
    back_node, (back_leaf, base) = swap_node(out_node, -1, (back_leaf, base))
    later, *out_leaf = call(
        part_of(dual_leaf, False),
        [kids_field] + [block] * 4,
        back_leaf + [lback, linking, base, rates, lsend],
        2 * unit,
    )
    y_next, ylow, *out_node = call(
        dual_node,
        [field, field_low] + [block] * 4,
        back_node + [nback, linking, base, later, rates, nsend],
        2 * unit,
        held,
    )
    got_leaf, ylow = sum_leaf(out_leaf, own_root, None, ylow)
    (own,) = call(own_adjoint, [kids], [ylow, scol, coupling], 2 * unit)
    got_node, (got_leaf, own) = swap_node(out_node, 1, (got_leaf, own))

    extra_root, x_top = call(
        root_second,
        [block, tops],
        got_leaf + [own_root, x_root, rates],
        0,
    )
    own, extra_root = lax.optimization_barrier((own, extra_root))
    x_child_next, extra_child, *out_node = call(
        primal_second,
        [kids, kids_low] + [block] * 4,
        got_node + [own, x_child, cost_vec, rates, wrow, wcol],
        unit // 4,
        held,
    )
    x_average, primal_move = call(
        averages,
        [states, ((8, 128), F32)],
        [x_start, x_root, x_top, x_child, x_child_next],
        0,
    )
    (base,) = call(
        part_of(own_image, True),
        [field],
        [extra_child, extra_root, scol, coupling_root, coupling, y_next, right_side, rates, cost_top],
        2 * unit,
    )
    back_leaf = ring_gather(extra_root, outer_ring)
    back_node, (back_leaf, base) = swap_node(out_node, -1, (back_leaf, base))
    (later,) = call(
        part_of(dual_leaf, True), [kids_field], back_leaf + [lback, linking, base, rates], unit
    )
    y_average, load = call(
        dual_last,
        [field, ((N_LEAF * N_NODE, 1, 128), F32)],
        back_node + [nback, linking, base, later, rates, y_next, y_start, primal_move],
        unit,
        held,
    )
    moves = lax.all_to_all(load, ("leaf", "node"), split_axis=0, concat_axis=0, tiled=True)
    moves = jnp.sum(moves[:, 0, :2], axis=0)
    omega_new = jnp.sqrt((moves[1:] + 1e-06) / (moves[:1] + 1e-06))
    return (x_average, y_average, omega_new)


def solution(mesh):
    both = P(("leaf", "node"), None)
    flat = P(("leaf", "node"))
    return jax.shard_map(
        shards,
        mesh=mesh,
        in_specs=(both, both, both, both, P(), P(), P(), flat, flat),
        out_specs=(both, both, P()),
        check_vma=False,
    )
```

```python
import jax
import jax.numpy as jnp
from jax import lax
from jax.experimental import pallas as pl
from jax.experimental.pallas import tpu as pltpu
from jax.sharding import PartitionSpec as P

NS = 512
NC = 2048
ROOTS = 32
CHILD = 256
NODES = 288
N_LEAF = 16
N_NODE = 8
CAP_NODE = 64
SLOTS = 512
TILE = 512
VMEM_LIMIT = 24 * 2**20
STEP = 0.3
F32 = jnp.float32
BF16 = jnp.bfloat16
ROWS = slice(ROOTS, NODES)


def times(a, b):
    return lax.dot_general(a, b, (((1,), (0,)), ((), ())), preferred_element_type=F32)


def times_t(a, b):
    return lax.dot_general(a, b, (((1,), (1,)), ((), ())), preferred_element_type=F32)


def hot_rows(code, count):
    places = lax.broadcasted_iota(jnp.int32, (count, code.shape[1]), 0).astype(F32)
    return jnp.where(places == code, 1.0, 0.0).astype(BF16)


def hot_lanes(code, count):
    wide = jnp.concatenate([code] * (count // 128), axis=1)
    places = lax.broadcasted_iota(jnp.int32, wide.shape, 1).astype(F32)
    return jnp.where(places == wide, 1.0, 0.0).astype(BF16)


def to_lanes(row):
    return jnp.broadcast_to(row, (128, row.shape[1])).T


def call(kernel, outs, arrays, flops, scratch=(), far=()):
    out_shapes = [jax.ShapeDtypeStruct(shape, dtype) for shape, dtype in outs]
    moved = sum(a.size * a.dtype.itemsize for a in list(arrays) + out_shapes)
    out_shapes = [pltpu.VMEM(shape, dtype) for shape, dtype in outs]
    arrays = [
        pltpu.with_memory_space_constraint(a, pltpu.HBM) if i in far else a for i, a in enumerate(arrays)
    ]
    return pl.pallas_call(
        kernel,
        out_shape=out_shapes,
        in_specs=[pl.BlockSpec(memory_space=pl.ANY if i in far else pltpu.VMEM) for i in range(len(arrays))],
        out_specs=[pl.BlockSpec(memory_space=pltpu.VMEM)] * len(outs),
        scratch_shapes=list(scratch),
        compiler_params=pltpu.CompilerParams(vmem_limit_bytes=VMEM_LIMIT),
        cost_estimate=pl.CostEstimate(flops=flops, bytes_accessed=moved // 8, transcendentals=0),
    )(*arrays)


def parts():
    return [slice(i * TILE, (i + 1) * TILE) for i in range(NC // TILE)]


def first(parent_far, section_far, y_far, linking_far, x_far, cost_far, *refs):
    *outs, y, linking, ylow, nsend, nback, lsend, lback, scol, x_top, cost_top, state, parent_of, section_of, sem = refs
    chunks = parts()
    copies = []
    for cols in chunks:
        copies.append((y_far.at[:, cols], y.at[:, cols]))
        copies.append((linking_far.at[1, cols], linking.at[1, cols]))
    for cols in chunks:
        copies.append((linking_far.at[0, cols], linking.at[0, cols]))
    copies += [(x_far.at[:ROOTS], x_top), (cost_far.at[:ROOTS], cost_top)]
    copies = [(parent_far, parent_of), (section_far, section_of)] + copies
    copies = [pltpu.make_async_copy(a, b, sem.at[i]) for i, (a, b) in enumerate(copies)]
    for copy in copies:
        copy.start()
    copies[0].wait()
    copies[1].wait()
    copies = copies[2:]
    upper = section_of[...].reshape(1, NODES)[:, ROWS] == 1
    parent = parent_of[...].reshape(1, NODES)[:, ROWS]
    here = lax.axis_index("leaf") * N_NODE + lax.axis_index("node")
    owner = ((parent.astype(F32) + 0.5) * (1.0 / NODES)).astype(jnp.int32)
    local = parent - owner * NODES
    ry = ((owner >> 5) - (here >> 5)) & 3
    rz = ((owner >> 3) - (here >> 3)) & 3
    rx = ((owner >> 1) - (here >> 1)) & 3
    rc = (owner ^ here) & 1
    odd = (here & 1) == 1
    outer = jnp.where(odd, rz, ry)
    inner = jnp.where(odd, ry, rz)
    lrow = jnp.where(upper, outer * 128 + inner * ROOTS + local, -1).astype(F32)
    lend = jnp.where(upper, ((-outer) & 3) * 128 + inner * ROOTS + local, -1).astype(F32)
    peer = rx * 2 + rc
    peers = lax.broadcasted_iota(jnp.int32, (N_NODE, CHILD), 0)
    member = jnp.where((peers == peer) & jnp.logical_not(upper), 1.0, 0.0)
    before = lax.broadcasted_iota(jnp.int32, (CHILD, CHILD), 0) <= lax.broadcasted_iota(
        jnp.int32, (CHILD, CHILD), 1
    )
    counts = times(member.astype(BF16), jnp.where(before, 1.0, 0.0).astype(BF16))
    rank = jnp.sum(member * counts, axis=0, keepdims=True) - 1.0
    nrow = jnp.where(upper, -1.0, (peer * CAP_NODE).astype(F32) + rank)
    nend = jnp.where(upper, -1.0, (rc * 256 + rx * CAP_NODE).astype(F32) + rank)
    mark = jnp.where(upper, 0, local - (ROOTS - 1)).astype(F32)
    nsend[...] = nrow
    lsend[...] = lrow
    nback[...] = to_lanes(nend)
    lback[...] = to_lanes(lend)
    scol[...] = to_lanes(jnp.where(upper, 1.0, 2.0))
    total = None
    for i, cols in enumerate(chunks):
        copies[2 * i].wait()
        copies[2 * i + 1].wait()
        low = y[:, cols].astype(BF16)
        ylow[:, cols] = low
        term = times(low[ROWS], linking[1, cols])
        total = term if total is None else total + term
    load = jnp.concatenate([total.astype(BF16), to_lanes(mark).astype(BF16)], axis=1)
    spread(nrow, load, outs[:4])
    total = None
    for i, cols in enumerate(chunks):
        copies[2 * len(chunks) + i].wait()
        term = times(ylow[ROWS, cols], linking[0, cols])
        total = term if total is None else total + term
    spread(lrow, total.astype(BF16), outs[4:])
    copies[-2].wait()
    copies[-1].wait()
    state[...] = x_top[...].astype(BF16)


def spread(row, load, outs):
    hot = hot_rows(row, SLOTS)
    for k, out in enumerate(outs):
        out[...] = times(hot[k * 128 : (k + 1) * 128], load).astype(BF16)


def own_adjoint(ylow, scol, coupling, own):
    upper = jnp.concatenate([scol[...]] * (NS // 128), axis=1) == 1.0
    low = ylow[ROWS]
    own[...] = jnp.where(upper, times(low, coupling[1]), times(low, coupling[2]))


def own_root_first(ylow, cost_top, coupling, own_root):
    own_root[...] = times(ylow[:ROOTS], coupling[0]) - cost_top[...]


def join(blocks, swapped, held):
    for k, block in enumerate(blocks):
        held[k * CAP_NODE : (k + 1) * CAP_NODE] = block[:CAP_NODE]
    held[256:] = swapped[...]


def primal_first(g0, g1, g2, g3, swapped, own, x, cost, rates, wrow, wcol, x_next, extra, *refs):
    *sends, held = refs
    join((g0, g1, g2, g3), swapped, held)
    mark = held[:, NS:].astype(F32)
    row = mark.T[:8]
    wcol[...] = mark
    wrow[...] = row
    primal_child(held[:, :NS], own, x[ROWS], cost, rates, mark, row, x_next, extra, sends)


def primal_second(g0, g1, g2, g3, swapped, own, x, cost, rates, wrow, wcol, x_next, extra, *refs):
    *sends, held = refs
    join((g0, g1, g2, g3), swapped, held)
    primal_child(held[...], own, x[...], cost, rates, wcol[...], wrow[...], x_next, extra, sends)


def primal_child(got, own, x_old, cost, rates, mark, row, x_next, extra, sends):
    tau = rates[:1, :1]
    adjoint = own[...] + times(hot_rows(row[:1] - 1.0, CHILD), got)
    new = jnp.maximum(x_old - tau * (cost[ROWS] - adjoint), 0.0)
    low = (2.0 * new - x_old).astype(BF16)
    x_next[...] = new
    extra[...] = low
    reply = times(hot_lanes(mark - 1.0, CHILD), low).astype(BF16)
    for k, send in enumerate(sends):
        send[:CAP_NODE] = reply[k * CAP_NODE : (k + 1) * CAP_NODE]
        send[CAP_NODE:] = reply[256 + k * CAP_NODE : 256 + (k + 1) * CAP_NODE]


def rooted(j):
    return slice(j * ROOTS, (j + 1) * ROOTS)


def summed(blocks, j):
    return sum(block[rooted((j + k) & 3)].astype(F32) for k, block in enumerate(blocks))


def root_first(g0, g1, g2, g3, own, x, rates, x_next, extra):
    blocks = (g0, g1, g2, g3)
    tau = rates[:1, :1]
    for j in range(4):
        slope = summed(blocks, j)
        if j == 0:
            x_old = x[...]
            slope = slope + own[...]
        else:
            x_old = blocks[(-j) & 3][rooted(4)].astype(F32)
        new = jnp.maximum(x_old + tau * slope, 0.0)
        x_next[rooted(j)] = new
        extra[rooted(j)] = (2.0 * new - x_old).astype(BF16)


def root_second(g0, g1, g2, g3, own, x, rates, extra, x_next):
    blocks = (g0, g1, g2, g3)
    tau = rates[:1, :1]
    for j in range(4):
        slope = summed(blocks, j)
        if j == 0:
            slope = slope + own[...]
        x_old = x[rooted(j)]
        new = jnp.maximum(x_old + tau * slope, 0.0)
        extra[rooted(j)] = (2.0 * new - x_old).astype(BF16)
        if j == 0:
            x_next[...] = new


def averages(x_start, x_root, x_root_next, x_child, x_child_next, average, move):
    roots = (x_root[:ROOTS] + x_root_next[...]) * 0.5
    children = (x_child[...] + x_child_next[...]) * 0.5
    average[:ROOTS] = roots
    average[ROWS] = children
    gap_roots = roots - x_start[:ROOTS]
    gap_children = children - x_start[ROWS]
    total = jnp.sum(gap_roots * gap_roots) + jnp.sum(gap_children * gap_children)
    move[...] = jnp.full((8, 128), total, F32)


def own_image(
    last, extra_child, extra_root, scol, coupling, y, right, rates, cost_top, base, *refs
):
    sigma = rates[1:2, :1]
    upper = jnp.concatenate([scol[...]] * (TILE // 128), axis=1) == 1.0
    child = extra_child[...]
    root = extra_root[:ROOTS]
    total = -cost_top[...]
    for cols in parts():
        image = jnp.where(
            upper, times_t(child, coupling[1, cols]), times_t(child, coupling[2, cols])
        )
        weights = coupling[0, cols]
        base_root = y[:ROOTS, cols] + sigma * (right[:ROOTS, cols] - times_t(root, weights))
        base[:ROOTS, cols] = base_root
        if not last:
            total = total + times(jnp.maximum(base_root, 0.0).astype(BF16), weights)
        base[ROWS, cols] = y[ROWS, cols] + sigma * (right[ROWS, cols] - image)
    if not last:
        (own_root,) = refs
        own_root[...] = total


def from_leaf(blocks, lback):
    hot = hot_lanes(lback[...], SLOTS)
    rows = None
    for k, block in enumerate(blocks):
        term = times(hot[:, k * 128 : (k + 1) * 128], block[...])
        rows = term if rows is None else rows + term
    return rows.astype(BF16)


def dual_leaf(last, b0, b1, b2, b3, lback, linking, base, rates, *refs):
    if last:
        (later,) = refs
    else:
        lsend, later, *outs = refs
    rows = from_leaf((b0, b1, b2, b3), lback)
    sigma = rates[1:2, :1]
    total = None
    for cols in parts():
        weights = linking[0, cols]
        new = base[ROWS, cols] - sigma * times_t(rows, weights)
        later[:, cols] = new
        if not last:
            product = times(jnp.maximum(new, 0.0).astype(BF16), weights)
            total = product if total is None else total + product
    if not last:
        spread(lsend[...], total.astype(BF16), outs)


def from_node(blocks, swapped, nback, held):
    join(blocks, swapped, held)
    return times(hot_lanes(nback[...], SLOTS), held[...]).astype(BF16)


def dual_node(g0, g1, g2, g3, swapped, nback, linking, base, later, rates, nsend, *refs):
    y_next, ylow, *outs, held = refs
    rows = from_node((g0, g1, g2, g3), swapped, nback, held)
    sigma = rates[1:2, :1]
    total = None
    for cols in parts():
        weights = linking[1, cols]
        new_root = jnp.maximum(base[:ROOTS, cols], 0.0)
        new = jnp.maximum(later[:, cols] - sigma * times_t(rows, weights), 0.0)
        low = new.astype(BF16)
        y_next[:ROOTS, cols] = new_root
        y_next[ROWS, cols] = new
        ylow[:ROOTS, cols] = new_root.astype(BF16)
        ylow[ROWS, cols] = low
        product = times(low, weights)
        total = product if total is None else total + product
    spread(nsend[...], total.astype(BF16), outs)


def dual_last(
    g0, g1, g2, g3, swapped, nback, linking, base, later, rates, y, y_start, primal_move, average, load, held
):
    rows = from_node((g0, g1, g2, g3), swapped, nback, held)
    sigma = rates[1:2, :1]
    move = jnp.zeros((1, TILE), F32)
    for cols in parts():
        new_root = jnp.maximum(base[:ROOTS, cols], 0.0)
        new = jnp.maximum(later[:, cols] - sigma * times_t(rows, linking[1, cols]), 0.0)
        mean_root = (y[:ROOTS, cols] + new_root) * 0.5
        mean = (y[ROWS, cols] + new) * 0.5
        average[:ROOTS, cols] = mean_root
        average[ROWS, cols] = mean
        gap_root = mean_root - y_start[:ROOTS, cols]
        gap = mean - y_start[ROWS, cols]
        move = move + jnp.sum(gap_root * gap_root, axis=0, keepdims=True)
        move = move + jnp.sum(gap * gap, axis=0, keepdims=True)
    lane = lax.broadcasted_iota(jnp.int32, load.shape, 2)
    load[...] = jnp.where(lane == 0, primal_move[:1], jnp.sum(move))


def pairs_of(place):
    pairs = []
    for i in range(N_LEAF * N_NODE):
        y, z, x, core = place(i >> 5, (i >> 3) & 3, (i >> 1) & 3, i & 1)
        pairs.append((i, ((y & 3) * 4 + (z & 3)) * N_NODE + (x & 3) * 2 + core))
    return ("leaf", "node"), pairs


def outer_ring(k):
    return pairs_of(lambda y, z, x, c: (y, z + k, x, c) if c else (y + k, z, x, c))


def inner_ring(k):
    return pairs_of(lambda y, z, x, c: (y + k, z, x, c) if c else (y, z + k, x, c))


def ring_x(k):
    return pairs_of(lambda y, z, x, c: (y, z, x + k, c))


def sibling(array):
    return lax.ppermute(array, *pairs_of(lambda y, z, x, c: (y, z, x, 1 - c)))


def shifted(blocks, ring, sign=1):
    got = {0: blocks[0]}
    for k in (2, 1, 3):
        got[k] = lax.ppermute(blocks[k], *ring((sign * k) % 4))
    return [got[k] for k in range(4)]


def swap_node(blocks, sign, before):
    got = shifted(blocks, ring_x, sign)
    halves = jnp.concatenate([block[CAP_NODE:] for block in got], axis=0)
    halves, before = lax.optimization_barrier((halves, before))
    return got + [sibling(halves)], before


def ring_gather(rows, ring):
    one = lax.ppermute(rows, *ring(1))
    three = lax.ppermute(rows, *ring(3))
    return [rows, one, lax.ppermute(one, *ring(1)), three]


def sum_leaf(blocks, own, state, before):
    got, before = lax.optimization_barrier((shifted(blocks, outer_ring), before))
    got = [block.astype(F32) for block in got]
    total = ((got[0] + got[1]) + got[2]) + got[3]
    sent = jnp.concatenate([total[:ROOTS] + own, total[ROOTS:]], axis=0).astype(BF16)
    if state is not None:
        sent = jnp.concatenate([sent, state], axis=0)
    return [total.astype(BF16)] + shifted([sent] * 4, inner_ring)[1:], before


def part_of(kernel, flag):
    def run(*refs):
        kernel(flag, *refs)

    return run


def shards(x_start, y_start, cost_vec, right_side, omega, coupling, linking, parent, section):
    unit = 2 * CHILD * NS * NC
    rates = jnp.broadcast_to(jnp.stack([STEP / omega[0], STEP * omega[0]])[:, None], (2, 128))
    field = ((NODES, NC), F32)
    field_low = ((NODES, NC), BF16)
    states = ((NODES, NS), F32)
    block = ((128, NS), BF16)
    block_mark = ((128, NS + 128), BF16)
    kids = ((CHILD, NS), F32)
    kids_low = ((CHILD, NS), BF16)
    kids_field = ((CHILD, NC), F32)
    tops = ((ROOTS, NS), F32)
    plane = ((4 * ROOTS, NS), F32)
    row = ((1, CHILD), F32)
    col = ((CHILD, 128), F32)
    held = [pltpu.VMEM((SLOTS, NS), BF16)]

    *sent, y_start, linking, ylow, nsend, nback, lsend, lback, scol, x_top, cost_top, state = call(
        first,
        [block_mark] * 4 + [block] * 4
        + [field, ((2, NC, NS), BF16), field_low, row, col, row, col, col, tops, tops, ((ROOTS, NS), BF16)],
        [parent, section, y_start, linking, x_start, cost_vec],
        2 * unit,
        [
            pltpu.VMEM((NODES,), jnp.int32),
            pltpu.VMEM((NODES,), jnp.int32),
            pltpu.SemaphoreType.DMA((3 * NC // TILE + 4,)),
        ],
        (0, 1, 2, 3, 4, 5),
    )
    (own_root,) = call(own_root_first, [tops], [ylow, cost_top, coupling], unit // 8)
    (own,) = call(own_adjoint, [kids], [ylow, scol, coupling], 2 * unit)
    got_leaf, _ = sum_leaf(sent[4:], own_root, state, own_root)
    got_node, (got_leaf, own) = swap_node(sent[:4], 1, (got_leaf, own))

    x_root, extra_root = call(
        root_first,
        [plane, block],
        got_leaf + [own_root, x_top, rates],
        0,
    )
    own, extra_root = lax.optimization_barrier((own, extra_root))
    wrow, wcol, x_child, extra_child, *out_node = call(
        primal_first,
        [((8, SLOTS), F32), ((SLOTS, 128), F32), kids, kids_low] + [block] * 4,
        got_node + [own, x_start, cost_vec, rates],
        unit // 4,
        [pltpu.VMEM((SLOTS, NS + 128), BF16)],
    )
    base, own_root = call(
        part_of(own_image, False),
        [field, tops],
        [
            extra_child, extra_root, scol, coupling, y_start, right_side, rates, cost_top
        ],
        2 * unit,
    )
    back_leaf = ring_gather(extra_root, outer_ring)
    back_node, (back_leaf, base) = swap_node(out_node, -1, (back_leaf, base))
    later, *out_leaf = call(
        part_of(dual_leaf, False),
        [kids_field] + [block] * 4,
        back_leaf + [lback, linking, base, rates, lsend],
        2 * unit,
    )
    y_next, ylow, *out_node = call(
        dual_node,
        [field, field_low] + [block] * 4,
        back_node + [nback, linking, base, later, rates, nsend],
        2 * unit,
        held,
    )
    got_leaf, ylow = sum_leaf(out_leaf, own_root, None, ylow)
    (own,) = call(own_adjoint, [kids], [ylow, scol, coupling], 2 * unit)
    got_node, (got_leaf, own) = swap_node(out_node, 1, (got_leaf, own))

    extra_root, x_top = call(
        root_second,
        [block, tops],
        got_leaf + [own_root, x_root, rates],
        0,
    )
    own, extra_root = lax.optimization_barrier((own, extra_root))
    x_child_next, extra_child, *out_node = call(
        primal_second,
        [kids, kids_low] + [block] * 4,
        got_node + [own, x_child, cost_vec, rates, wrow, wcol],
        unit // 4,
        held,
    )
    x_average, primal_move = call(
        averages,
        [states, ((8, 128), F32)],
        [x_start, x_root, x_top, x_child, x_child_next],
        0,
    )
    (base,) = call(
        part_of(own_image, True),
        [field],
        [extra_child, extra_root, scol, coupling, y_next, right_side, rates, cost_top],
        2 * unit,
    )
    back_leaf = ring_gather(extra_root, outer_ring)
    back_node, (back_leaf, base) = swap_node(out_node, -1, (back_leaf, base))
    (later,) = call(
        part_of(dual_leaf, True), [kids_field], back_leaf + [lback, linking, base, rates], unit
    )
    y_average, load = call(
        dual_last,
        [field, ((N_LEAF * N_NODE, 1, 128), F32)],
        back_node + [nback, linking, base, later, rates, y_next, y_start, primal_move],
        unit,
        held,
    )
    moves = lax.all_to_all(load, ("leaf", "node"), split_axis=0, concat_axis=0, tiled=True)
    moves = jnp.sum(moves[:, 0, :2], axis=0)
    omega_new = jnp.sqrt((moves[1:] + 1e-06) / (moves[:1] + 1e-06))
    return (x_average, y_average, omega_new)


def solution(mesh):
    both = P(("leaf", "node"), None)
    flat = P(("leaf", "node"))
    return jax.shard_map(
        shards,
        mesh=mesh,
        in_specs=(both, both, both, both, P(), P(), P(), flat, flat),
        out_specs=(both, both, P()),
        check_vma=False,
    )
```

```python
import jax
import jax.numpy as jnp
from jax import lax
from jax.experimental import pallas as pl
from jax.experimental.pallas import tpu as pltpu
from jax.sharding import PartitionSpec as P

NS = 512
NC = 2048
ROOTS = 32
CHILD = 256
NODES = 288
N_LEAF = 16
N_NODE = 8
CAP_NODE = 64
SLOTS = 512
TILE = 512
VMEM_LIMIT = 24 * 2**20
STEP = 0.3
F32 = jnp.float32
BF16 = jnp.bfloat16
ROWS = slice(ROOTS, NODES)


def times(a, b):
    return lax.dot_general(a, b, (((1,), (0,)), ((), ())), preferred_element_type=F32)


def times_t(a, b):
    return lax.dot_general(a, b, (((1,), (1,)), ((), ())), preferred_element_type=F32)


def hot_rows(code, count):
    places = lax.broadcasted_iota(jnp.int32, (count, code.shape[1]), 0).astype(F32)
    return jnp.where(places == code, 1.0, 0.0).astype(BF16)


def hot_lanes(code, count):
    wide = jnp.concatenate([code] * (count // 128), axis=1)
    places = lax.broadcasted_iota(jnp.int32, wide.shape, 1).astype(F32)
    return jnp.where(places == wide, 1.0, 0.0).astype(BF16)


def to_lanes(row):
    return jnp.broadcast_to(row, (128, row.shape[1])).T


def call(kernel, outs, arrays, flops, scratch=(), far=(), final=()):
    out_shapes = [jax.ShapeDtypeStruct(shape, dtype) for shape, dtype in outs]
    moved = sum(a.size * a.dtype.itemsize for a in list(arrays) + out_shapes)
    out_shapes = [
        (pltpu.HBM if i in final else pltpu.VMEM)(shape, dtype) for i, (shape, dtype) in enumerate(outs)
    ]
    arrays = [
        pltpu.with_memory_space_constraint(a, pltpu.HBM) if i in far else a for i, a in enumerate(arrays)
    ]
    return pl.pallas_call(
        kernel,
        out_shape=out_shapes,
        in_specs=[pl.BlockSpec(memory_space=pl.ANY if i in far else pltpu.VMEM) for i in range(len(arrays))],
        out_specs=[pl.BlockSpec(memory_space=pltpu.VMEM)] * len(outs),
        scratch_shapes=list(scratch),
        compiler_params=pltpu.CompilerParams(vmem_limit_bytes=VMEM_LIMIT),
        cost_estimate=pl.CostEstimate(flops=flops, bytes_accessed=moved // 8, transcendentals=0),
    )(*arrays)


def parts():
    return [slice(i * TILE, (i + 1) * TILE) for i in range(NC // TILE)]


def first(parent_far, section_far, y_far, linking_far, x_far, cost_far, *refs):
    *outs, y, linking, ylow, nsend, nback, lsend, lback, scol, x_top, cost_top, state, parent_of, section_of, sem = refs
    chunks = parts()
    copies = []
    for cols in chunks:
        copies.append((y_far.at[:, cols], y.at[:, cols]))
        copies.append((linking_far.at[1, cols], linking.at[1, cols]))
    for cols in chunks:
        copies.append((linking_far.at[0, cols], linking.at[0, cols]))
    copies += [(x_far.at[:ROOTS], x_top), (cost_far.at[:ROOTS], cost_top)]
    copies = [(parent_far, parent_of), (section_far, section_of)] + copies
    copies = [pltpu.make_async_copy(a, b, sem.at[i]) for i, (a, b) in enumerate(copies)]
    for copy in copies:
        copy.start()
    copies[0].wait()
    copies[1].wait()
    copies = copies[2:]
    upper = section_of[...].reshape(1, NODES)[:, ROWS] == 1
    parent = parent_of[...].reshape(1, NODES)[:, ROWS]
    here = lax.axis_index("leaf") * N_NODE + lax.axis_index("node")
    owner = ((parent.astype(F32) + 0.5) * (1.0 / NODES)).astype(jnp.int32)
    local = parent - owner * NODES
    ry = ((owner >> 5) - (here >> 5)) & 3
    rz = ((owner >> 3) - (here >> 3)) & 3
    rx = ((owner >> 1) - (here >> 1)) & 3
    rc = (owner ^ here) & 1
    odd = (here & 1) == 1
    outer = jnp.where(odd, rz, ry)
    inner = jnp.where(odd, ry, rz)
    lrow = jnp.where(upper, outer * 128 + inner * ROOTS + local, -1).astype(F32)
    lend = jnp.where(upper, ((-outer) & 3) * 128 + inner * ROOTS + local, -1).astype(F32)
    peer = rx * 2 + rc
    peers = lax.broadcasted_iota(jnp.int32, (N_NODE, CHILD), 0)
    member = jnp.where((peers == peer) & jnp.logical_not(upper), 1.0, 0.0)
    before = lax.broadcasted_iota(jnp.int32, (CHILD, CHILD), 0) <= lax.broadcasted_iota(
        jnp.int32, (CHILD, CHILD), 1
    )
    counts = times(member.astype(BF16), jnp.where(before, 1.0, 0.0).astype(BF16))
    rank = jnp.sum(member * counts, axis=0, keepdims=True) - 1.0
    nrow = jnp.where(upper, -1.0, (peer * CAP_NODE).astype(F32) + rank)
    nend = jnp.where(upper, -1.0, (rc * 256 + rx * CAP_NODE).astype(F32) + rank)
    mark = jnp.where(upper, 0, local - (ROOTS - 1)).astype(F32)
    nsend[...] = nrow
    lsend[...] = lrow
    nback[...] = to_lanes(nend)
    lback[...] = to_lanes(lend)
    scol[...] = to_lanes(jnp.where(upper, 1.0, 2.0))
    total = None
    for i, cols in enumerate(chunks):
        copies[2 * i].wait()
        copies[2 * i + 1].wait()
        low = y[:, cols].astype(BF16)
        ylow[:, cols] = low
        term = times(low[ROWS], linking[1, cols])
        total = term if total is None else total + term
    load = jnp.concatenate([total.astype(BF16), to_lanes(mark).astype(BF16)], axis=1)
    spread(nrow, load, outs[:4])
    total = None
    for i, cols in enumerate(chunks):
        copies[2 * len(chunks) + i].wait()
        term = times(ylow[ROWS, cols], linking[0, cols])
        total = term if total is None else total + term
    spread(lrow, total.astype(BF16), outs[4:])
    copies[-2].wait()
    copies[-1].wait()
    state[...] = x_top[...].astype(BF16)


def spread(row, load, outs):
    hot = hot_rows(row, SLOTS)
    for k, out in enumerate(outs):
        out[...] = times(hot[k * 128 : (k + 1) * 128], load).astype(BF16)


def own_adjoint(ylow, scol, coupling, own):
    upper = jnp.concatenate([scol[...]] * (NS // 128), axis=1) == 1.0
    low = ylow[ROWS]
    own[...] = jnp.where(upper, times(low, coupling[1]), times(low, coupling[2]))


def own_root_first(ylow, cost_top, coupling, own_root):
    own_root[...] = times(ylow[:ROOTS], coupling[0]) - cost_top[...]


def join(blocks, swapped, held):
    for k, block in enumerate(blocks):
        held[k * CAP_NODE : (k + 1) * CAP_NODE] = block[:CAP_NODE]
    held[256:] = swapped[...]


def primal_first(g0, g1, g2, g3, swapped, own, x, cost, rates, wrow, wcol, x_next, extra, *refs):
    *sends, held = refs
    join((g0, g1, g2, g3), swapped, held)
    mark = held[:, NS:].astype(F32)
    row = mark.T[:8]
    wcol[...] = mark
    wrow[...] = row
    primal_child(held[:, :NS], own, x[ROWS], cost, rates, mark, row, x_next, extra, sends)


def primal_second(g0, g1, g2, g3, swapped, own, x, cost, rates, wrow, wcol, x_next, extra, *refs):
    *sends, held = refs
    join((g0, g1, g2, g3), swapped, held)
    primal_child(held[...], own, x[...], cost, rates, wcol[...], wrow[...], x_next, extra, sends)


def primal_child(got, own, x_old, cost, rates, mark, row, x_next, extra, sends):
    tau = rates[:1, :1]
    adjoint = own[...] + times(hot_rows(row[:1] - 1.0, CHILD), got)
    new = jnp.maximum(x_old - tau * (cost[ROWS] - adjoint), 0.0)
    low = (2.0 * new - x_old).astype(BF16)
    x_next[...] = new
    extra[...] = low
    reply = times(hot_lanes(mark - 1.0, CHILD), low).astype(BF16)
    for k, send in enumerate(sends):
        send[:CAP_NODE] = reply[k * CAP_NODE : (k + 1) * CAP_NODE]
        send[CAP_NODE:] = reply[256 + k * CAP_NODE : 256 + (k + 1) * CAP_NODE]


def rooted(j):
    return slice(j * ROOTS, (j + 1) * ROOTS)


def summed(blocks, j):
    return sum(block[rooted((j + k) & 3)].astype(F32) for k, block in enumerate(blocks))


def root_first(g0, g1, g2, g3, own, x, rates, x_next, extra):
    blocks = (g0, g1, g2, g3)
    tau = rates[:1, :1]
    for j in range(4):
        slope = summed(blocks, j)
        if j == 0:
            x_old = x[...]
            slope = slope + own[...]
        else:
            x_old = blocks[(-j) & 3][rooted(4)].astype(F32)
        new = jnp.maximum(x_old + tau * slope, 0.0)
        x_next[rooted(j)] = new
        extra[rooted(j)] = (2.0 * new - x_old).astype(BF16)


def root_second(g0, g1, g2, g3, own, x, rates, extra, x_next):
    blocks = (g0, g1, g2, g3)
    tau = rates[:1, :1]
    for j in range(4):
        slope = summed(blocks, j)
        if j == 0:
            slope = slope + own[...]
        x_old = x[rooted(j)]
        new = jnp.maximum(x_old + tau * slope, 0.0)
        extra[rooted(j)] = (2.0 * new - x_old).astype(BF16)
        if j == 0:
            x_next[...] = new


def averages(x_start, x_root, x_root_next, x_child, x_child_next, average, move):
    roots = (x_root[:ROOTS] + x_root_next[...]) * 0.5
    children = (x_child[...] + x_child_next[...]) * 0.5
    average[:ROOTS] = roots
    average[ROWS] = children
    gap_roots = roots - x_start[:ROOTS]
    gap_children = children - x_start[ROWS]
    total = jnp.sum(gap_roots * gap_roots) + jnp.sum(gap_children * gap_children)
    move[...] = jnp.full((8, 128), total, F32)


def own_image(
    last, extra_child, extra_root, scol, coupling, y, right, rates, cost_top, base, *refs
):
    sigma = rates[1:2, :1]
    upper = jnp.concatenate([scol[...]] * (TILE // 128), axis=1) == 1.0
    child = extra_child[...]
    root = extra_root[:ROOTS]
    total = -cost_top[...]
    for cols in parts():
        image = jnp.where(
            upper, times_t(child, coupling[1, cols]), times_t(child, coupling[2, cols])
        )
        weights = coupling[0, cols]
        base_root = y[:ROOTS, cols] + sigma * (right[:ROOTS, cols] - times_t(root, weights))
        base[:ROOTS, cols] = base_root
        if not last:
            total = total + times(jnp.maximum(base_root, 0.0).astype(BF16), weights)
        base[ROWS, cols] = y[ROWS, cols] + sigma * (right[ROWS, cols] - image)
    if not last:
        (own_root,) = refs
        own_root[...] = total


def from_leaf(blocks, lback):
    hot = hot_lanes(lback[...], SLOTS)
    rows = None
    for k, block in enumerate(blocks):
        term = times(hot[:, k * 128 : (k + 1) * 128], block[...])
        rows = term if rows is None else rows + term
    return rows.astype(BF16)


def dual_leaf(last, b0, b1, b2, b3, lback, linking, base, rates, *refs):
    if last:
        (later,) = refs
    else:
        lsend, later, *outs = refs
    rows = from_leaf((b0, b1, b2, b3), lback)
    sigma = rates[1:2, :1]
    total = None
    for cols in parts():
        weights = linking[0, cols]
        new = base[ROWS, cols] - sigma * times_t(rows, weights)
        later[:, cols] = new
        if not last:
            product = times(jnp.maximum(new, 0.0).astype(BF16), weights)
            total = product if total is None else total + product
    if not last:
        spread(lsend[...], total.astype(BF16), outs)


def from_node(blocks, swapped, nback, held):
    join(blocks, swapped, held)
    return times(hot_lanes(nback[...], SLOTS), held[...]).astype(BF16)


def dual_node(g0, g1, g2, g3, swapped, nback, linking, base, later, rates, nsend, *refs):
    y_next, ylow, *outs, held = refs
    rows = from_node((g0, g1, g2, g3), swapped, nback, held)
    sigma = rates[1:2, :1]
    total = None
    for cols in parts():
        weights = linking[1, cols]
        new_root = jnp.maximum(base[:ROOTS, cols], 0.0)
        new = jnp.maximum(later[:, cols] - sigma * times_t(rows, weights), 0.0)
        low = new.astype(BF16)
        y_next[:ROOTS, cols] = new_root
        y_next[ROWS, cols] = new
        ylow[:ROOTS, cols] = new_root.astype(BF16)
        ylow[ROWS, cols] = low
        product = times(low, weights)
        total = product if total is None else total + product
    spread(nsend[...], total.astype(BF16), outs)


def dual_last(
    g0, g1, g2, g3, swapped, nback, linking, base, later, rates, y, y_start, primal_move, average, load, held
):
    rows = from_node((g0, g1, g2, g3), swapped, nback, held)
    sigma = rates[1:2, :1]
    move = jnp.zeros((1, TILE), F32)
    for cols in parts():
        new_root = jnp.maximum(base[:ROOTS, cols], 0.0)
        new = jnp.maximum(later[:, cols] - sigma * times_t(rows, linking[1, cols]), 0.0)
        mean_root = (y[:ROOTS, cols] + new_root) * 0.5
        mean = (y[ROWS, cols] + new) * 0.5
        average[:ROOTS, cols] = mean_root
        average[ROWS, cols] = mean
        gap_root = mean_root - y_start[:ROOTS, cols]
        gap = mean - y_start[ROWS, cols]
        move = move + jnp.sum(gap_root * gap_root, axis=0, keepdims=True)
        move = move + jnp.sum(gap * gap, axis=0, keepdims=True)
    lane = lax.broadcasted_iota(jnp.int32, load.shape, 2)
    load[...] = jnp.where(lane == 0, primal_move[:1], jnp.sum(move))


def pairs_of(place):
    pairs = []
    for i in range(N_LEAF * N_NODE):
        y, z, x, core = place(i >> 5, (i >> 3) & 3, (i >> 1) & 3, i & 1)
        pairs.append((i, ((y & 3) * 4 + (z & 3)) * N_NODE + (x & 3) * 2 + core))
    return ("leaf", "node"), pairs


def outer_ring(k):
    return pairs_of(lambda y, z, x, c: (y, z + k, x, c) if c else (y + k, z, x, c))


def inner_ring(k):
    return pairs_of(lambda y, z, x, c: (y + k, z, x, c) if c else (y, z + k, x, c))


def ring_x(k):
    return pairs_of(lambda y, z, x, c: (y, z, x + k, c))


def sibling(array):
    return lax.ppermute(array, *pairs_of(lambda y, z, x, c: (y, z, x, 1 - c)))


def shifted(blocks, ring, sign=1):
    got = {0: blocks[0]}
    for k in (2, 1, 3):
        got[k] = lax.ppermute(blocks[k], *ring((sign * k) % 4))
    return [got[k] for k in range(4)]


def swap_node(blocks, sign, before):
    got = shifted(blocks, ring_x, sign)
    halves = jnp.concatenate([block[CAP_NODE:] for block in got], axis=0)
    halves, before = lax.optimization_barrier((halves, before))
    return got + [sibling(halves)], before


def ring_gather(rows, ring):
    one = lax.ppermute(rows, *ring(1))
    three = lax.ppermute(rows, *ring(3))
    return [rows, one, lax.ppermute(one, *ring(1)), three]


def sum_leaf(blocks, own, state, before):
    got, before = lax.optimization_barrier((shifted(blocks, outer_ring), before))
    got = [block.astype(F32) for block in got]
    total = ((got[0] + got[1]) + got[2]) + got[3]
    sent = jnp.concatenate([total[:ROOTS] + own, total[ROOTS:]], axis=0).astype(BF16)
    if state is not None:
        sent = jnp.concatenate([sent, state], axis=0)
    return [total.astype(BF16)] + shifted([sent] * 4, inner_ring)[1:], before


def part_of(kernel, flag):
    def run(*refs):
        kernel(flag, *refs)

    return run


def shards(x_start, y_start, cost_vec, right_side, omega, coupling, linking, parent, section):
    unit = 2 * CHILD * NS * NC
    rates = jnp.broadcast_to(jnp.stack([STEP / omega[0], STEP * omega[0]])[:, None], (2, 128))
    field = ((NODES, NC), F32)
    field_low = ((NODES, NC), BF16)
    states = ((NODES, NS), F32)
    block = ((128, NS), BF16)
    block_mark = ((128, NS + 128), BF16)
    kids = ((CHILD, NS), F32)
    kids_low = ((CHILD, NS), BF16)
    kids_field = ((CHILD, NC), F32)
    tops = ((ROOTS, NS), F32)
    plane = ((4 * ROOTS, NS), F32)
    row = ((1, CHILD), F32)
    col = ((CHILD, 128), F32)
    held = [pltpu.VMEM((SLOTS, NS), BF16)]

    *sent, y_start, linking, ylow, nsend, nback, lsend, lback, scol, x_top, cost_top, state = call(
        first,
        [block_mark] * 4 + [block] * 4
        + [field, ((2, NC, NS), BF16), field_low, row, col, row, col, col, tops, tops, ((ROOTS, NS), BF16)],
        [parent, section, y_start, linking, x_start, cost_vec],
        2 * unit,
        [
            pltpu.VMEM((NODES,), jnp.int32),
            pltpu.VMEM((NODES,), jnp.int32),
            pltpu.SemaphoreType.DMA((3 * NC // TILE + 4,)),
        ],
        (0, 1, 2, 3, 4, 5),
    )
    (own_root,) = call(own_root_first, [tops], [ylow, cost_top, coupling], unit // 8)
    (own,) = call(own_adjoint, [kids], [ylow, scol, coupling], 2 * unit)
    got_leaf, _ = sum_leaf(sent[4:], own_root, state, own_root)
    got_node, (got_leaf, own) = swap_node(sent[:4], 1, (got_leaf, own))

    x_root, extra_root = call(
        root_first,
        [plane, block],
        got_leaf + [own_root, x_top, rates],
        0,
    )
    own, extra_root = lax.optimization_barrier((own, extra_root))
    wrow, wcol, x_child, extra_child, *out_node = call(
        primal_first,
        [((8, SLOTS), F32), ((SLOTS, 128), F32), kids, kids_low] + [block] * 4,
        got_node + [own, x_start, cost_vec, rates],
        unit // 4,
        [pltpu.VMEM((SLOTS, NS + 128), BF16)],
    )
    base, own_root = call(
        part_of(own_image, False),
        [field, tops],
        [
            extra_child, extra_root, scol, coupling, y_start, right_side, rates, cost_top
        ],
        2 * unit,
    )
    back_leaf = ring_gather(extra_root, outer_ring)
    back_node, (back_leaf, base) = swap_node(out_node, -1, (back_leaf, base))
    later, *out_leaf = call(
        part_of(dual_leaf, False),
        [kids_field] + [block] * 4,
        back_leaf + [lback, linking, base, rates, lsend],
        2 * unit,
    )
    y_next, ylow, *out_node = call(
        dual_node,
        [field, field_low] + [block] * 4,
        back_node + [nback, linking, base, later, rates, nsend],
        2 * unit,
        held,
    )
    got_leaf, ylow = sum_leaf(out_leaf, own_root, None, ylow)
    (own,) = call(own_adjoint, [kids], [ylow, scol, coupling], 2 * unit)
    got_node, (got_leaf, own) = swap_node(out_node, 1, (got_leaf, own))

    extra_root, x_top = call(
        root_second,
        [block, tops],
        got_leaf + [own_root, x_root, rates],
        0,
    )
    own, extra_root = lax.optimization_barrier((own, extra_root))
    x_child_next, extra_child, *out_node = call(
        primal_second,
        [kids, kids_low] + [block] * 4,
        got_node + [own, x_child, cost_vec, rates, wrow, wcol],
        unit // 4,
        held,
    )
    x_average, primal_move = call(
        averages,
        [states, ((8, 128), F32)],
        [x_start, x_root, x_top, x_child, x_child_next],
        0,
        final=(0,),
    )
    (base,) = call(
        part_of(own_image, True),
        [field],
        [extra_child, extra_root, scol, coupling, y_next, right_side, rates, cost_top],
        2 * unit,
    )
    back_leaf = ring_gather(extra_root, outer_ring)
    back_node, (back_leaf, base, primal_move) = swap_node(
        out_node, -1, (back_leaf, base, primal_move)
    )
    (later,) = call(
        part_of(dual_leaf, True), [kids_field], back_leaf + [lback, linking, base, rates], unit
    )
    y_average, load = call(
        dual_last,
        [field, ((N_LEAF * N_NODE, 1, 128), F32)],
        back_node + [nback, linking, base, later, rates, y_next, y_start, primal_move],
        unit,
        held,
    )
    moves = lax.all_to_all(load, ("leaf", "node"), split_axis=0, concat_axis=0, tiled=True)
    moves = jnp.sum(moves[:, 0, :2], axis=0)
    omega_new = jnp.sqrt((moves[1:] + 1e-06) / (moves[:1] + 1e-06))
    return (x_average, y_average, omega_new)


def solution(mesh):
    both = P(("leaf", "node"), None)
    flat = P(("leaf", "node"))
    return jax.shard_map(
        shards,
        mesh=mesh,
        in_specs=(both, both, both, both, P(), P(), P(), flat, flat),
        out_specs=(both, both, P()),
        check_vma=False,
    )
```

```python
import jax
import jax.numpy as jnp
from jax import lax
from jax.experimental import pallas as pl
from jax.experimental.pallas import tpu as pltpu
from jax.sharding import PartitionSpec as P

NS = 512
NC = 2048
ROOTS = 32
CHILD = 256
NODES = 288
N_LEAF = 16
N_NODE = 8
CAP_NODE = 64
SLOTS = 512
TILE = 512
VMEM_LIMIT = 24 * 2**20
STEP = 0.3
F32 = jnp.float32
BF16 = jnp.bfloat16
ROWS = slice(ROOTS, NODES)


def times(a, b):
    return lax.dot_general(a, b, (((1,), (0,)), ((), ())), preferred_element_type=F32)


def times_t(a, b):
    return lax.dot_general(a, b, (((1,), (1,)), ((), ())), preferred_element_type=F32)


def hot_rows(code, count):
    places = lax.broadcasted_iota(jnp.int32, (count, code.shape[1]), 0).astype(F32)
    return jnp.where(places == code, 1.0, 0.0).astype(BF16)


def hot_lanes(code, count):
    wide = jnp.concatenate([code] * (count // 128), axis=1)
    places = lax.broadcasted_iota(jnp.int32, wide.shape, 1).astype(F32)
    return jnp.where(places == wide, 1.0, 0.0).astype(BF16)


def to_lanes(row):
    return jnp.broadcast_to(row, (128, row.shape[1])).T


def call(kernel, outs, arrays, flops, scratch=(), far=(), final=()):
    out_shapes = [jax.ShapeDtypeStruct(shape, dtype) for shape, dtype in outs]
    moved = sum(a.size * a.dtype.itemsize for a in list(arrays) + out_shapes)
    out_shapes = [
        (pltpu.HBM if i in final else pltpu.VMEM)(shape, dtype) for i, (shape, dtype) in enumerate(outs)
    ]
    arrays = [
        pltpu.with_memory_space_constraint(a, pltpu.HBM) if i in far else a for i, a in enumerate(arrays)
    ]
    return pl.pallas_call(
        kernel,
        out_shape=out_shapes,
        in_specs=[pl.BlockSpec(memory_space=pl.ANY if i in far else pltpu.VMEM) for i in range(len(arrays))],
        out_specs=[pl.BlockSpec(memory_space=pltpu.VMEM)] * len(outs),
        scratch_shapes=list(scratch),
        compiler_params=pltpu.CompilerParams(vmem_limit_bytes=VMEM_LIMIT),
        cost_estimate=pl.CostEstimate(flops=flops, bytes_accessed=moved // 8, transcendentals=0),
    )(*arrays)


def parts():
    return [slice(i * TILE, (i + 1) * TILE) for i in range(NC // TILE)]


def first(parent_far, section_far, y_far, linking_far, x_far, cost_far, *refs):
    *outs, y, linking, ylow, nsend, nback, lsend, lback, scol, x_top, cost_top, state, parent_of, section_of, sem = refs
    chunks = parts()
    copies = []
    for cols in chunks:
        copies.append((y_far.at[:, cols], y.at[:, cols]))
        copies.append((linking_far.at[1, cols], linking.at[1, cols]))
    for cols in chunks:
        copies.append((linking_far.at[0, cols], linking.at[0, cols]))
    copies += [(x_far.at[:ROOTS], x_top), (cost_far.at[:ROOTS], cost_top)]
    copies = [(parent_far, parent_of), (section_far, section_of)] + copies
    copies = [pltpu.make_async_copy(a, b, sem.at[i]) for i, (a, b) in enumerate(copies)]
    for copy in copies:
        copy.start()
    copies[0].wait()
    copies[1].wait()
    copies = copies[2:]
    upper = section_of[...].reshape(1, NODES)[:, ROWS] == 1
    parent = parent_of[...].reshape(1, NODES)[:, ROWS]
    here = lax.axis_index("leaf") * N_NODE + lax.axis_index("node")
    owner = ((parent.astype(F32) + 0.5) * (1.0 / NODES)).astype(jnp.int32)
    local = parent - owner * NODES
    ry = ((owner >> 5) - (here >> 5)) & 3
    rz = ((owner >> 3) - (here >> 3)) & 3
    rx = ((owner >> 1) - (here >> 1)) & 3
    rc = (owner ^ here) & 1
    odd = (here & 1) == 1
    outer = jnp.where(odd, rz, ry)
    inner = jnp.where(odd, ry, rz)
    lrow = jnp.where(upper, outer * 128 + inner * ROOTS + local, -1).astype(F32)
    lend = jnp.where(upper, ((-outer) & 3) * 128 + inner * ROOTS + local, -1).astype(F32)
    peer = rx * 2 + rc
    peers = lax.broadcasted_iota(jnp.int32, (N_NODE, CHILD), 0)
    member = jnp.where((peers == peer) & jnp.logical_not(upper), 1.0, 0.0)
    before = lax.broadcasted_iota(jnp.int32, (CHILD, CHILD), 0) <= lax.broadcasted_iota(
        jnp.int32, (CHILD, CHILD), 1
    )
    counts = times(member.astype(BF16), jnp.where(before, 1.0, 0.0).astype(BF16))
    rank = jnp.sum(member * counts, axis=0, keepdims=True) - 1.0
    nrow = jnp.where(upper, -1.0, (rc * 256 + rx * CAP_NODE).astype(F32) + rank)
    mark = jnp.where(upper, 0, local - (ROOTS - 1)).astype(F32)
    nsend[...] = nrow
    lsend[...] = lrow
    nback[...] = to_lanes(nrow)
    lback[...] = to_lanes(lend)
    scol[...] = to_lanes(jnp.where(upper, 1.0, 2.0))
    total = None
    for i, cols in enumerate(chunks):
        copies[2 * i].wait()
        copies[2 * i + 1].wait()
        low = y[:, cols].astype(BF16)
        ylow[:, cols] = low
        term = times(low[ROWS], linking[1, cols])
        total = term if total is None else total + term
    load = jnp.concatenate([total.astype(BF16), to_lanes(mark).astype(BF16)], axis=1)
    spread(nrow, load, outs[:2])
    total = None
    for i, cols in enumerate(chunks):
        copies[2 * len(chunks) + i].wait()
        term = times(ylow[ROWS, cols], linking[0, cols])
        total = term if total is None else total + term
    spread(lrow, total.astype(BF16), outs[2:])
    copies[-2].wait()
    copies[-1].wait()
    state[...] = x_top[...].astype(BF16)


def spread(row, load, outs):
    hot = hot_rows(row, SLOTS)
    rows = SLOTS // len(outs)
    for k, out in enumerate(outs):
        out[...] = times(hot[k * rows : (k + 1) * rows], load).astype(BF16)


def own_adjoint(ylow, scol, coupling, own):
    upper = jnp.concatenate([scol[...]] * (NS // 128), axis=1) == 1.0
    low = ylow[ROWS]
    own[...] = jnp.where(upper, times(low, coupling[1]), times(low, coupling[2]))


def own_root_first(ylow, cost_top, coupling, own_root):
    own_root[...] = times(ylow[:ROOTS], coupling[0]) - cost_top[...]


def join(blocks, swapped, held):
    for k, block in enumerate(blocks):
        held[k * CAP_NODE : (k + 1) * CAP_NODE] = block[:CAP_NODE]
    held[256:] = swapped[...]


def stack(blocks, held):
    for k, block in enumerate(blocks):
        held[k * 128 : (k + 1) * 128] = block[...]


def primal_first(g0, g1, g2, g3, own, x, cost, rates, wrow, wcol, x_next, extra, *refs):
    *sends, held = refs
    stack((g0, g1, g2, g3), held)
    mark = held[:, NS:].astype(F32)
    row = mark.T[:8]
    wcol[...] = mark
    wrow[...] = row
    primal_child(held[:, :NS], own, x[ROWS], cost, rates, mark, row, x_next, extra, sends)


def primal_second(g0, g1, g2, g3, own, x, cost, rates, wrow, wcol, x_next, extra, *refs):
    *sends, held = refs
    stack((g0, g1, g2, g3), held)
    primal_child(held[...], own, x[...], cost, rates, wcol[...], wrow[...], x_next, extra, sends)


def primal_child(got, own, x_old, cost, rates, mark, row, x_next, extra, sends):
    tau = rates[:1, :1]
    adjoint = own[...] + times(hot_rows(row[:1] - 1.0, CHILD), got)
    new = jnp.maximum(x_old - tau * (cost[ROWS] - adjoint), 0.0)
    low = (2.0 * new - x_old).astype(BF16)
    x_next[...] = new
    extra[...] = low
    reply = times(hot_lanes(mark - 1.0, CHILD), low).astype(BF16)
    for k, send in enumerate(sends):
        send[...] = reply[k * 128 : (k + 1) * 128]


def rooted(j):
    return slice(j * ROOTS, (j + 1) * ROOTS)


def summed(blocks, j):
    return sum(block[rooted((j + k) & 3)].astype(F32) for k, block in enumerate(blocks))


def root_first(g0, g1, g2, g3, own, x, rates, x_next, extra):
    blocks = (g0, g1, g2, g3)
    tau = rates[:1, :1]
    for j in range(4):
        slope = summed(blocks, j)
        if j == 0:
            x_old = x[...]
            slope = slope + own[...]
        else:
            x_old = blocks[(-j) & 3][rooted(4)].astype(F32)
        new = jnp.maximum(x_old + tau * slope, 0.0)
        x_next[rooted(j)] = new
        extra[rooted(j)] = (2.0 * new - x_old).astype(BF16)


def root_second(g0, g1, g2, g3, own, x, rates, extra, x_next):
    blocks = (g0, g1, g2, g3)
    tau = rates[:1, :1]
    for j in range(4):
        slope = summed(blocks, j)
        if j == 0:
            slope = slope + own[...]
        x_old = x[rooted(j)]
        new = jnp.maximum(x_old + tau * slope, 0.0)
        extra[rooted(j)] = (2.0 * new - x_old).astype(BF16)
        if j == 0:
            x_next[...] = new


def averages(x_start, x_root, x_root_next, x_child, x_child_next, average, move):
    roots = (x_root[:ROOTS] + x_root_next[...]) * 0.5
    children = (x_child[...] + x_child_next[...]) * 0.5
    average[:ROOTS] = roots
    average[ROWS] = children
    gap_roots = roots - x_start[:ROOTS]
    gap_children = children - x_start[ROWS]
    total = jnp.sum(gap_roots * gap_roots) + jnp.sum(gap_children * gap_children)
    move[...] = jnp.full((8, 128), total, F32)


def own_image(
    last, extra_child, extra_root, scol, coupling, y, right, rates, cost_top, base, *refs
):
    sigma = rates[1:2, :1]
    upper = jnp.concatenate([scol[...]] * (TILE // 128), axis=1) == 1.0
    child = extra_child[...]
    root = extra_root[:ROOTS]
    total = -cost_top[...]
    for cols in parts():
        image = jnp.where(
            upper, times_t(child, coupling[1, cols]), times_t(child, coupling[2, cols])
        )
        weights = coupling[0, cols]
        base_root = y[:ROOTS, cols] + sigma * (right[:ROOTS, cols] - times_t(root, weights))
        base[:ROOTS, cols] = base_root
        if not last:
            total = total + times(jnp.maximum(base_root, 0.0).astype(BF16), weights)
        base[ROWS, cols] = y[ROWS, cols] + sigma * (right[ROWS, cols] - image)
    if not last:
        (own_root,) = refs
        own_root[...] = total


def from_leaf(blocks, lback):
    hot = hot_lanes(lback[...], SLOTS)
    rows = None
    for k, block in enumerate(blocks):
        term = times(hot[:, k * 128 : (k + 1) * 128], block[...])
        rows = term if rows is None else rows + term
    return rows.astype(BF16)


def dual_leaf(last, b0, b1, b2, b3, lback, linking, base, rates, *refs):
    if last:
        (later,) = refs
    else:
        lsend, later, *outs = refs
    rows = from_leaf((b0, b1, b2, b3), lback)
    sigma = rates[1:2, :1]
    total = None
    for cols in parts():
        weights = linking[0, cols]
        new = base[ROWS, cols] - sigma * times_t(rows, weights)
        later[:, cols] = new
        if not last:
            product = times(jnp.maximum(new, 0.0).astype(BF16), weights)
            total = product if total is None else total + product
    if not last:
        spread(lsend[...], total.astype(BF16), outs)


def from_node(blocks, swapped, nback, held):
    join(blocks, swapped, held)
    return times(hot_lanes(nback[...], SLOTS), held[...]).astype(BF16)


def dual_node(g0, g1, g2, g3, swapped, nback, linking, base, later, rates, nsend, *refs):
    y_next, ylow, *outs, held = refs
    rows = from_node((g0, g1, g2, g3), swapped, nback, held)
    sigma = rates[1:2, :1]
    total = None
    for cols in parts():
        weights = linking[1, cols]
        new_root = jnp.maximum(base[:ROOTS, cols], 0.0)
        new = jnp.maximum(later[:, cols] - sigma * times_t(rows, weights), 0.0)
        low = new.astype(BF16)
        y_next[:ROOTS, cols] = new_root
        y_next[ROWS, cols] = new
        ylow[:ROOTS, cols] = new_root.astype(BF16)
        ylow[ROWS, cols] = low
        product = times(low, weights)
        total = product if total is None else total + product
    spread(nsend[...], total.astype(BF16), outs)


def dual_last(
    g0, g1, g2, g3, swapped, nback, linking, base, later, rates, y, y_start, primal_move, average, load, held
):
    rows = from_node((g0, g1, g2, g3), swapped, nback, held)
    sigma = rates[1:2, :1]
    move = jnp.zeros((1, TILE), F32)
    for cols in parts():
        new_root = jnp.maximum(base[:ROOTS, cols], 0.0)
        new = jnp.maximum(later[:, cols] - sigma * times_t(rows, linking[1, cols]), 0.0)
        mean_root = (y[:ROOTS, cols] + new_root) * 0.5
        mean = (y[ROWS, cols] + new) * 0.5
        average[:ROOTS, cols] = mean_root
        average[ROWS, cols] = mean
        gap_root = mean_root - y_start[:ROOTS, cols]
        gap = mean - y_start[ROWS, cols]
        move = move + jnp.sum(gap_root * gap_root, axis=0, keepdims=True)
        move = move + jnp.sum(gap * gap, axis=0, keepdims=True)
    lane = lax.broadcasted_iota(jnp.int32, load.shape, 2)
    load[...] = jnp.where(lane == 0, primal_move[:1], jnp.sum(move))


def pairs_of(place):
    pairs = []
    for i in range(N_LEAF * N_NODE):
        y, z, x, core = place(i >> 5, (i >> 3) & 3, (i >> 1) & 3, i & 1)
        pairs.append((i, ((y & 3) * 4 + (z & 3)) * N_NODE + (x & 3) * 2 + core))
    return ("leaf", "node"), pairs


def outer_ring(k):
    return pairs_of(lambda y, z, x, c: (y, z + k, x, c) if c else (y + k, z, x, c))


def inner_ring(k):
    return pairs_of(lambda y, z, x, c: (y + k, z, x, c) if c else (y, z + k, x, c))


def ring_x(k):
    return pairs_of(lambda y, z, x, c: (y, z, x + k, c))


def sibling(array):
    return lax.ppermute(array, *pairs_of(lambda y, z, x, c: (y, z, x, 1 - c)))


def shifted(blocks, ring, sign=1):
    got = {0: blocks[0]}
    for k in (2, 1, 3):
        got[k] = lax.ppermute(blocks[k], *ring((sign * k) % 4))
    return [got[k] for k in range(4)]


def swap_node(blocks, sign, before):
    got = shifted(blocks, ring_x, sign)
    halves = jnp.concatenate([block[CAP_NODE:] for block in got], axis=0)
    halves, before = lax.optimization_barrier((halves, before))
    return got + [sibling(halves)], before


def ring_gather(rows, ring):
    one = lax.ppermute(rows, *ring(1))
    three = lax.ppermute(rows, *ring(3))
    return [rows, one, lax.ppermute(one, *ring(1)), three]


def node_up(mine, swapped):
    blocks = []
    for k in range(4):
        rows = slice(k * CAP_NODE, (k + 1) * CAP_NODE)
        blocks.append(jnp.concatenate([mine[rows], swapped[rows]], axis=0))
    return shifted(blocks, ring_x, 1)


def sum_leaf(blocks, own, state, beside):
    got = [block.astype(F32) for block in shifted(blocks, outer_ring)]
    total = ((got[0] + got[1]) + got[2]) + got[3]
    ahead, total = lax.optimization_barrier(([beside[k] for k in (1,)], total))
    for k, block in zip((1,), ahead):
        beside[k] = block
    sent = jnp.concatenate([total[:ROOTS] + own, total[ROOTS:]], axis=0).astype(BF16)
    if state is not None:
        sent = jnp.concatenate([sent, state], axis=0)
    return [total.astype(BF16)] + shifted([sent] * 4, inner_ring)[1:], beside


def part_of(kernel, flag):
    def run(*refs):
        kernel(flag, *refs)

    return run


def shards(x_start, y_start, cost_vec, right_side, omega, coupling, linking, parent, section):
    unit = 2 * CHILD * NS * NC
    rates = jnp.broadcast_to(jnp.stack([STEP / omega[0], STEP * omega[0]])[:, None], (2, 128))
    field = ((NODES, NC), F32)
    field_low = ((NODES, NC), BF16)
    states = ((NODES, NS), F32)
    block = ((128, NS), BF16)
    half = ((256, NS), BF16)
    half_mark = ((256, NS + 128), BF16)
    kids = ((CHILD, NS), F32)
    kids_low = ((CHILD, NS), BF16)
    kids_field = ((CHILD, NC), F32)
    tops = ((ROOTS, NS), F32)
    plane = ((4 * ROOTS, NS), F32)
    row = ((1, CHILD), F32)
    col = ((CHILD, 128), F32)
    held = [pltpu.VMEM((SLOTS, NS), BF16)]

    *sent, y_start, linking, ylow, nsend, nback, lsend, lback, scol, x_top, cost_top, state = call(
        first,
        [half_mark] * 2 + [block] * 4
        + [field, ((2, NC, NS), BF16), field_low, row, col, row, col, col, tops, tops, ((ROOTS, NS), BF16)],
        [parent, section, y_start, linking, x_start, cost_vec],
        2 * unit,
        [
            pltpu.VMEM((NODES,), jnp.int32),
            pltpu.VMEM((NODES,), jnp.int32),
            pltpu.SemaphoreType.DMA((3 * NC // TILE + 4,)),
        ],
        (0, 1, 2, 3, 4, 5),
    )
    (own_root,) = call(own_root_first, [tops], [ylow, cost_top, coupling], unit // 8)
    (own,) = call(own_adjoint, [kids], [ylow, scol, coupling], 2 * unit)
    swapped = sibling(sent[1])
    got_node = node_up(sent[0], swapped)
    got_leaf, got_node = sum_leaf(sent[2:], own_root, state, got_node)

    wrow, wcol, x_child, extra_child, *out_node = call(
        primal_first,
        [((8, SLOTS), F32), ((SLOTS, 128), F32), kids, kids_low] + [block] * 4,
        got_node + [own, x_start, cost_vec, rates],
        unit // 4,
        [pltpu.VMEM((SLOTS, NS + 128), BF16)],
    )
    got_leaf, extra_child = lax.optimization_barrier((got_leaf, extra_child))
    x_root, extra_root = call(
        root_first,
        [plane, block],
        got_leaf + [own_root, x_top, rates],
        0,
    )
    base, own_root = call(
        part_of(own_image, False),
        [field, tops],
        [
            extra_child, extra_root, scol, coupling, y_start, right_side, rates, cost_top
        ],
        2 * unit,
    )
    back_leaf = ring_gather(extra_root, outer_ring)
    back_node, (back_leaf, base) = swap_node(out_node, -1, (back_leaf, base))
    later, *out_leaf = call(
        part_of(dual_leaf, False),
        [kids_field] + [block] * 4,
        back_leaf + [lback, linking, base, rates, lsend],
        2 * unit,
    )
    y_next, ylow, *out_node = call(
        dual_node,
        [field, field_low] + [half] * 2,
        back_node + [nback, linking, base, later, rates, nsend],
        2 * unit,
        held,
    )
    swapped = sibling(out_node[1])
    got_node = node_up(out_node[0], swapped)
    got_leaf, got_node = sum_leaf(out_leaf, own_root, None, got_node)
    (own,) = call(own_adjoint, [kids], [ylow, scol, coupling], 2 * unit)

    x_child_next, extra_child, *out_node = call(
        primal_second,
        [kids, kids_low] + [block] * 4,
        got_node + [own, x_child, cost_vec, rates, wrow, wcol],
        unit // 4,
        held,
    )
    got_leaf, extra_child = lax.optimization_barrier((got_leaf, extra_child))
    extra_root, x_top = call(
        root_second,
        [block, tops],
        got_leaf + [own_root, x_root, rates],
        0,
    )
    x_average, primal_move = call(
        averages,
        [states, ((8, 128), F32)],
        [x_start, x_root, x_top, x_child, x_child_next],
        0,
        final=(0,),
    )
    (base,) = call(
        part_of(own_image, True),
        [field],
        [extra_child, extra_root, scol, coupling, y_next, right_side, rates, cost_top],
        2 * unit,
    )
    back_leaf = ring_gather(extra_root, outer_ring)
    back_node, (back_leaf, base, primal_move) = swap_node(
        out_node, -1, (back_leaf, base, primal_move)
    )
    (later,) = call(
        part_of(dual_leaf, True), [kids_field], back_leaf + [lback, linking, base, rates], unit
    )
    y_average, load = call(
        dual_last,
        [field, ((N_LEAF * N_NODE, 1, 128), F32)],
        back_node + [nback, linking, base, later, rates, y_next, y_start, primal_move],
        unit,
        held,
    )
    moves = lax.all_to_all(load, ("leaf", "node"), split_axis=0, concat_axis=0, tiled=True)
    moves = jnp.sum(moves[:, 0, :2], axis=0)
    omega_new = jnp.sqrt((moves[1:] + 1e-06) / (moves[:1] + 1e-06))
    return (x_average, y_average, omega_new)


def solution(mesh):
    both = P(("leaf", "node"), None)
    flat = P(("leaf", "node"))
    return jax.shard_map(
        shards,
        mesh=mesh,
        in_specs=(both, both, both, both, P(), P(), P(), flat, flat),
        out_specs=(both, both, P()),
        check_vma=False,
    )
```

```python
import jax
import jax.numpy as jnp
from jax import lax
from jax.experimental import pallas as pl
from jax.experimental.pallas import tpu as pltpu
from jax.sharding import PartitionSpec as P

NS = 512
NC = 2048
ROOTS = 32
CHILD = 256
NODES = 288
N_LEAF = 16
N_NODE = 8
CAP_NODE = 64
SLOTS = 512
TILE = 1024
CHUNK = 512
VMEM_LIMIT = 24 * 2**20
STEP = 0.3
F32 = jnp.float32
BF16 = jnp.bfloat16
ROWS = slice(ROOTS, NODES)


def times(a, b):
    return lax.dot_general(a, b, (((1,), (0,)), ((), ())), preferred_element_type=F32)


def times_t(a, b):
    return lax.dot_general(a, b, (((1,), (1,)), ((), ())), preferred_element_type=F32)


def hot_rows(code, count):
    places = lax.broadcasted_iota(jnp.int32, (count, code.shape[1]), 0).astype(F32)
    return jnp.where(places == code, 1.0, 0.0).astype(BF16)


def hot_lanes(code, count):
    wide = jnp.concatenate([code] * (count // 128), axis=1)
    places = lax.broadcasted_iota(jnp.int32, wide.shape, 1).astype(F32)
    return jnp.where(places == wide, 1.0, 0.0).astype(BF16)


def to_lanes(row):
    return jnp.broadcast_to(row, (128, row.shape[1])).T


def call(kernel, outs, arrays, flops, scratch=(), far=(), final=()):
    out_shapes = [jax.ShapeDtypeStruct(shape, dtype) for shape, dtype in outs]
    moved = sum(a.size * a.dtype.itemsize for a in list(arrays) + out_shapes)
    out_shapes = [
        (pltpu.HBM if i in final else pltpu.VMEM)(shape, dtype) for i, (shape, dtype) in enumerate(outs)
    ]
    arrays = [
        pltpu.with_memory_space_constraint(a, pltpu.HBM) if i in far else a for i, a in enumerate(arrays)
    ]
    return pl.pallas_call(
        kernel,
        out_shape=out_shapes,
        in_specs=[pl.BlockSpec(memory_space=pl.ANY if i in far else pltpu.VMEM) for i in range(len(arrays))],
        out_specs=[pl.BlockSpec(memory_space=pltpu.VMEM)] * len(outs),
        scratch_shapes=list(scratch),
        compiler_params=pltpu.CompilerParams(vmem_limit_bytes=VMEM_LIMIT),
        cost_estimate=pl.CostEstimate(flops=flops, bytes_accessed=moved // 8, transcendentals=0),
    )(*arrays)


def parts(size=TILE):
    return [slice(i * size, (i + 1) * size) for i in range(NC // size)]


def first(parent_far, section_far, y_far, linking_far, x_far, cost_far, *refs):
    *outs, y, linking, ylow, nsend, nback, lsend, lback, scol, x_top, cost_top, state, parent_of, section_of, sem = refs
    chunks = parts(CHUNK)
    copies = []
    for cols in chunks:
        copies.append((y_far.at[:, cols], y.at[:, cols]))
        copies.append((linking_far.at[1, cols], linking.at[1, cols]))
    for cols in chunks:
        copies.append((linking_far.at[0, cols], linking.at[0, cols]))
    copies += [(x_far.at[:ROOTS], x_top), (cost_far.at[:ROOTS], cost_top)]
    copies = [(parent_far, parent_of), (section_far, section_of)] + copies
    copies = [pltpu.make_async_copy(a, b, sem.at[i]) for i, (a, b) in enumerate(copies)]
    for copy in copies:
        copy.start()
    copies[0].wait()
    copies[1].wait()
    copies = copies[2:]
    upper = section_of[...].reshape(1, NODES)[:, ROWS] == 1
    parent = parent_of[...].reshape(1, NODES)[:, ROWS]
    here = lax.axis_index("leaf") * N_NODE + lax.axis_index("node")
    owner = ((parent.astype(F32) + 0.5) * (1.0 / NODES)).astype(jnp.int32)
    local = parent - owner * NODES
    ry = ((owner >> 5) - (here >> 5)) & 3
    rz = ((owner >> 3) - (here >> 3)) & 3
    rx = ((owner >> 1) - (here >> 1)) & 3
    rc = (owner ^ here) & 1
    odd = (here & 1) == 1
    outer = jnp.where(odd, rz, ry)
    inner = jnp.where(odd, ry, rz)
    lrow = jnp.where(upper, outer * 128 + inner * ROOTS + local, -1).astype(F32)
    lend = jnp.where(upper, ((-outer) & 3) * 128 + inner * ROOTS + local, -1).astype(F32)
    peer = rx * 2 + rc
    peers = lax.broadcasted_iota(jnp.int32, (N_NODE, CHILD), 0)
    member = jnp.where((peers == peer) & jnp.logical_not(upper), 1.0, 0.0)
    before = lax.broadcasted_iota(jnp.int32, (CHILD, CHILD), 0) <= lax.broadcasted_iota(
        jnp.int32, (CHILD, CHILD), 1
    )
    counts = times(member.astype(BF16), jnp.where(before, 1.0, 0.0).astype(BF16))
    rank = jnp.sum(member * counts, axis=0, keepdims=True) - 1.0
    nrow = jnp.where(upper, -1.0, (peer * CAP_NODE).astype(F32) + rank)
    nend = jnp.where(upper, -1.0, (rc * 256 + rx * CAP_NODE).astype(F32) + rank)
    mark = jnp.where(upper, 0, local - (ROOTS - 1)).astype(F32)
    nsend[...] = nrow
    lsend[...] = lrow
    nback[...] = to_lanes(nend)
    lback[...] = to_lanes(lend)
    scol[...] = to_lanes(jnp.where(upper, 1.0, 2.0))
    total = None
    for i, cols in enumerate(chunks):
        copies[2 * i].wait()
        copies[2 * i + 1].wait()
        low = y[:, cols].astype(BF16)
        ylow[:, cols] = low
        term = times(low[ROWS], linking[1, cols])
        total = term if total is None else total + term
    load = jnp.concatenate([total.astype(BF16), to_lanes(mark).astype(BF16)], axis=1)
    spread(nrow, load, outs[:4])
    total = None
    for i, cols in enumerate(chunks):
        copies[2 * len(chunks) + i].wait()
        term = times(ylow[ROWS, cols], linking[0, cols])
        total = term if total is None else total + term
    spread(lrow, total.astype(BF16), outs[4:])
    copies[-2].wait()
    copies[-1].wait()
    state[...] = x_top[...].astype(BF16)


def spread(row, load, outs):
    hot = hot_rows(row, SLOTS)
    for k, out in enumerate(outs):
        out[...] = times(hot[k * 128 : (k + 1) * 128], load).astype(BF16)


def own_adjoint(ylow, scol, coupling, own):
    upper = jnp.concatenate([scol[...]] * (NS // 128), axis=1) == 1.0
    low = ylow[ROWS]
    own[...] = jnp.where(upper, times(low, coupling[1]), times(low, coupling[2]))


def own_root_first(ylow, cost_top, coupling, own_root):
    own_root[...] = times(ylow[:ROOTS], coupling[0]) - cost_top[...]


def join(blocks, swapped, held):
    for k, block in enumerate(blocks):
        held[k * CAP_NODE : (k + 1) * CAP_NODE] = block[:CAP_NODE]
    held[256:] = swapped[...]


def primal_first(g0, g1, g2, g3, swapped, own, x, cost, rates, wrow, wcol, x_next, extra, *refs):
    *sends, held = refs
    join((g0, g1, g2, g3), swapped, held)
    mark = held[:, NS:].astype(F32)
    row = mark.T[:8]
    wcol[...] = mark
    wrow[...] = row
    primal_child(held[:, :NS], own, x[ROWS], cost, rates, mark, row, x_next, extra, sends)


def primal_second(g0, g1, g2, g3, swapped, own, x, cost, rates, wrow, wcol, x_next, extra, *refs):
    *sends, held = refs
    join((g0, g1, g2, g3), swapped, held)
    primal_child(held[...], own, x[...], cost, rates, wcol[...], wrow[...], x_next, extra, sends)


def primal_child(got, own, x_old, cost, rates, mark, row, x_next, extra, sends):
    tau = rates[:1, :1]
    adjoint = own[...] + times(hot_rows(row[:1] - 1.0, CHILD), got)
    new = jnp.maximum(x_old - tau * (cost[ROWS] - adjoint), 0.0)
    low = (2.0 * new - x_old).astype(BF16)
    x_next[...] = new
    extra[...] = low
    reply = times(hot_lanes(mark - 1.0, CHILD), low).astype(BF16)
    for k, send in enumerate(sends):
        send[:CAP_NODE] = reply[k * CAP_NODE : (k + 1) * CAP_NODE]
        send[CAP_NODE:] = reply[256 + k * CAP_NODE : 256 + (k + 1) * CAP_NODE]


def rooted(j):
    return slice(j * ROOTS, (j + 1) * ROOTS)


def summed(blocks, j):
    return sum(block[rooted((j + k) & 3)].astype(F32) for k, block in enumerate(blocks))


def root_first(g0, g1, g2, g3, own, x, rates, x_next, extra):
    blocks = (g0, g1, g2, g3)
    tau = rates[:1, :1]
    for j in range(4):
        slope = summed(blocks, j)
        if j == 0:
            x_old = x[...]
            slope = slope + own[...]
        else:
            x_old = blocks[(-j) & 3][rooted(4)].astype(F32)
        new = jnp.maximum(x_old + tau * slope, 0.0)
        x_next[rooted(j)] = new
        extra[rooted(j)] = (2.0 * new - x_old).astype(BF16)


def root_second(g0, g1, g2, g3, own, x, rates, extra, x_next):
    blocks = (g0, g1, g2, g3)
    tau = rates[:1, :1]
    for j in range(4):
        slope = summed(blocks, j)
        if j == 0:
            slope = slope + own[...]
        x_old = x[rooted(j)]
        new = jnp.maximum(x_old + tau * slope, 0.0)
        extra[rooted(j)] = (2.0 * new - x_old).astype(BF16)
        if j == 0:
            x_next[...] = new


def averages(x_start, x_root, x_root_next, x_child, x_child_next, average, move):
    roots = (x_root[:ROOTS] + x_root_next[...]) * 0.5
    children = (x_child[...] + x_child_next[...]) * 0.5
    average[:ROOTS] = roots
    average[ROWS] = children
    gap_roots = roots - x_start[:ROOTS]
    gap_children = children - x_start[ROWS]
    total = jnp.sum(gap_roots * gap_roots) + jnp.sum(gap_children * gap_children)
    move[...] = jnp.full((8, 128), total, F32)


def own_image(
    last, extra_child, extra_root, scol, coupling, y, right, rates, cost_top, base, *refs
):
    sigma = rates[1:2, :1]
    upper = jnp.concatenate([scol[...]] * (TILE // 128), axis=1) == 1.0
    child = extra_child[...]
    root = extra_root[:ROOTS]
    total = -cost_top[...]
    for cols in parts():
        image = jnp.where(
            upper, times_t(child, coupling[1, cols]), times_t(child, coupling[2, cols])
        )
        weights = coupling[0, cols]
        base_root = y[:ROOTS, cols] + sigma * (right[:ROOTS, cols] - times_t(root, weights))
        base[:ROOTS, cols] = base_root
        if not last:
            total = total + times(jnp.maximum(base_root, 0.0).astype(BF16), weights)
        base[ROWS, cols] = y[ROWS, cols] + sigma * (right[ROWS, cols] - image)
    if not last:
        (own_root,) = refs
        own_root[...] = total


def from_leaf(blocks, lback):
    hot = hot_lanes(lback[...], SLOTS)
    rows = None
    for k, block in enumerate(blocks):
        term = times(hot[:, k * 128 : (k + 1) * 128], block[...])
        rows = term if rows is None else rows + term
    return rows.astype(BF16)


def dual_leaf(last, b0, b1, b2, b3, lback, linking, base, rates, *refs):
    if last:
        (later,) = refs
    else:
        lsend, later, *outs = refs
    rows = from_leaf((b0, b1, b2, b3), lback)
    sigma = rates[1:2, :1]
    total = None
    for cols in parts():
        weights = linking[0, cols]
        new = base[ROWS, cols] - sigma * times_t(rows, weights)
        later[:, cols] = new
        if not last:
            product = times(jnp.maximum(new, 0.0).astype(BF16), weights)
            total = product if total is None else total + product
    if not last:
        spread(lsend[...], total.astype(BF16), outs)


def from_node(blocks, swapped, nback, held):
    join(blocks, swapped, held)
    return times(hot_lanes(nback[...], SLOTS), held[...]).astype(BF16)


def dual_node(g0, g1, g2, g3, swapped, nback, linking, base, later, rates, nsend, *refs):
    y_next, ylow, *outs, held = refs
    rows = from_node((g0, g1, g2, g3), swapped, nback, held)
    sigma = rates[1:2, :1]
    total = None
    for cols in parts():
        weights = linking[1, cols]
        new_root = jnp.maximum(base[:ROOTS, cols], 0.0)
        new = jnp.maximum(later[:, cols] - sigma * times_t(rows, weights), 0.0)
        low = new.astype(BF16)
        y_next[:ROOTS, cols] = new_root
        y_next[ROWS, cols] = new
        ylow[:ROOTS, cols] = new_root.astype(BF16)
        ylow[ROWS, cols] = low
        product = times(low, weights)
        total = product if total is None else total + product
    spread(nsend[...], total.astype(BF16), outs)


def dual_last(
    g0, g1, g2, g3, swapped, nback, linking, base, later, rates, y, y_start, primal_move, average, load, held
):
    rows = from_node((g0, g1, g2, g3), swapped, nback, held)
    sigma = rates[1:2, :1]
    move = jnp.zeros((1, TILE), F32)
    for cols in parts():
        new_root = jnp.maximum(base[:ROOTS, cols], 0.0)
        new = jnp.maximum(later[:, cols] - sigma * times_t(rows, linking[1, cols]), 0.0)
        mean_root = (y[:ROOTS, cols] + new_root) * 0.5
        mean = (y[ROWS, cols] + new) * 0.5
        average[:ROOTS, cols] = mean_root
        average[ROWS, cols] = mean
        gap_root = mean_root - y_start[:ROOTS, cols]
        gap = mean - y_start[ROWS, cols]
        move = move + jnp.sum(gap_root * gap_root, axis=0, keepdims=True)
        move = move + jnp.sum(gap * gap, axis=0, keepdims=True)
    lane = lax.broadcasted_iota(jnp.int32, load.shape, 2)
    load[...] = jnp.where(lane == 0, primal_move[:1], jnp.sum(move))


def pairs_of(place):
    pairs = []
    for i in range(N_LEAF * N_NODE):
        y, z, x, core = place(i >> 5, (i >> 3) & 3, (i >> 1) & 3, i & 1)
        pairs.append((i, ((y & 3) * 4 + (z & 3)) * N_NODE + (x & 3) * 2 + core))
    return ("leaf", "node"), pairs


def outer_ring(k):
    return pairs_of(lambda y, z, x, c: (y, z + k, x, c) if c else (y + k, z, x, c))


def inner_ring(k):
    return pairs_of(lambda y, z, x, c: (y + k, z, x, c) if c else (y, z + k, x, c))


def ring_x(k):
    return pairs_of(lambda y, z, x, c: (y, z, x + k, c))


def sibling(array):
    return lax.ppermute(array, *pairs_of(lambda y, z, x, c: (y, z, x, 1 - c)))


def shifted(blocks, ring, sign=1):
    got = {0: blocks[0]}
    for k in (2, 1, 3):
        got[k] = lax.ppermute(blocks[k], *ring((sign * k) % 4))
    return [got[k] for k in range(4)]


def swap_node(blocks, sign, before):
    got = shifted(blocks, ring_x, sign)
    halves = jnp.concatenate([block[CAP_NODE:] for block in got], axis=0)
    halves, before = lax.optimization_barrier((halves, before))
    return got + [sibling(halves)], before


def ring_gather(rows, ring):
    one = lax.ppermute(rows, *ring(1))
    three = lax.ppermute(rows, *ring(3))
    return [rows, one, lax.ppermute(one, *ring(1)), three]


def sum_leaf(blocks, own, state, before):
    got, before = lax.optimization_barrier((shifted(blocks, outer_ring), before))
    got = [block.astype(F32) for block in got]
    total = ((got[0] + got[1]) + got[2]) + got[3]
    sent = jnp.concatenate([total[:ROOTS] + own, total[ROOTS:]], axis=0).astype(BF16)
    if state is not None:
        sent = jnp.concatenate([sent, state], axis=0)
    return [total.astype(BF16)] + shifted([sent] * 4, inner_ring)[1:], before


def part_of(kernel, flag):
    def run(*refs):
        kernel(flag, *refs)

    return run


def shards(x_start, y_start, cost_vec, right_side, omega, coupling, linking, parent, section):
    unit = 2 * CHILD * NS * NC
    rates = jnp.broadcast_to(jnp.stack([STEP / omega[0], STEP * omega[0]])[:, None], (2, 128))
    field = ((NODES, NC), F32)
    field_low = ((NODES, NC), BF16)
    states = ((NODES, NS), F32)
    block = ((128, NS), BF16)
    block_mark = ((128, NS + 128), BF16)
    kids = ((CHILD, NS), F32)
    kids_low = ((CHILD, NS), BF16)
    kids_field = ((CHILD, NC), F32)
    tops = ((ROOTS, NS), F32)
    plane = ((4 * ROOTS, NS), F32)
    row = ((1, CHILD), F32)
    col = ((CHILD, 128), F32)
    held = [pltpu.VMEM((SLOTS, NS), BF16)]

    *sent, y_start, linking, ylow, nsend, nback, lsend, lback, scol, x_top, cost_top, state = call(
        first,
        [block_mark] * 4 + [block] * 4
        + [field, ((2, NC, NS), BF16), field_low, row, col, row, col, col, tops, tops, ((ROOTS, NS), BF16)],
        [parent, section, y_start, linking, x_start, cost_vec],
        2 * unit,
        [
            pltpu.VMEM((NODES,), jnp.int32),
            pltpu.VMEM((NODES,), jnp.int32),
            pltpu.SemaphoreType.DMA((3 * NC // CHUNK + 4,)),
        ],
        (0, 1, 2, 3, 4, 5),
    )
    (own_root,) = call(own_root_first, [tops], [ylow, cost_top, coupling], unit // 8)
    (own,) = call(own_adjoint, [kids], [ylow, scol, coupling], 2 * unit)
    got_leaf, _ = sum_leaf(sent[4:], own_root, state, own_root)
    got_node, (got_leaf, own) = swap_node(sent[:4], 1, (got_leaf, own))

    x_root, extra_root = call(
        root_first,
        [plane, block],
        got_leaf + [own_root, x_top, rates],
        0,
    )
    own, extra_root = lax.optimization_barrier((own, extra_root))
    wrow, wcol, x_child, extra_child, *out_node = call(
        primal_first,
        [((8, SLOTS), F32), ((SLOTS, 128), F32), kids, kids_low] + [block] * 4,
        got_node + [own, x_start, cost_vec, rates],
        unit // 4,
        [pltpu.VMEM((SLOTS, NS + 128), BF16)],
    )
    base, own_root = call(
        part_of(own_image, False),
        [field, tops],
        [
            extra_child, extra_root, scol, coupling, y_start, right_side, rates, cost_top
        ],
        2 * unit,
    )
    back_leaf = ring_gather(extra_root, outer_ring)
    back_node, (back_leaf, base) = swap_node(out_node, -1, (back_leaf, base))
    later, *out_leaf = call(
        part_of(dual_leaf, False),
        [kids_field] + [block] * 4,
        back_leaf + [lback, linking, base, rates, lsend],
        2 * unit,
    )
    y_next, ylow, *out_node = call(
        dual_node,
        [field, field_low] + [block] * 4,
        back_node + [nback, linking, base, later, rates, nsend],
        2 * unit,
        held,
    )
    got_leaf, ylow = sum_leaf(out_leaf, own_root, None, ylow)
    (own,) = call(own_adjoint, [kids], [ylow, scol, coupling], 2 * unit)
    got_node, (got_leaf, own) = swap_node(out_node, 1, (got_leaf, own))

    extra_root, x_top = call(
        root_second,
        [block, tops],
        got_leaf + [own_root, x_root, rates],
        0,
    )
    own, extra_root = lax.optimization_barrier((own, extra_root))
    x_child_next, extra_child, *out_node = call(
        primal_second,
        [kids, kids_low] + [block] * 4,
        got_node + [own, x_child, cost_vec, rates, wrow, wcol],
        unit // 4,
        held,
    )
    x_average, primal_move = call(
        averages,
        [states, ((8, 128), F32)],
        [x_start, x_root, x_top, x_child, x_child_next],
        0,
        final=(0,),
    )
    (base,) = call(
        part_of(own_image, True),
        [field],
        [extra_child, extra_root, scol, coupling, y_next, right_side, rates, cost_top],
        2 * unit,
    )
    back_leaf = ring_gather(extra_root, outer_ring)
    back_node, (back_leaf, base, primal_move) = swap_node(
        out_node, -1, (back_leaf, base, primal_move)
    )
    (later,) = call(
        part_of(dual_leaf, True), [kids_field], back_leaf + [lback, linking, base, rates], unit
    )
    y_average, load = call(
        dual_last,
        [field, ((N_LEAF * N_NODE, 1, 128), F32)],
        back_node + [nback, linking, base, later, rates, y_next, y_start, primal_move],
        unit,
        held,
    )
    moves = lax.all_to_all(load, ("leaf", "node"), split_axis=0, concat_axis=0, tiled=True)
    moves = jnp.sum(moves[:, 0, :2], axis=0)
    omega_new = jnp.sqrt((moves[1:] + 1e-06) / (moves[:1] + 1e-06))
    return (x_average, y_average, omega_new)


def solution(mesh):
    both = P(("leaf", "node"), None)
    flat = P(("leaf", "node"))
    return jax.shard_map(
        shards,
        mesh=mesh,
        in_specs=(both, both, both, both, P(), P(), P(), flat, flat),
        out_specs=(both, both, P()),
        check_vma=False,
    )
```

```python
import jax
import jax.numpy as jnp
from jax import lax
from jax.experimental import pallas as pl
from jax.experimental.pallas import tpu as pltpu
from jax.sharding import PartitionSpec as P

NS = 512
NC = 2048
ROOTS = 32
CHILD = 256
NODES = 288
N_LEAF = 16
N_NODE = 8
CAP_NODE = 64
SLOTS = 512
TILE = 1024
CHUNK = 512
VMEM_LIMIT = 24 * 2**20
STEP = 0.3
F32 = jnp.float32
BF16 = jnp.bfloat16
ROWS = slice(ROOTS, NODES)


def times(a, b):
    return lax.dot_general(a, b, (((1,), (0,)), ((), ())), preferred_element_type=F32)


def times_t(a, b):
    return lax.dot_general(a, b, (((1,), (1,)), ((), ())), preferred_element_type=F32)


def hot_rows(code, count):
    places = lax.broadcasted_iota(jnp.int32, (count, code.shape[1]), 0).astype(F32)
    return jnp.where(places == code, 1.0, 0.0).astype(BF16)


def hot_lanes(code, count):
    wide = jnp.concatenate([code] * (count // 128), axis=1)
    places = lax.broadcasted_iota(jnp.int32, wide.shape, 1).astype(F32)
    return jnp.where(places == wide, 1.0, 0.0).astype(BF16)


def to_lanes(row):
    return jnp.broadcast_to(row, (128, row.shape[1])).T


def call(kernel, outs, arrays, flops, scratch=(), far=(), final=()):
    out_shapes = [jax.ShapeDtypeStruct(shape, dtype) for shape, dtype in outs]
    moved = sum(a.size * a.dtype.itemsize for a in list(arrays) + out_shapes)
    out_shapes = [
        (pltpu.HBM if i in final else pltpu.VMEM)(shape, dtype) for i, (shape, dtype) in enumerate(outs)
    ]
    arrays = [
        pltpu.with_memory_space_constraint(a, pltpu.HBM) if i in far else a for i, a in enumerate(arrays)
    ]
    return pl.pallas_call(
        kernel,
        out_shape=out_shapes,
        in_specs=[pl.BlockSpec(memory_space=pl.ANY if i in far else pltpu.VMEM) for i in range(len(arrays))],
        out_specs=[pl.BlockSpec(memory_space=pltpu.VMEM)] * len(outs),
        scratch_shapes=list(scratch),
        compiler_params=pltpu.CompilerParams(vmem_limit_bytes=VMEM_LIMIT),
        cost_estimate=pl.CostEstimate(flops=flops, bytes_accessed=moved // 8, transcendentals=0),
    )(*arrays)


def parts(size=TILE):
    return [slice(i * size, (i + 1) * size) for i in range(NC // size)]


def first(parent_far, section_far, y_far, linking_far, x_far, cost_far, *refs):
    *outs, y, linking, ylow, nsend, nback, lsend, lback, scol, x_top, cost_top, state, parent_of, section_of, sem = refs
    chunks = parts(CHUNK)
    copies = []
    for cols in chunks:
        copies.append((y_far.at[:, cols], y.at[:, cols]))
        copies.append((linking_far.at[1, cols], linking.at[1, cols]))
    for cols in chunks:
        copies.append((linking_far.at[0, cols], linking.at[0, cols]))
    copies += [(x_far.at[:ROOTS], x_top), (cost_far.at[:ROOTS], cost_top)]
    copies = [(parent_far, parent_of), (section_far, section_of)] + copies
    copies = [pltpu.make_async_copy(a, b, sem.at[i]) for i, (a, b) in enumerate(copies)]
    for copy in copies:
        copy.start()
    copies[0].wait()
    copies[1].wait()
    copies = copies[2:]
    upper = section_of[...].reshape(1, NODES)[:, ROWS] == 1
    parent = parent_of[...].reshape(1, NODES)[:, ROWS]
    here = lax.axis_index("leaf") * N_NODE + lax.axis_index("node")
    owner = ((parent.astype(F32) + 0.5) * (1.0 / NODES)).astype(jnp.int32)
    local = parent - owner * NODES
    ry = ((owner >> 5) - (here >> 5)) & 3
    rz = ((owner >> 3) - (here >> 3)) & 3
    rx = ((owner >> 1) - (here >> 1)) & 3
    rc = (owner ^ here) & 1
    odd = (here & 1) == 1
    outer = jnp.where(odd, rz, ry)
    inner = jnp.where(odd, ry, rz)
    lrow = jnp.where(upper, outer * 128 + inner * ROOTS + local, -1).astype(F32)
    lend = jnp.where(upper, ((-outer) & 3) * 128 + inner * ROOTS + local, -1).astype(F32)
    peer = rx * 2 + rc
    peers = lax.broadcasted_iota(jnp.int32, (N_NODE, CHILD), 0)
    member = jnp.where((peers == peer) & jnp.logical_not(upper), 1.0, 0.0)
    before = lax.broadcasted_iota(jnp.int32, (CHILD, CHILD), 0) <= lax.broadcasted_iota(
        jnp.int32, (CHILD, CHILD), 1
    )
    counts = times(member.astype(BF16), jnp.where(before, 1.0, 0.0).astype(BF16))
    rank = jnp.sum(member * counts, axis=0, keepdims=True) - 1.0
    nrow = jnp.where(upper, -1.0, (peer * CAP_NODE).astype(F32) + rank)
    nend = jnp.where(upper, -1.0, (rc * 256 + rx * CAP_NODE).astype(F32) + rank)
    mark = jnp.where(upper, 0, local - (ROOTS - 1)).astype(F32)
    nsend[...] = nrow
    lsend[...] = lrow
    nback[...] = to_lanes(nend)
    lback[...] = to_lanes(lend)
    scol[...] = to_lanes(jnp.where(upper, 1.0, 2.0))
    total = None
    for i, cols in enumerate(chunks):
        copies[2 * i].wait()
        copies[2 * i + 1].wait()
        low = y[:, cols].astype(BF16)
        ylow[:, cols] = low
        term = times(low[ROWS], linking[1, cols])
        total = term if total is None else total + term
    load = jnp.concatenate([total.astype(BF16), to_lanes(mark).astype(BF16)], axis=1)
    spread(nrow, load, outs[:4])
    total = None
    for i, cols in enumerate(chunks):
        copies[2 * len(chunks) + i].wait()
        term = times(ylow[ROWS, cols], linking[0, cols])
        total = term if total is None else total + term
    spread(lrow, total.astype(BF16), outs[4:])
    copies[-2].wait()
    copies[-1].wait()
    state[...] = x_top[...].astype(BF16)


def spread(row, load, outs):
    hot = hot_rows(row, SLOTS)
    for k, out in enumerate(outs):
        out[...] = times(hot[k * 128 : (k + 1) * 128], load).astype(BF16)


def own_adjoint(ylow, scol, coupling, own):
    upper = jnp.concatenate([scol[...]] * (NS // 128), axis=1) == 1.0
    low = ylow[ROWS]
    own[...] = jnp.where(upper, times(low, coupling[1]), times(low, coupling[2]))


def own_root_first(ylow, cost_top, coupling, own_root):
    own_root[...] = times(ylow[:ROOTS], coupling[0]) - cost_top[...]


def join(blocks, swapped, held):
    for k, block in enumerate(blocks):
        held[k * CAP_NODE : (k + 1) * CAP_NODE] = block[:CAP_NODE]
    held[256:] = swapped[...]


def primal_first(g0, g1, g2, g3, swapped, own, x, cost, rates, wrow, wcol, x_next, extra, *refs):
    *sends, held = refs
    join((g0, g1, g2, g3), swapped, held)
    mark = held[:, NS:].astype(F32)
    row = mark.T[:8]
    wcol[...] = mark
    wrow[...] = row
    primal_child(held[:, :NS], own, x[ROWS], cost, rates, mark, row, x_next, extra, sends)


def primal_second(g0, g1, g2, g3, swapped, own, x, cost, rates, wrow, wcol, x_next, extra, *refs):
    *sends, held = refs
    join((g0, g1, g2, g3), swapped, held)
    primal_child(held[...], own, x[...], cost, rates, wcol[...], wrow[...], x_next, extra, sends)


def primal_child(got, own, x_old, cost, rates, mark, row, x_next, extra, sends):
    tau = rates[:1, :1]
    adjoint = own[...] + times(hot_rows(row[:1] - 1.0, CHILD), got)
    new = jnp.maximum(x_old - tau * (cost[ROWS] - adjoint), 0.0)
    low = (2.0 * new - x_old).astype(BF16)
    x_next[...] = new
    extra[...] = low
    reply = times(hot_lanes(mark - 1.0, CHILD), low).astype(BF16)
    for k, send in enumerate(sends):
        send[:CAP_NODE] = reply[k * CAP_NODE : (k + 1) * CAP_NODE]
        send[CAP_NODE:] = reply[256 + k * CAP_NODE : 256 + (k + 1) * CAP_NODE]


def rooted(j):
    return slice(j * ROOTS, (j + 1) * ROOTS)


def summed(blocks, j):
    return sum(block[rooted((j + k) & 3)].astype(F32) for k, block in enumerate(blocks))


def root_first(g0, g1, g2, g3, own, x, rates, x_next, extra):
    blocks = (g0, g1, g2, g3)
    tau = rates[:1, :1]
    for j in range(4):
        slope = summed(blocks, j)
        if j == 0:
            x_old = x[...]
            slope = slope + own[...]
        else:
            x_old = blocks[(-j) & 3][rooted(4)].astype(F32)
        new = jnp.maximum(x_old + tau * slope, 0.0)
        x_next[rooted(j)] = new
        extra[rooted(j)] = (2.0 * new - x_old).astype(BF16)


def root_second(g0, g1, g2, g3, own, x, rates, extra, x_next):
    blocks = (g0, g1, g2, g3)
    tau = rates[:1, :1]
    for j in range(4):
        slope = summed(blocks, j)
        if j == 0:
            slope = slope + own[...]
        x_old = x[rooted(j)]
        new = jnp.maximum(x_old + tau * slope, 0.0)
        extra[rooted(j)] = (2.0 * new - x_old).astype(BF16)
        if j == 0:
            x_next[...] = new


def averages(x_start, x_root, x_root_next, x_child, x_child_next, average, move):
    roots = (x_root[:ROOTS] + x_root_next[...]) * 0.5
    children = (x_child[...] + x_child_next[...]) * 0.5
    average[:ROOTS] = roots
    average[ROWS] = children
    gap_roots = roots - x_start[:ROOTS]
    gap_children = children - x_start[ROWS]
    total = jnp.sum(gap_roots * gap_roots) + jnp.sum(gap_children * gap_children)
    move[...] = jnp.full((8, 128), total, F32)


def own_image(
    last, extra_child, extra_root, scol, coupling, y, right, rates, cost_top, base, *refs
):
    sigma = rates[1:2, :1]
    upper = jnp.concatenate([scol[...]] * (TILE // 128), axis=1) == 1.0
    child = extra_child[...]
    root = extra_root[:ROOTS]
    total = -cost_top[...]
    for cols in parts():
        image = jnp.where(
            upper, times_t(child, coupling[1, cols]), times_t(child, coupling[2, cols])
        )
        weights = coupling[0, cols]
        base_root = y[:ROOTS, cols] + sigma * (right[:ROOTS, cols] - times_t(root, weights))
        base[:ROOTS, cols] = base_root
        if not last:
            total = total + times(jnp.maximum(base_root, 0.0).astype(BF16), weights)
        base[ROWS, cols] = y[ROWS, cols] + sigma * (right[ROWS, cols] - image)
    if not last:
        (own_root,) = refs
        own_root[...] = total


def from_leaf(blocks, lback):
    hot = hot_lanes(lback[...], SLOTS)
    rows = None
    for k, block in enumerate(blocks):
        term = times(hot[:, k * 128 : (k + 1) * 128], block[...])
        rows = term if rows is None else rows + term
    return rows.astype(BF16)


def dual_leaf(last, b0, b1, b2, b3, lback, linking, base, rates, *refs):
    if last:
        (later,) = refs
    else:
        lsend, later, *outs = refs
    rows = from_leaf((b0, b1, b2, b3), lback)
    sigma = rates[1:2, :1]
    total = None
    for cols in parts():
        weights = linking[0, cols]
        new = base[ROWS, cols] - sigma * times_t(rows, weights)
        later[:, cols] = new
        if not last:
            product = times(jnp.maximum(new, 0.0).astype(BF16), weights)
            total = product if total is None else total + product
    if not last:
        spread(lsend[...], total.astype(BF16), outs)


def from_node(blocks, swapped, nback, held):
    join(blocks, swapped, held)
    return times(hot_lanes(nback[...], SLOTS), held[...]).astype(BF16)


def dual_node(g0, g1, g2, g3, swapped, nback, linking, base, later, rates, nsend, *refs):
    y_next, ylow, *outs, held = refs
    rows = from_node((g0, g1, g2, g3), swapped, nback, held)
    sigma = rates[1:2, :1]
    total = None
    for cols in parts():
        weights = linking[1, cols]
        new_root = jnp.maximum(base[:ROOTS, cols], 0.0)
        new = jnp.maximum(later[:, cols] - sigma * times_t(rows, weights), 0.0)
        low = new.astype(BF16)
        y_next[:ROOTS, cols] = new_root
        y_next[ROWS, cols] = new
        ylow[:ROOTS, cols] = new_root.astype(BF16)
        ylow[ROWS, cols] = low
        product = times(low, weights)
        total = product if total is None else total + product
    spread(nsend[...], total.astype(BF16), outs)


def dual_last(
    g0, g1, g2, g3, swapped, nback, linking, base, later, rates, y, y_start, primal_move, average, load, held
):
    rows = from_node((g0, g1, g2, g3), swapped, nback, held)
    sigma = rates[1:2, :1]
    move = jnp.zeros((1, TILE), F32)
    for cols in parts():
        new_root = jnp.maximum(base[:ROOTS, cols], 0.0)
        new = jnp.maximum(later[:, cols] - sigma * times_t(rows, linking[1, cols]), 0.0)
        mean_root = (y[:ROOTS, cols] + new_root) * 0.5
        mean = (y[ROWS, cols] + new) * 0.5
        average[:ROOTS, cols] = mean_root
        average[ROWS, cols] = mean
        gap_root = mean_root - y_start[:ROOTS, cols]
        gap = mean - y_start[ROWS, cols]
        move = move + jnp.sum(gap_root * gap_root, axis=0, keepdims=True)
        move = move + jnp.sum(gap * gap, axis=0, keepdims=True)
    lane = lax.broadcasted_iota(jnp.int32, load.shape, 2)
    load[...] = jnp.where(lane == 0, primal_move[:1], jnp.sum(move))


def pairs_of(place):
    pairs = []
    for i in range(N_LEAF * N_NODE):
        y, z, x, core = place(i >> 5, (i >> 3) & 3, (i >> 1) & 3, i & 1)
        pairs.append((i, ((y & 3) * 4 + (z & 3)) * N_NODE + (x & 3) * 2 + core))
    return ("leaf", "node"), pairs


def outer_ring(k):
    return pairs_of(lambda y, z, x, c: (y, z + k, x, c) if c else (y + k, z, x, c))


def inner_ring(k):
    return pairs_of(lambda y, z, x, c: (y + k, z, x, c) if c else (y, z + k, x, c))


def ring_x(k):
    return pairs_of(lambda y, z, x, c: (y, z, x + k, c))


def sibling(array):
    return lax.ppermute(array, *pairs_of(lambda y, z, x, c: (y, z, x, 1 - c)))


def shifted(blocks, ring, sign=1):
    got = {0: blocks[0]}
    for k in (2, 1, 3):
        got[k] = lax.ppermute(blocks[k], *ring((sign * k) % 4))
    return [got[k] for k in range(4)]


def swap_node(blocks, sign, before):
    got = shifted(blocks, ring_x, sign)
    halves = jnp.concatenate([block[CAP_NODE:] for block in got], axis=0)
    halves, before = lax.optimization_barrier((halves, before))
    return got + [sibling(halves)], before


def ring_gather(rows, ring):
    one = lax.ppermute(rows, *ring(1))
    three = lax.ppermute(rows, *ring(3))
    return [rows, one, lax.ppermute(one, *ring(1)), three]


def sum_leaf(blocks, own, state, before):
    got, before = lax.optimization_barrier((shifted(blocks, outer_ring), before))
    got = [block.astype(F32) for block in got]
    total = ((got[0] + got[1]) + got[2]) + got[3]
    sent = jnp.concatenate([total[:ROOTS] + own, total[ROOTS:]], axis=0).astype(BF16)
    if state is not None:
        sent = jnp.concatenate([sent, state], axis=0)
    return [total.astype(BF16)] + shifted([sent] * 4, inner_ring)[1:], before


def part_of(kernel, flag):
    def run(*refs):
        kernel(flag, *refs)

    return run


def shards(x_start, y_start, cost_vec, right_side, omega, coupling, linking, parent, section):
    unit = 2 * CHILD * NS * NC
    rates = jnp.broadcast_to(jnp.stack([STEP / omega[0], STEP * omega[0]])[:, None], (2, 128))
    field = ((NODES, NC), F32)
    field_low = ((NODES, NC), BF16)
    states = ((NODES, NS), F32)
    block = ((128, NS), BF16)
    block_mark = ((128, NS + 128), BF16)
    kids = ((CHILD, NS), F32)
    kids_low = ((CHILD, NS), BF16)
    kids_field = ((CHILD, NC), F32)
    tops = ((ROOTS, NS), F32)
    plane = ((4 * ROOTS, NS), F32)
    row = ((1, CHILD), F32)
    col = ((CHILD, 128), F32)
    held = [pltpu.VMEM((SLOTS, NS), BF16)]

    *sent, y_start, linking, ylow, nsend, nback, lsend, lback, scol, x_top, cost_top, state = call(
        first,
        [block_mark] * 4 + [block] * 4
        + [field, ((2, NC, NS), BF16), field_low, row, col, row, col, col, tops, tops, ((ROOTS, NS), BF16)],
        [parent, section, y_start, linking, x_start, cost_vec],
        2 * unit,
        [
            pltpu.VMEM((NODES,), jnp.int32),
            pltpu.VMEM((NODES,), jnp.int32),
            pltpu.SemaphoreType.DMA((3 * NC // CHUNK + 4,)),
        ],
        (0, 1, 2, 3, 4, 5),
    )
    (own_root,) = call(own_root_first, [tops], [ylow, cost_top, coupling], unit // 8)
    (own,) = call(own_adjoint, [kids], [ylow, scol, coupling], 2 * unit)
    got_leaf, _ = sum_leaf(sent[4:], own_root, state, own_root)
    got_node, (got_leaf, own) = swap_node(sent[:4], 1, (got_leaf, own))

    x_root, extra_root = call(
        root_first,
        [plane, block],
        got_leaf + [own_root, x_top, rates],
        0,
    )
    own, extra_root = lax.optimization_barrier((own, extra_root))
    wrow, wcol, x_child, extra_child, *out_node = call(
        primal_first,
        [((8, SLOTS), F32), ((SLOTS, 128), F32), kids, kids_low] + [block] * 4,
        got_node + [own, x_start, cost_vec, rates],
        unit // 4,
        [pltpu.VMEM((SLOTS, NS + 128), BF16)],
    )
    base, own_root = call(
        part_of(own_image, False),
        [field, tops],
        [
            extra_child, extra_root, scol, coupling, y_start, right_side, rates, cost_top
        ],
        2 * unit,
    )
    back_leaf = ring_gather(extra_root, outer_ring)
    back_node, (back_leaf[1], back_leaf[3], base) = swap_node(
        out_node, -1, (back_leaf[1], back_leaf[3], base)
    )
    later, *out_leaf = call(
        part_of(dual_leaf, False),
        [kids_field] + [block] * 4,
        back_leaf + [lback, linking, base, rates, lsend],
        2 * unit,
    )
    y_next, ylow, *out_node = call(
        dual_node,
        [field, field_low] + [block] * 4,
        back_node + [nback, linking, base, later, rates, nsend],
        2 * unit,
        held,
    )
    got_leaf, ylow = sum_leaf(out_leaf, own_root, None, ylow)
    (own,) = call(own_adjoint, [kids], [ylow, scol, coupling], 2 * unit)
    got_node, (got_leaf, own) = swap_node(out_node, 1, (got_leaf, own))

    extra_root, x_top = call(
        root_second,
        [block, tops],
        got_leaf + [own_root, x_root, rates],
        0,
    )
    own, extra_root = lax.optimization_barrier((own, extra_root))
    x_child_next, extra_child, *out_node = call(
        primal_second,
        [kids, kids_low] + [block] * 4,
        got_node + [own, x_child, cost_vec, rates, wrow, wcol],
        unit // 4,
        held,
    )
    x_average, primal_move = call(
        averages,
        [states, ((8, 128), F32)],
        [x_start, x_root, x_top, x_child, x_child_next],
        0,
        final=(0,),
    )
    (base,) = call(
        part_of(own_image, True),
        [field],
        [extra_child, extra_root, scol, coupling, y_next, right_side, rates, cost_top],
        2 * unit,
    )
    back_leaf = ring_gather(extra_root, outer_ring)
    back_node, (back_leaf, base, primal_move) = swap_node(
        out_node, -1, (back_leaf, base, primal_move)
    )
    (later,) = call(
        part_of(dual_leaf, True), [kids_field], back_leaf + [lback, linking, base, rates], unit
    )
    y_average, load = call(
        dual_last,
        [field, ((N_LEAF * N_NODE, 1, 128), F32)],
        back_node + [nback, linking, base, later, rates, y_next, y_start, primal_move],
        unit,
        held,
    )
    moves = lax.all_to_all(load, ("leaf", "node"), split_axis=0, concat_axis=0, tiled=True)
    moves = jnp.sum(moves[:, 0, :2], axis=0)
    omega_new = jnp.sqrt((moves[1:] + 1e-06) / (moves[:1] + 1e-06))
    return (x_average, y_average, omega_new)


def solution(mesh):
    both = P(("leaf", "node"), None)
    flat = P(("leaf", "node"))
    return jax.shard_map(
        shards,
        mesh=mesh,
        in_specs=(both, both, both, both, P(), P(), P(), flat, flat),
        out_specs=(both, both, P()),
        check_vma=False,
    )
```
